32 devices in a mesh: acq: 4 (over y, x), pix: 8 (over z, core).
Axes of the slice: x: 2, y: 2, z: 4, core: 2. Of those that a mesh axis runs over, the one named last changes fastest.
Arguments:
- slc: bfloat16 [12, 2, 768, 3072], P('acq', None, 'pix')
- offsets: int32 [12, 768], P('acq', 'pix'), may hold values from -16 to 16
- weights: bfloat16 [12, 8], replicated, may hold values from -0.29882812 to 1
- pairs: int32 [60, 2], replicated, may hold values from 0 to 11, as said below
Outputs:
- coherence: float32 [2, 60, 192, 192], P(None, None, 'pix', 'acq')
The draws below stay inside these ranges and needn't reach their ends.
Inputs may be any that keep to these rules, and one draw needn't show every extreme that they name: `pairs`: the two acquisitions of an interferogram differ.
All inputs are finite; a program needn't handle non-finite values.
Results may differ from the reference program's by a relative error of at most 0.0031.
Values may be sent and summed in bfloat16 or wider, within the bound.
No kernel may reach another device: no remote copies, remote signals or barrier semaphores. Data moves between devices by JAX's collectives and lax.ppermute only.
A program may use at most 64 MiB of HBM per device.

```python
import jax
import jax.numpy as jnp
from jax import lax

COLS = 3072
TAPS = 8
MAX_OFF = 16
LOOK_R = 4
LOOK_C = 16
ACQ = 12
LINES = 768
PAIRS = 60
HALO = 20


def geometry(key):
    base_key = jax.random.fold_in(key, 11)
    k_base = jax.random.fold_in(base_key, 1)
    k_first = jax.random.fold_in(base_key, 2)
    k_second = jax.random.fold_in(base_key, 3)
    k_jitter = jax.random.fold_in(base_key, 4)
    base = jax.random.randint(k_base, (ACQ,), -(MAX_OFF - 1), MAX_OFF)
    first = jax.random.randint(k_first, (), 0, ACQ)
    second = (first + jax.random.randint(k_second, (), 1, ACQ)) % ACQ
    index = jnp.arange(ACQ)
    base = jnp.where(index == first, MAX_OFF - 1, base)
    base = jnp.where(index == second, -(MAX_OFF - 1), base)
    code = jax.random.randint(k_jitter, (ACQ, LINES), 0, 4)
    jitter = jnp.where(code == 0, -1, jnp.where(code == 3, 1, 0))
    line = jnp.arange(LINES)
    jitter = jnp.where((index[:, None] == first) & (line[None, :] == 0), 1, jitter)
    jitter = jnp.where((index[:, None] == second) & (line[None, :] == 0), -1, jitter)
    return (base.astype(jnp.int32), jitter.astype(jnp.int32))


def draw_offsets(key, part):
    base, jitter = geometry(key)
    return (base[:, None] + jitter).astype(jnp.int32)


def draw_slc(key, part):
    base, jitter = geometry(key)
    scene = jax.random.normal(jax.random.fold_in(key, 21), (2, LINES, COLS), jnp.float32)
    line = jnp.arange(LINES)
    index = (line[None, :] - base[:, None]) % LINES
    shifted = jnp.moveaxis(scene[:, index, :], 1, 0)
    noise = jax.random.normal(jax.random.fold_in(key, 22), (ACQ, 2, LINES, COLS), jnp.float32)
    field = 0.8 * shifted + 0.6 * noise
    return field.astype(jnp.bfloat16)


def draw_pairs(key, part):
    k_first = jax.random.fold_in(key, 31)
    k_step = jax.random.fold_in(key, 32)
    first = jax.random.randint(k_first, (PAIRS,), 0, ACQ)
    second = (first + jax.random.randint(k_step, (PAIRS,), 1, ACQ)) % ACQ
    row = jnp.arange(PAIRS)
    first = jnp.where(row == 0, ACQ - 1, first)
    second = jnp.where(row == 0, 0, second)
    return jnp.stack([first, second], axis=1).astype(jnp.int32)


def setup_inputs(seed: int = 0) -> dict:
    streams_of = jax.random.split(jax.random.key(seed), 5)
    return {
        "slc": draw_slc(jax.random.fold_in(streams_of[4], 71), 0),
        "offsets": draw_offsets(jax.random.fold_in(streams_of[4], 71), 0),
        "weights": jnp.clip(jax.random.uniform(streams_of[2], (ACQ, TAPS), jnp.float32, -0.29882812, 1.0), -0.29882812, 1.0).astype(jnp.bfloat16),
        "pairs": draw_pairs(jax.random.fold_in(streams_of[4], 71), 0),
    }


def resample_one(slab, line_off, kernel):
    padded = jnp.pad(slab, ((0, 0), (HALO, HALO), (0, 0)))
    total = jnp.zeros(slab.shape, jnp.float32)
    base = jnp.arange(LINES, dtype=jnp.int32) + HALO + line_off.astype(jnp.int32)
    for k in range(TAPS):
        index = (base + (k - (TAPS // 2 - 1))).astype(jnp.int32)
        rows = jnp.take(padded, index, axis=1)
        total = total + kernel[k].astype(jnp.float32) * rows.astype(jnp.float32)
    return total.astype(jnp.bfloat16)

def look_mean(field):
    shaped = field.reshape(LINES // LOOK_R, LOOK_R, COLS // LOOK_C, LOOK_C)
    return lax.optimization_barrier(jnp.mean(shaped, axis=(1, 3)))

def reference(slc, offsets, weights, pairs):
    resampled = lax.map(lambda item: resample_one(item[0], item[1], item[2]), (slc, offsets, weights))

    def power_one(field):
        wide = field.astype(jnp.float32)
        return look_mean(wide[0] * wide[0] + wide[1] * wide[1])
    power = lax.map(power_one, resampled)

    def pair_one(pair):
        first = resampled[pair[0]].astype(jnp.float32)
        second = resampled[pair[1]].astype(jnp.float32)
        real_part = look_mean(first[0] * second[0] + first[1] * second[1])
        imag_part = look_mean(first[1] * second[0] - first[0] * second[1])
        scale = jnp.sqrt((power[pair[0]] + 1e-06) * (power[pair[1]] + 1e-06))
        return jnp.stack([real_part / scale, imag_part / scale])
    result = lax.map(pair_one, pairs)
    return jnp.moveaxis(result, 1, 0)
```

```python
import functools

import jax
import jax.numpy as jnp
from jax import lax
from jax.experimental import pallas as pl
from jax.experimental.pallas import tpu as pltpu
from jax.sharding import PartitionSpec as P

LOOK_R = 4
LOOK_C = 16
CHUNK = 32
VMEM_BYTES = 48 * 1024 * 1024


def resample_kernel(first, group, kernel, off, top, mid, low, *rest):
    outs, band = rest[:-1], rest[-1]
    acq = top.shape[0]
    taps = kernel.shape[1]
    rows = 3 * CHUNK
    step = pl.program_id(0)

    @pl.when(step == 0)
    def _():
        source = lax.broadcasted_iota(jnp.int32, (rows, CHUNK), 0)
        target = lax.broadcasted_iota(jnp.int32, (rows, CHUNK), 1)
        base = source - target - (CHUNK - (taps // 2 - 1))
        row = lax.broadcasted_iota(jnp.int32, (CHUNK, CHUNK), 0)
        col = lax.broadcasted_iota(jnp.int32, (CHUNK, CHUNK), 1)
        blocks = CHUNK // LOOK_R
        order = jnp.where(col == (row % blocks) * LOOK_R + row // blocks, 1.0, 0.0).astype(jnp.bfloat16)
        for a in range(acq):
            tap = base - off[a : a + 1, first : first + CHUNK]
            total = jnp.zeros((rows, CHUNK), jnp.float32)
            for k in range(taps):
                total = jnp.where(tap == k, kernel[group[0] * acq + a, k], total)
            turned = lax.dot_general(
                order, total.astype(jnp.bfloat16), (((1,), (1,)), ((), ())),
                preferred_element_type=jnp.float32,
            )
            band[a] = turned.astype(jnp.bfloat16)

    for s, out in enumerate(outs):

        @pl.when(step == s)
        def _(out=out):
            for a in range(acq):
                for x in range(2):
                    lines = jnp.concatenate([top[a, x], mid[a, x], low[a, x]], axis=0)
                    total = jnp.dot(band[a], lines, preferred_element_type=jnp.float32)
                    out[a, x] = total.astype(jnp.bfloat16)


def resample(first, group, kernel, offsets, parts, groups):
    acq, cols = parts[0][0].shape[0], parts[0][0].shape[3]
    width = cols // groups
    shape = (acq, 2, CHUNK, width)

    def source(index):
        return pl.BlockSpec(shape, lambda t, g: (0, 0, index, t ^ g[0]))

    return pl.pallas_call(
        functools.partial(resample_kernel, first),
        grid_spec=pltpu.PrefetchScalarGridSpec(
            num_scalar_prefetch=1,
            grid=(groups,),
            in_specs=[
                pl.BlockSpec(memory_space=pltpu.SMEM),
                pl.BlockSpec(offsets.shape, lambda t, g: (0, 0)),
                *[source(index) for _, index in parts],
            ],
            out_specs=[pl.BlockSpec(shape, lambda t, g: (0, 0, 0, 0))] * groups,
            scratch_shapes=[pltpu.VMEM((acq, CHUNK, 3 * CHUNK), jnp.bfloat16)],
        ),
        out_shape=[jax.ShapeDtypeStruct(shape, jnp.bfloat16)] * groups,
        compiler_params=pltpu.CompilerParams(vmem_limit_bytes=VMEM_BYTES),
        cost_estimate=pl.CostEstimate(
            flops=2 * acq * 2 * CHUNK * 3 * CHUNK * cols,
            bytes_accessed=acq * 2 * 4 * CHUNK * cols * 2,
            transcendentals=0,
        ),
        name="resample",
    )(group, kernel, offsets, *[array for array, _ in parts])


def interfere_kernel(groups, pairs, *rest):
    blocks, (out, wide, high, low, pooled, inverse) = rest[:groups], rest[-6:]
    acq, _, lines, width = blocks[0].shape
    looks = lines // LOOK_R
    count = pairs.shape[0]
    windows = width // LOOK_C

    for r, block in enumerate(blocks):
        for a in range(acq):
            for x in range(2):
                wide[r * acq + a, x] = block[a, x].astype(jnp.float32) * 0.125

    col = lax.broadcasted_iota(jnp.int32, (width, windows), 0)
    window = lax.broadcasted_iota(jnp.int32, (width, windows), 1)
    pool = jnp.where(col // LOOK_C == window, 1.0, 0.0).astype(jnp.bfloat16)

    def split(field):
        first = field.astype(jnp.bfloat16)
        return first, (field - first.astype(jnp.float32)).astype(jnp.bfloat16)

    def gather(first, second):
        return jnp.dot(first, pool, preferred_element_type=jnp.float32) + jnp.dot(
            second, pool, preferred_element_type=jnp.float32
        )

    def power_two(i, carry):
        fields = []
        for u in range(2):
            total = 0.0
            for j in range(LOOK_R):
                for x in range(2):
                    value = wide[2 * i + u, x, j * looks : (j + 1) * looks, :]
                    total = total + value * value
            fields.append(total)
        first, second = split(jnp.concatenate(fields, axis=0))
        at = pl.multiple_of(i * 2 * looks, 2 * looks)
        high[pl.ds(at, 2 * looks), :] = first
        low[pl.ds(at, 2 * looks), :] = second
        return carry

    total_acq = groups * acq
    lax.fori_loop(0, total_acq // 2, power_two, 0)
    power = gather(high[: total_acq * looks, :], low[: total_acq * looks, :])
    inverse[...] = lax.rsqrt(power + 1e-6).reshape(total_acq, looks, windows)

    def one_pair(p, carry):
        m, s = pairs[p, 0], pairs[p, 1]
        real, imag = 0.0, 0.0
        for j in range(LOOK_R):
            at = slice(j * looks, (j + 1) * looks)
            m0, m1, s0, s1 = wide[m, 0, at, :], wide[m, 1, at, :], wide[s, 0, at, :], wide[s, 1, at, :]
            real = real + (m0 * s0 + m1 * s1)
            imag = imag + (m1 * s0 - m0 * s1)
        first, second = split(jnp.concatenate([real, imag], axis=0))
        at = pl.multiple_of(p * 2 * looks, 2 * looks)
        high[pl.ds(at, 2 * looks), :] = first
        low[pl.ds(at, 2 * looks), :] = second
        return carry

    lax.fori_loop(0, count, one_pair, 0, unroll=2)
    pooled[...] = gather(high[: count * 2 * looks, :], low[: count * 2 * looks, :]).reshape(
        count, 2, looks, windows
    )

    def scale_pair(p, carry):
        scale = inverse[pairs[p, 0]] * inverse[pairs[p, 1]]
        for x in range(2):
            out[x, p] = pooled[p, x] * scale
        return carry

    lax.fori_loop(0, count, scale_pair, 0, unroll=4)


def interfere(place, chunks, pairs, blocks, before):
    groups = len(blocks)
    acq, _, lines, width = blocks[0].shape
    looks, windows, count = lines // LOOK_R, width // LOOK_C, pairs.shape[0]
    rows = max(count * 2, groups * acq) * looks
    whole = pl.BlockSpec(blocks[0].shape, lambda t: (0, 0, 0, 0))
    extra = [] if before is None else [before]
    return pl.pallas_call(
        functools.partial(interfere_kernel, groups),
        grid=(1,),
        in_specs=[pl.BlockSpec(memory_space=pltpu.SMEM)]
        + [whole] * groups
        + [pl.BlockSpec(memory_space=pl.ANY)] * len(extra),
        out_specs=pl.BlockSpec((2, count, looks, windows), lambda t: (0, 0, place, 0)),
        out_shape=jax.ShapeDtypeStruct((2, count, chunks * looks, windows), jnp.float32),
        scratch_shapes=[
            pltpu.VMEM((groups * acq, 2, lines, width), jnp.float32),
            pltpu.VMEM((rows, width), jnp.bfloat16),
            pltpu.VMEM((rows, width), jnp.bfloat16),
            pltpu.VMEM((count, 2, looks, windows), jnp.float32),
            pltpu.VMEM((groups * acq, looks, windows), jnp.float32),
        ],
        input_output_aliases={} if before is None else {1 + groups: 0},
        compiler_params=pltpu.CompilerParams(vmem_limit_bytes=VMEM_BYTES),
        cost_estimate=pl.CostEstimate(
            flops=count * 8 * lines * width,
            bytes_accessed=groups * acq * 2 * lines * width * 2,
            transcendentals=0,
        ),
        name="interfere",
    )(pairs, *blocks, *extra)


def local(slc, offsets, weights, pairs):
    acq, _, lines, cols = slc.shape
    groups = lax.axis_size("acq")
    size = lax.axis_size("pix")
    mine = lax.axis_index("acq")
    group = jnp.reshape(mine, (1,)).astype(jnp.int32)
    kernel = weights.astype(jnp.float32)
    placed = ((pairs // acq) ^ mine) * acq + pairs % acq
    chunks = lines // CHUNK
    last = chunks - 1

    up = [(i, i + 1) for i in range(size - 1)]
    down = [(j, i) for i, j in up]
    above = lax.ppermute(slc[:, :, lines - CHUNK :], "pix", up)
    below = lax.ppermute(slc[:, :, :CHUNK], "pix", down)

    def piece(index):
        if index < 0:
            return (above, 0)
        return (below, 0) if index > last else (slc, index)

    result = None
    held = []
    for c in [*range(1, last), 0, last]:
        parts = [piece(c - 1), piece(c), piece(c + 1)]
        blocks = resample(c * CHUNK, group, kernel, offsets, parts, groups)
        moved = [blocks[0]]
        for s in range(1, groups):
            moved.append(lax.ppermute(blocks[s], "acq", [(i, i ^ s) for i in range(groups)]))
        held.append((c, moved))
    for c, moved in held:
        result = interfere(c, chunks, placed, moved, result)
    return result


def solution(mesh):
    placed = (P("acq", None, "pix", None), P("acq", "pix"), P(), P())
    return jax.shard_map(
        local, mesh=mesh, in_specs=placed, out_specs=P(None, None, "pix", "acq"), check_vma=False
    )
```

```python
import functools

import jax
import jax.numpy as jnp
from jax import lax
from jax.experimental import pallas as pl
from jax.experimental.pallas import tpu as pltpu
from jax.sharding import PartitionSpec as P

LOOK_R = 4
LOOK_C = 16
CHUNK = 32
HALO = 24
TILE = 16
MIB = 1024 * 1024


def build_bands(first, sources, group, kernel, off, band):
    acq, taps = off.shape[0], kernel.shape[0]
    rows = sum(count for _, count in sources)
    index = lax.broadcasted_iota(jnp.int32, (rows, CHUNK), 0)
    source = jnp.zeros((rows, CHUNK), jnp.int32)
    at = 0
    for begin, count in sources:
        source = jnp.where(index >= at, index + (begin - at), source)
        at += count
    target = first + lax.broadcasted_iota(jnp.int32, (rows, CHUNK), 1)
    base = source - target + (taps // 2 - 1)
    row = lax.broadcasted_iota(jnp.int32, (CHUNK, CHUNK), 0)
    col = lax.broadcasted_iota(jnp.int32, (CHUNK, CHUNK), 1)
    blocks = CHUNK // LOOK_R
    order = jnp.where(col == (row % blocks) * LOOK_R + row // blocks, 1.0, 0.0).astype(jnp.bfloat16)
    for a in range(acq):
        tap = base - off[a : a + 1, first : first + CHUNK]
        total = jnp.zeros((rows, CHUNK), jnp.float32)
        for k in range(taps):
            total = jnp.where(tap == k, kernel[k, group[0] * acq + a], total)
        turned = lax.dot_general(
            order, total.astype(jnp.bfloat16), (((1,), (1,)), ((), ())),
            preferred_element_type=jnp.float32,
        )
        band[a] = turned.astype(jnp.bfloat16)


def first_kernel(first, groups, group, kernel, off, slc, *rest):
    outs, (head, tail, slab, band, sems) = rest[:groups], rest[groups:]
    acq, _, lines, cols = slc.shape
    width = cols // groups

    def columns(s):
        return pl.ds(pl.multiple_of((group[0] ^ s) * width, width), width)

    order = [*range(1, groups), 0]
    copies = {}
    for s in order:
        at = columns(s)
        copies[s] = pltpu.make_async_copy(slc.at[:, :, :, at], slab.at[:, :, :, at], sems.at[s])
        copies[s].start()
    build_bands(first, [(0, lines)], group, kernel, off, band)
    for s in order:
        copies[s].wait()
        at = columns(s)
        for a in range(acq):
            for x in range(2):
                total = jnp.dot(band[a], slab[a, x, :, at], preferred_element_type=jnp.float32)
                outs[s][a, x] = total.astype(jnp.bfloat16)
    head[...] = slab[:, :, :HALO, :]
    tail[...] = slab[:, :, lines - HALO :, :]


def edge_kernel(first, groups, begin, count, halo_at, group, kernel, off, slab, halo, *rest):
    outs, band = rest[:groups], rest[groups]
    acq, _, _, cols = slab.shape
    width = cols // groups
    build_bands(first, [(begin, count), (halo_at, HALO)], group, kernel, off, band)
    for s in [*range(1, groups), 0]:
        at = pl.ds(pl.multiple_of((group[0] ^ s) * width, width), width)
        for a in range(acq):
            for x in range(2):
                lines = jnp.concatenate(
                    [slab[a, x, begin : begin + count, at], halo[a, x, :, at]], axis=0
                )
                total = jnp.dot(band[a], lines, preferred_element_type=jnp.float32)
                outs[s][a, x] = total.astype(jnp.bfloat16)


SMEM = pl.BlockSpec(memory_space=pltpu.SMEM)
VMEM = pl.BlockSpec(memory_space=pltpu.VMEM)
ANY = pl.BlockSpec(memory_space=pl.ANY)


def resample_cost(acq, cols, rows):
    return pl.CostEstimate(
        flops=2 * acq * 2 * CHUNK * rows * cols,
        bytes_accessed=acq * 2 * (rows + CHUNK) * cols * 2,
        transcendentals=0,
    )


def resample_first(first, group, kernel, offsets, slc, groups):
    acq, _, lines, cols = slc.shape
    piece = pltpu.VMEM((acq, 2, CHUNK, cols // groups), jnp.bfloat16)
    halo = pltpu.VMEM((acq, 2, HALO, cols), jnp.bfloat16)
    slab = pltpu.VMEM(slc.shape, jnp.bfloat16)
    return pl.pallas_call(
        functools.partial(first_kernel, first, groups),
        in_specs=[SMEM, SMEM, VMEM, ANY],
        out_specs=[VMEM] * (groups + 3),
        out_shape=[piece] * groups + [halo, halo, slab],
        scratch_shapes=[
            pltpu.VMEM((acq, CHUNK, lines), jnp.bfloat16),
            pltpu.SemaphoreType.DMA((groups,)),
        ],
        compiler_params=pltpu.CompilerParams(vmem_limit_bytes=16 * MIB),
        cost_estimate=resample_cost(acq, cols, lines),
        name="resample_first",
    )(group, kernel, offsets, slc)


def resample_edge(first, begin, count, halo_at, group, kernel, offsets, slab, halo, groups):
    acq, _, lines, cols = slab.shape
    piece = pltpu.VMEM((acq, 2, CHUNK, cols // groups), jnp.bfloat16)
    return pl.pallas_call(
        functools.partial(edge_kernel, first, groups, begin, count, halo_at),
        in_specs=[SMEM, SMEM, VMEM, VMEM, VMEM],
        out_specs=[VMEM] * groups,
        out_shape=[piece] * groups,
        scratch_shapes=[pltpu.VMEM((acq, CHUNK, count + HALO), jnp.bfloat16)],
        compiler_params=pltpu.CompilerParams(vmem_limit_bytes=16 * MIB),
        cost_estimate=resample_cost(acq, cols, count + HALO),
        name="resample_edge",
    )(group, kernel, offsets, slab, halo)


def interfere_kernel(groups, place, batch, group, pairs, *rest):
    blocks, (out, wide, high, low, flat, inverse, slab, sem) = rest[:groups], rest[-8:]
    acq, _, lines, width = blocks[0].shape
    looks = lines // LOOK_R
    count = pairs.shape[1]
    windows = width // LOOK_C
    both = 2 * looks
    total_acq = groups * acq

    for r, block in enumerate(blocks):
        for a in range(acq):
            for x in range(2):
                wide[(group[0] ^ r) * acq + a, x] = block[a, x].astype(jnp.float32) * 0.125

    col = lax.broadcasted_iota(jnp.int32, (width, windows), 0)
    window = lax.broadcasted_iota(jnp.int32, (width, windows), 1)
    pool = jnp.where(col // LOOK_C == window, 1.0, 0.0).astype(jnp.bfloat16)

    def put(at, field):
        first = field.astype(jnp.bfloat16)
        high[at : at + both, :] = first
        low[at : at + both, :] = (field - first.astype(jnp.float32)).astype(jnp.bfloat16)

    def gather(rows):
        return jnp.dot(high[:rows, :], pool, preferred_element_type=jnp.float32) + jnp.dot(
            low[:rows, :], pool, preferred_element_type=jnp.float32
        )

    for i in range(0, total_acq, 2):
        fields = []
        for u in (i, i + 1):
            total = 0.0
            for j in range(LOOK_R):
                for x in range(2):
                    value = wide[u, x, j * looks : (j + 1) * looks, :]
                    total = total + value * value
            fields.append(total)
        put(i * looks, jnp.concatenate(fields, axis=0))
    power = gather(total_acq * looks)
    inverse[...] = lax.rsqrt(power + 1e-6).reshape(total_acq, looks, windows)

    def products(i):
        for u in range(batch):
            m, s = pairs[0, i * batch + u], pairs[1, i * batch + u]
            real, imag = 0.0, 0.0
            for j in range(LOOK_R):
                at = slice(j * looks, (j + 1) * looks)
                m0, m1, s0, s1 = wide[m, 0, at, :], wide[m, 1, at, :], wide[s, 0, at, :], wide[s, 1, at, :]
                real = real + (m0 * s0 + m1 * s1)
                imag = imag + (m1 * s0 - m0 * s1)
            put(u * both, jnp.concatenate([real, imag], axis=0))

    def settle(i):
        pooled = gather(batch * both)
        for u in range(batch):
            p = i * batch + u
            scale = inverse[pairs[0, p]] * inverse[pairs[1, p]]
            scaled = pooled[u * both : (u + 1) * both] * jnp.concatenate([scale, scale], axis=0)
            flat[pl.ds(pl.multiple_of(p * both, both), both), :] = scaled

    def turn(i, carry):
        settle(i - 1)
        products(i)
        return carry

    products(0)
    lax.fori_loop(1, count // batch, turn, 0)
    settle(count // batch - 1)

    for x in range(2):
        for g in range(looks):
            slab[x, g] = flat[pl.ds(x * looks + g, count, stride=both), :].T
    copy = pltpu.make_async_copy(slab, out.at[:, pl.ds(place * looks, looks)], sem)
    copy.start()
    copy.wait()


def interfere(place, chunks, group, pairs, blocks, before):
    groups = len(blocks)
    acq, _, lines, width = blocks[0].shape
    looks, windows, count = lines // LOOK_R, width // LOOK_C, pairs.shape[1]
    batch = max(b for b in range(1, 7) if count % b == 0)
    rows = max(batch * 2, groups * acq) * looks
    extra = [] if before is None else [before]
    return pl.pallas_call(
        functools.partial(interfere_kernel, groups, place, batch),
        in_specs=[SMEM, SMEM] + [VMEM] * groups + [ANY] * len(extra),
        out_specs=ANY,
        out_shape=pltpu.HBM((2, chunks * looks, windows, count), jnp.float32),
        scratch_shapes=[
            pltpu.VMEM((groups * acq, 2, lines, width), jnp.float32),
            pltpu.VMEM((rows, width), jnp.bfloat16),
            pltpu.VMEM((rows, width), jnp.bfloat16),
            pltpu.VMEM((count * 2 * looks, windows), jnp.float32),
            pltpu.VMEM((groups * acq, looks, windows), jnp.float32),
            pltpu.VMEM((2, looks, windows, count), jnp.float32),
            pltpu.SemaphoreType.DMA,
        ],
        input_output_aliases={} if before is None else {2 + groups: 0},
        compiler_params=pltpu.CompilerParams(vmem_limit_bytes=16 * MIB),
        cost_estimate=pl.CostEstimate(
            flops=count * 8 * lines * width,
            bytes_accessed=groups * acq * 2 * lines * width * 2,
            transcendentals=0,
        ),
        name="interfere",
    )(group, pairs, *blocks, *extra)


def local(slc, offsets, weights, pairs):
    acq, _, lines, cols = slc.shape
    groups = lax.axis_size("acq")
    size = lax.axis_size("pix")
    group = jnp.reshape(lax.axis_index("acq"), (1,)).astype(jnp.int32)
    kernel = weights.T.astype(jnp.float32)
    turned = pairs.T
    chunks = lines // CHUNK
    reach = CHUNK + TILE * 2

    up = [(i, i + 1) for i in range(size - 1)]
    down = [(j, i) for i, j in up]

    def send(blocks):
        moved = [blocks[0]]
        for s in range(1, groups):
            moved.append(lax.ppermute(blocks[s], "acq", [(i, i ^ s) for i in range(groups)]))
        return moved

    slc = pltpu.with_memory_space_constraint(slc, pltpu.HBM)
    *blocks, head, tail, slab = resample_first(CHUNK, group, kernel, offsets, slc, groups)
    above = lax.ppermute(tail, "pix", up)
    below = lax.ppermute(head, "pix", down)
    middle = send(blocks)
    top = send(
        resample_edge(0, 0, reach, -HALO, group, kernel, offsets, slab, above, groups)
    )
    bottom = send(
        resample_edge(
            lines - CHUNK, lines - reach, reach, lines, group, kernel, offsets, slab, below, groups
        )
    )
    result = None
    for place, moved in ((1, middle), (0, top), (2, bottom)):
        result = interfere(place, chunks, group, turned, moved, result)
    return jnp.transpose(result, (0, 3, 1, 2))


def solution(mesh):
    placed = (P("acq", None, "pix", None), P("acq", "pix"), P(), P())
    return jax.shard_map(
        local, mesh=mesh, in_specs=placed, out_specs=P(None, None, "pix", "acq"), check_vma=False
    )
```

```python
import functools

import jax
import jax.numpy as jnp
from jax import lax
from jax.experimental import pallas as pl
from jax.experimental.pallas import tpu as pltpu
from jax.sharding import PartitionSpec as P

LOOK_R = 4
LOOK_C = 16
CHUNK = 32
HALO = 24
TILE = 16
MIB = 1024 * 1024


def build_bands(first, sources, group, kernel, off, band):
    acq, taps = off.shape[0], kernel.shape[0]
    rows = sum(count for _, count in sources)
    index = lax.broadcasted_iota(jnp.int32, (rows, CHUNK), 0)
    source = jnp.zeros((rows, CHUNK), jnp.int32)
    at = 0
    for begin, count in sources:
        source = jnp.where(index >= at, index + (begin - at), source)
        at += count
    target = first + lax.broadcasted_iota(jnp.int32, (rows, CHUNK), 1)
    base = source - target + (taps // 2 - 1)
    row = lax.broadcasted_iota(jnp.int32, (CHUNK, CHUNK), 0)
    col = lax.broadcasted_iota(jnp.int32, (CHUNK, CHUNK), 1)
    blocks = CHUNK // LOOK_R
    order = jnp.where(col == (row % blocks) * LOOK_R + row // blocks, 1.0, 0.0).astype(jnp.bfloat16)
    for a in range(acq):
        tap = base - off[a : a + 1, first : first + CHUNK]
        total = jnp.zeros((rows, CHUNK), jnp.float32)
        for k in range(taps):
            total = jnp.where(tap == k, kernel[k, group[0] * acq + a], total)
        turned = lax.dot_general(
            order, total.astype(jnp.bfloat16), (((1,), (1,)), ((), ())),
            preferred_element_type=jnp.float32,
        )
        band[a] = turned.astype(jnp.bfloat16)


def first_kernel(first, groups, group, kernel, off, slc, *rest):
    outs, head, tail, slab, band, sems = rest
    acq, _, lines, cols = slc.shape
    width = cols // groups

    def columns(s):
        return slice(s * width, (s + 1) * width)

    order = range(groups)
    copies = {}
    for s in order:
        at = columns(s)
        copies[s] = pltpu.make_async_copy(slc.at[:, :, :, at], slab.at[:, :, :, at], sems.at[s])
        copies[s].start()
    build_bands(first, [(0, lines)], group, kernel, off, band)
    for s in order:
        copies[s].wait()
        at = columns(s)
        for a in range(acq):
            for x in range(2):
                total = jnp.dot(band[a], slab[a, x, :, at], preferred_element_type=jnp.float32)
                outs[s, a, x] = total.astype(jnp.bfloat16)
    head[...] = slab[:, :, :HALO, :]
    tail[...] = slab[:, :, lines - HALO :, :]


def edge_kernel(first, groups, begin, count, halo_at, group, kernel, off, slab, halo, *rest):
    outs, band = rest
    acq, _, _, cols = slab.shape
    width = cols // groups
    build_bands(first, [(begin, count), (halo_at, HALO)], group, kernel, off, band)
    for s in range(groups):
        at = slice(s * width, (s + 1) * width)
        for a in range(acq):
            for x in range(2):
                lines = jnp.concatenate(
                    [slab[a, x, begin : begin + count, at], halo[a, x, :, at]], axis=0
                )
                total = jnp.dot(band[a], lines, preferred_element_type=jnp.float32)
                outs[s, a, x] = total.astype(jnp.bfloat16)


SMEM = pl.BlockSpec(memory_space=pltpu.SMEM)
VMEM = pl.BlockSpec(memory_space=pltpu.VMEM)
ANY = pl.BlockSpec(memory_space=pl.ANY)


def resample_cost(acq, cols, rows):
    return pl.CostEstimate(
        flops=2 * acq * 2 * CHUNK * rows * cols,
        bytes_accessed=acq * 2 * (rows + CHUNK) * cols * 2,
        transcendentals=0,
    )


def resample_first(first, group, kernel, offsets, slc, groups):
    acq, _, lines, cols = slc.shape
    piece = pltpu.VMEM((groups, acq, 2, CHUNK, cols // groups), jnp.bfloat16)
    halo = pltpu.VMEM((acq, 2, HALO, cols), jnp.bfloat16)
    slab = pltpu.VMEM(slc.shape, jnp.bfloat16)
    return pl.pallas_call(
        functools.partial(first_kernel, first, groups),
        in_specs=[SMEM, SMEM, VMEM, ANY],
        out_specs=[VMEM] * 4,
        out_shape=[piece, halo, halo, slab],
        scratch_shapes=[
            pltpu.VMEM((acq, CHUNK, lines), jnp.bfloat16),
            pltpu.SemaphoreType.DMA((groups,)),
        ],
        compiler_params=pltpu.CompilerParams(vmem_limit_bytes=16 * MIB),
        cost_estimate=resample_cost(acq, cols, lines),
        name="resample_first",
    )(group, kernel, offsets, slc)


def resample_edge(first, begin, count, halo_at, group, kernel, offsets, slab, halo, groups):
    acq, _, lines, cols = slab.shape
    piece = pltpu.VMEM((groups, acq, 2, CHUNK, cols // groups), jnp.bfloat16)
    return pl.pallas_call(
        functools.partial(edge_kernel, first, groups, begin, count, halo_at),
        in_specs=[SMEM, SMEM, VMEM, VMEM, VMEM],
        out_specs=VMEM,
        out_shape=piece,
        scratch_shapes=[pltpu.VMEM((acq, CHUNK, count + HALO), jnp.bfloat16)],
        compiler_params=pltpu.CompilerParams(vmem_limit_bytes=16 * MIB),
        cost_estimate=resample_cost(acq, cols, count + HALO),
        name="resample_edge",
    )(group, kernel, offsets, slab, halo)


def interfere_kernel(place, batch, pairs, blocks, *rest):
    (out, wide, high, low, flat, inverse, slab, sem) = rest[-8:]
    groups, acq, _, lines, width = blocks.shape
    looks = lines // LOOK_R
    count = pairs.shape[1]
    windows = width // LOOK_C
    both = 2 * looks
    total_acq = groups * acq

    for r in range(groups):
        for a in range(acq):
            for x in range(2):
                wide[r * acq + a, x] = blocks[r, a, x].astype(jnp.float32) * 0.125

    col = lax.broadcasted_iota(jnp.int32, (width, windows), 0)
    window = lax.broadcasted_iota(jnp.int32, (width, windows), 1)
    pool = jnp.where(col // LOOK_C == window, 1.0, 0.0).astype(jnp.bfloat16)

    def put(at, field):
        first = field.astype(jnp.bfloat16)
        high[at : at + both, :] = first
        low[at : at + both, :] = (field - first.astype(jnp.float32)).astype(jnp.bfloat16)

    def gather(rows):
        return jnp.dot(high[:rows, :], pool, preferred_element_type=jnp.float32) + jnp.dot(
            low[:rows, :], pool, preferred_element_type=jnp.float32
        )

    for i in range(0, total_acq, 2):
        fields = []
        for u in (i, i + 1):
            total = 0.0
            for j in range(LOOK_R):
                for x in range(2):
                    value = wide[u, x, j * looks : (j + 1) * looks, :]
                    total = total + value * value
            fields.append(total)
        put(i * looks, jnp.concatenate(fields, axis=0))
    power = gather(total_acq * looks)
    inverse[...] = lax.rsqrt(power + 1e-6).reshape(total_acq, looks, windows)

    def products(i):
        for u in range(batch):
            m, s = pairs[0, i * batch + u], pairs[1, i * batch + u]
            real, imag = 0.0, 0.0
            for j in range(LOOK_R):
                at = slice(j * looks, (j + 1) * looks)
                m0, m1, s0, s1 = wide[m, 0, at, :], wide[m, 1, at, :], wide[s, 0, at, :], wide[s, 1, at, :]
                real = real + (m0 * s0 + m1 * s1)
                imag = imag + (m1 * s0 - m0 * s1)
            put(u * both, jnp.concatenate([real, imag], axis=0))

    def settle(i):
        pooled = gather(batch * both)
        for u in range(batch):
            p = i * batch + u
            scale = inverse[pairs[0, p]] * inverse[pairs[1, p]]
            scaled = pooled[u * both : (u + 1) * both] * jnp.concatenate([scale, scale], axis=0)
            flat[pl.ds(pl.multiple_of(p * both, both), both), :] = scaled

    def turn(i, carry):
        settle(i - 1)
        products(i)
        return carry

    products(0)
    lax.fori_loop(1, count // batch, turn, 0)
    settle(count // batch - 1)

    for x in range(2):
        for g in range(looks):
            slab[x, g] = flat[pl.ds(x * looks + g, count, stride=both), :].T
    copy = pltpu.make_async_copy(slab, out.at[:, pl.ds(place * looks, looks)], sem)
    copy.start()
    copy.wait()


def interfere(place, chunks, pairs, blocks, before):
    groups, acq, _, lines, width = blocks.shape
    looks, windows, count = lines // LOOK_R, width // LOOK_C, pairs.shape[1]
    batch = max(b for b in range(1, 7) if count % b == 0)
    rows = max(batch * 2, groups * acq) * looks
    extra = [] if before is None else [before]
    return pl.pallas_call(
        functools.partial(interfere_kernel, place, batch),
        in_specs=[SMEM, VMEM] + [ANY] * len(extra),
        out_specs=ANY,
        out_shape=pltpu.HBM((2, chunks * looks, windows, count), jnp.float32),
        scratch_shapes=[
            pltpu.VMEM((groups * acq, 2, lines, width), jnp.float32),
            pltpu.VMEM((rows, width), jnp.bfloat16),
            pltpu.VMEM((rows, width), jnp.bfloat16),
            pltpu.VMEM((count * 2 * looks, windows), jnp.float32),
            pltpu.VMEM((groups * acq, looks, windows), jnp.float32),
            pltpu.VMEM((2, looks, windows, count), jnp.float32),
            pltpu.SemaphoreType.DMA,
        ],
        input_output_aliases={} if before is None else {2: 0},
        compiler_params=pltpu.CompilerParams(vmem_limit_bytes=16 * MIB),
        cost_estimate=pl.CostEstimate(
            flops=count * 8 * lines * width,
            bytes_accessed=groups * acq * 2 * lines * width * 2,
            transcendentals=0,
        ),
        name="interfere",
    )(pairs, blocks, *extra)


def local(slc, offsets, weights, pairs):
    acq, _, lines, cols = slc.shape
    groups = lax.axis_size("acq")
    size = lax.axis_size("pix")
    group = jnp.reshape(lax.axis_index("acq"), (1,)).astype(jnp.int32)
    kernel = weights.T.astype(jnp.float32)
    turned = pairs.T
    chunks = lines // CHUNK
    reach = CHUNK + TILE * 2

    up = [(i, i + 1) for i in range(size - 1)]
    down = [(j, i) for i, j in up]

    def send(blocks):
        return lax.all_to_all(blocks, "acq", split_axis=0, concat_axis=0, tiled=True)

    slc = pltpu.with_memory_space_constraint(slc, pltpu.HBM)
    blocks, head, tail, slab = resample_first(CHUNK, group, kernel, offsets, slc, groups)
    middle = send(blocks)
    above = lax.ppermute(tail, "pix", up)
    below = lax.ppermute(head, "pix", down)
    top = send(
        resample_edge(0, 0, reach, -HALO, group, kernel, offsets, slab, above, groups)
    )
    bottom = send(
        resample_edge(
            lines - CHUNK, lines - reach, reach, lines, group, kernel, offsets, slab, below, groups
        )
    )
    result = None
    for place, moved in ((1, middle), (0, top), (2, bottom)):
        result = interfere(place, chunks, turned, moved, result)
    return jnp.transpose(result, (0, 3, 1, 2))


def solution(mesh):
    placed = (P("acq", None, "pix", None), P("acq", "pix"), P(), P())
    return jax.shard_map(
        local, mesh=mesh, in_specs=placed, out_specs=P(None, None, "pix", "acq"), check_vma=False
    )
```

```python
import functools

import jax
import jax.numpy as jnp
from jax import lax
from jax.experimental import pallas as pl
from jax.experimental.pallas import tpu as pltpu
from jax.sharding import PartitionSpec as P

LOOK_R = 4
LOOK_C = 16
CHUNK = 32
HALO = 24
TILE = 16
LANES = 128
MIB = 1024 * 1024


def build_bands(first, sources, group, kernel, off, band):
    acq, taps = off.shape[0], kernel.shape[0]
    gains = kernel[...].astype(jnp.float32)
    lane = lax.broadcasted_iota(jnp.int32, gains.shape, 1)
    rows = sum(count for _, count in sources)
    index = lax.broadcasted_iota(jnp.int32, (rows, CHUNK), 0)
    source = jnp.zeros((rows, CHUNK), jnp.int32)
    at = 0
    for begin, count in sources:
        source = jnp.where(index >= at, index + (begin - at), source)
        at += count
    target = first + lax.broadcasted_iota(jnp.int32, (rows, CHUNK), 1)
    base = source - target + (taps // 2 - 1)
    row = lax.broadcasted_iota(jnp.int32, (CHUNK, CHUNK), 0)
    col = lax.broadcasted_iota(jnp.int32, (CHUNK, CHUNK), 1)
    blocks = CHUNK // LOOK_R
    order = jnp.where(col == (row % blocks) * LOOK_R + row // blocks, 1.0, 0.0).astype(jnp.bfloat16)
    for a in range(acq):
        tap = base - off[a : a + 1, first : first + CHUNK]
        total = jnp.zeros((rows, CHUNK), jnp.float32)
        gain = jnp.sum(jnp.where(lane == group[0] * acq + a, gains, 0.0), axis=1, keepdims=True)
        for k in range(taps):
            total = jnp.where(tap == k, gain[k : k + 1, :], total)
        turned = lax.dot_general(
            order, total.astype(jnp.bfloat16), (((1,), (1,)), ((), ())),
            preferred_element_type=jnp.float32,
        )
        band[a] = turned.astype(jnp.bfloat16)


def first_kernel(first, groups, group, kernel, off, slc, *rest):
    outs, (head, tail, slab, band, gains, shifts, sems) = rest[:groups], rest[groups:]
    acq, _, lines, cols = slc.shape
    width = cols // groups

    def columns(s):
        return pl.ds(pl.multiple_of((group[0] ^ s) * width, width), width)

    order = [*range(1, groups), 0]
    small = [
        pltpu.make_async_copy(kernel, gains, sems.at[groups]),
        pltpu.make_async_copy(off, shifts, sems.at[groups + 1]),
    ]
    for copy in small:
        copy.start()
    copies = {}
    for s in order:
        at = columns(s)
        copies[s] = pltpu.make_async_copy(slc.at[:, :, :, at], slab.at[:, :, :, at], sems.at[s])
        copies[s].start()
    for copy in small:
        copy.wait()
    build_bands(first, [(0, lines)], group, gains, shifts, band)
    for s in order:
        copies[s].wait()
        at = columns(s)
        for a in range(acq):
            for x in range(2):
                total = jnp.dot(band[a], slab[a, x, :, at], preferred_element_type=jnp.float32)
                outs[s][a, x] = total.astype(jnp.bfloat16)
    head[...] = slab[:, :, :HALO, :]
    tail[...] = slab[:, :, lines - HALO :, :]


def edge_kernel(first, groups, begin, count, halo_at, group, kernel, off, slab, halo, *rest):
    outs, band = rest[:groups], rest[groups]
    acq, _, _, cols = slab.shape
    width = cols // groups
    build_bands(first, [(begin, count), (halo_at, HALO)], group, kernel, off, band)
    for s in [*range(1, groups), 0]:
        at = pl.ds(pl.multiple_of((group[0] ^ s) * width, width), width)
        for a in range(acq):
            for x in range(2):
                lines = jnp.concatenate(
                    [slab[a, x, begin : begin + count, at], halo[a, x, :, at]], axis=0
                )
                total = jnp.dot(band[a], lines, preferred_element_type=jnp.float32)
                outs[s][a, x] = total.astype(jnp.bfloat16)


SMEM = pl.BlockSpec(memory_space=pltpu.SMEM)
VMEM = pl.BlockSpec(memory_space=pltpu.VMEM)
ANY = pl.BlockSpec(memory_space=pl.ANY)


def resample_cost(acq, cols, rows):
    return pl.CostEstimate(
        flops=2 * acq * 2 * CHUNK * rows * cols,
        bytes_accessed=acq * 2 * (rows + CHUNK) * cols * 2,
        transcendentals=0,
    )


def resample_first(first, group, kernel, offsets, slc, groups):
    acq, _, lines, cols = slc.shape
    piece = pltpu.VMEM((acq, 2, CHUNK, cols // groups), jnp.bfloat16)
    halo = pltpu.VMEM((acq, 2, HALO, cols), jnp.bfloat16)
    slab = pltpu.VMEM(slc.shape, jnp.bfloat16)
    return pl.pallas_call(
        functools.partial(first_kernel, first, groups),
        in_specs=[SMEM, ANY, ANY, ANY],
        out_specs=[VMEM] * (groups + 3),
        out_shape=[piece] * groups + [halo, halo, slab],
        scratch_shapes=[
            pltpu.VMEM((acq, CHUNK, lines), jnp.bfloat16),
            pltpu.VMEM(kernel.shape, kernel.dtype),
            pltpu.VMEM(offsets.shape, offsets.dtype),
            pltpu.SemaphoreType.DMA((groups + 2,)),
        ],
        compiler_params=pltpu.CompilerParams(vmem_limit_bytes=16 * MIB),
        cost_estimate=resample_cost(acq, cols, lines),
        name="resample_first",
    )(group, kernel, offsets, slc)


def resample_edge(first, begin, count, halo_at, group, kernel, offsets, slab, halo, groups):
    acq, _, lines, cols = slab.shape
    piece = pltpu.VMEM((acq, 2, CHUNK, cols // groups), jnp.bfloat16)
    return pl.pallas_call(
        functools.partial(edge_kernel, first, groups, begin, count, halo_at),
        in_specs=[SMEM, VMEM, VMEM, VMEM, VMEM],
        out_specs=[VMEM] * groups,
        out_shape=[piece] * groups,
        scratch_shapes=[pltpu.VMEM((acq, CHUNK, count + HALO), jnp.bfloat16)],
        compiler_params=pltpu.CompilerParams(vmem_limit_bytes=16 * MIB),
        cost_estimate=resample_cost(acq, cols, count + HALO),
        name="resample_edge",
    )(group, kernel, offsets, slab, halo)


def interfere_kernel(groups, place, table, *rest):
    blocks, (out, parts, terms, pooled, flat, inverse, slab, sem) = rest[:groups], rest[-8:]
    acq, _, lines, width = blocks[0].shape
    looks = lines // LOOK_R
    count = table.shape[1]
    windows = width // LOOK_C
    both = 2 * looks
    total_acq = groups * acq
    slots = total_acq * (total_acq - 1) // 2
    tiles = width // LANES

    def pool(tile):
        row = lax.broadcasted_iota(jnp.int32, (2 * LANES, windows), 0)
        window = lax.broadcasted_iota(jnp.int32, (2 * LANES, windows), 1)
        wanted = tile * (LANES // LOOK_C) + (row % LANES) // LOOK_C
        return jnp.where(wanted == window, 1.0, 0.0).astype(jnp.bfloat16)

    def put(row, field):
        first = field.astype(jnp.bfloat16)
        terms[row : row + both, :LANES] = first
        terms[row : row + both, LANES:] = (field - first.astype(jnp.float32)).astype(jnp.bfloat16)

    def settle(tile):
        pooled[...] += jnp.dot(terms[...], pool(tile), preferred_element_type=jnp.float32)

    def unpack(tile):
        at = pl.ds(pl.multiple_of(tile * LANES, LANES), LANES)
        for r, block in enumerate(blocks):
            for a in range(acq):
                real = block[a, 0, :, at].astype(jnp.float32) * 0.125
                imag = block[a, 1, :, at].astype(jnp.float32) * 0.125
                parts[r * acq + a, 0] = real
                parts[r * acq + a, 1] = imag
                parts[r * acq + a, 2] = real + imag
                parts[r * acq + a, 3] = real - imag

    def cross(pairs):
        sums = {pair: [0.0, 0.0, 0.0] for pair in pairs}
        for j in range(LOOK_R):
            at = slice(j * looks, (j + 1) * looks)
            left = {i: [parts[i, c, at, :] for c in (2, 0, 1)] for i in sorted({i for i, _ in pairs})}
            right = {i: [parts[i, c, at, :] for c in (0, 2, 3)] for i in sorted({i for _, i in pairs})}
            for pair in pairs:
                for t in range(3):
                    sums[pair][t] = sums[pair][t] + left[pair[0]][t] * right[pair[1]][t]
        for i, k in pairs:
            one, two, three = sums[i, k]
            slot = i * (2 * total_acq - i - 1) // 2 + k - i - 1
            put(slot * both, jnp.concatenate([one - three, one - two], axis=0))

    def powers(members):
        fields = []
        for i in members:
            total = 0.0
            for j in range(LOOK_R):
                for c in range(2):
                    value = parts[i, c, j * looks : (j + 1) * looks, :]
                    total = total + value * value
            fields.append(total)
        put(slots * both + members[0] * looks, jnp.concatenate(fields, axis=0))

    def work(tile):
        unpack(tile)
        for r in range(groups):
            for q in range(r, groups):
                cross(
                    [
                        (i, k)
                        for i in range(r * acq, (r + 1) * acq)
                        for k in range(q * acq, (q + 1) * acq)
                        if i < k
                    ]
                )
        for i in range(0, total_acq, 2):
            powers((i, i + 1))

    def turn(tile, carry):
        settle(tile - 1)
        work(tile)
        return carry

    pooled[...] = jnp.zeros(pooled.shape, jnp.float32)
    work(0)
    lax.fori_loop(1, tiles, turn, 0)
    settle(tiles - 1)

    inverse[...] = lax.rsqrt(pooled[slots * both :, :] + 1e-6)

    def select(p, carry):
        at = pl.multiple_of(table[0, p] * both, both)
        m = pl.multiple_of(table[1, p] * looks, looks)
        s = pl.multiple_of(table[2, p] * looks, looks)
        scale = inverse[pl.ds(m, looks), :] * inverse[pl.ds(s, looks), :]
        turned = scale * table[3, p].astype(jnp.float32)
        value = pooled[pl.ds(at, both), :] * jnp.concatenate([scale, turned], axis=0)
        flat[pl.ds(pl.multiple_of(p * both, both), both), :] = value
        return carry

    lax.fori_loop(0, count, select, 0, unroll=max(b for b in range(1, 7) if count % b == 0))
    for x in range(2):
        for g in range(looks):
            slab[x, g] = flat[pl.ds(x * looks + g, count, stride=both), :].T
    copy = pltpu.make_async_copy(slab, out.at[:, pl.ds(place * looks, looks)], sem)
    copy.start()
    copy.wait()


def interfere(place, chunks, table, blocks, before):
    groups = len(blocks)
    acq, _, lines, width = blocks[0].shape
    looks, windows, count = lines // LOOK_R, width // LOOK_C, table.shape[1]
    total = groups * acq
    rows = (total * (total - 1) + total) * looks
    extra = [] if before is None else [before]
    return pl.pallas_call(
        functools.partial(interfere_kernel, groups, place),
        in_specs=[SMEM] + [VMEM] * groups + [ANY] * len(extra),
        out_specs=ANY,
        out_shape=pltpu.HBM((2, chunks * looks, windows, count), jnp.float32),
        scratch_shapes=[
            pltpu.VMEM((total, 4, lines, LANES), jnp.float32),
            pltpu.VMEM((rows, 2 * LANES), jnp.bfloat16),
            pltpu.VMEM((rows, windows), jnp.float32),
            pltpu.VMEM((count * 2 * looks, windows), jnp.float32),
            pltpu.VMEM((total * looks, windows), jnp.float32),
            pltpu.VMEM((2, looks, windows, count), jnp.float32),
            pltpu.SemaphoreType.DMA,
        ],
        input_output_aliases={} if before is None else {1 + groups: 0},
        compiler_params=pltpu.CompilerParams(vmem_limit_bytes=16 * MIB),
        cost_estimate=pl.CostEstimate(
            flops=count * 8 * lines * width,
            bytes_accessed=groups * acq * 2 * lines * width * 2,
            transcendentals=0,
        ),
        name="interfere",
    )(table, *blocks, *extra)


def pair_table(pairs, groups, acq, mine):
    total = groups * acq
    near = ((pairs // acq) ^ mine) * acq + pairs % acq
    m, s = near[:, 0], near[:, 1]
    low, high = jnp.minimum(m, s), jnp.maximum(m, s)
    slot = low * (2 * total - low - 1) // 2 + high - low - 1
    return jnp.stack([slot, m, s, jnp.where(m < s, 1, -1)]).astype(jnp.int32)


def local(slc, offsets, weights, pairs):
    acq, _, lines, cols = slc.shape
    groups = lax.axis_size("acq")
    size = lax.axis_size("pix")
    group = jnp.reshape(lax.axis_index("acq"), (1,)).astype(jnp.int32)
    kernel = weights.T
    table = pair_table(pairs, groups, acq, group[0])
    chunks = lines // CHUNK
    reach = CHUNK + TILE * 2

    up = [(i, i + 1) for i in range(size - 1)]
    down = [(j, i) for i, j in up]

    def send(blocks):
        moved = [blocks[0]]
        for s in range(1, groups):
            moved.append(lax.ppermute(blocks[s], "acq", [(i, i ^ s) for i in range(groups)]))
        return moved

    *blocks, head, tail, slab = resample_first(
        CHUNK, group, *[pltpu.with_memory_space_constraint(t, pltpu.HBM) for t in (kernel, offsets, slc)], groups
    )
    above = lax.ppermute(tail, "pix", up)
    below = lax.ppermute(head, "pix", down)
    middle = send(blocks)
    top = send(
        resample_edge(0, 0, reach, -HALO, group, kernel, offsets, slab, above, groups)
    )
    late = resample_edge(
        lines - CHUNK, lines - reach, reach, lines, group, kernel, offsets, slab, below, groups
    )
    late, middle = lax.optimization_barrier((late, middle))
    bottom = send(late)
    result = None
    for place, moved in ((1, middle), (0, top), (2, bottom)):
        result = interfere(place, chunks, table, moved, result)
    return jnp.transpose(result, (0, 3, 1, 2))


def solution(mesh):
    placed = (P("acq", None, "pix", None), P("acq", "pix"), P(), P())
    return jax.shard_map(
        local, mesh=mesh, in_specs=placed, out_specs=P(None, None, "pix", "acq"), check_vma=False
    )
```

```python
import functools

import jax
import jax.numpy as jnp
from jax import lax
from jax.experimental import pallas as pl
from jax.experimental.pallas import tpu as pltpu
from jax.sharding import PartitionSpec as P

LOOK_R = 4
LOOK_C = 16
CHUNK = 32
HALO = 24
TILE = 16
LANES = 128
MIB = 1024 * 1024


def build_bands(first, sources, group, kernel, off, band):
    acq, taps = off.shape[0], kernel.shape[0]
    gains = kernel[...].astype(jnp.float32)
    lane = lax.broadcasted_iota(jnp.int32, gains.shape, 1)
    rows = sum(count for _, count in sources)
    index = lax.broadcasted_iota(jnp.int32, (rows, CHUNK), 0)
    source = jnp.zeros((rows, CHUNK), jnp.int32)
    at = 0
    for begin, count in sources:
        source = jnp.where(index >= at, index + (begin - at), source)
        at += count
    target = first + lax.broadcasted_iota(jnp.int32, (rows, CHUNK), 1)
    base = source - target + (taps // 2 - 1)
    row = lax.broadcasted_iota(jnp.int32, (CHUNK, CHUNK), 0)
    col = lax.broadcasted_iota(jnp.int32, (CHUNK, CHUNK), 1)
    blocks = CHUNK // LOOK_R
    order = jnp.where(col == (row % blocks) * LOOK_R + row // blocks, 1.0, 0.0).astype(jnp.bfloat16)
    for a in range(acq):
        tap = base - off[a : a + 1, first : first + CHUNK]
        total = jnp.zeros((rows, CHUNK), jnp.float32)
        gain = jnp.sum(jnp.where(lane == group[0] * acq + a, gains, 0.0), axis=1, keepdims=True)
        for k in range(taps):
            total = jnp.where(tap == k, gain[k : k + 1, :], total)
        turned = lax.dot_general(
            order, total.astype(jnp.bfloat16), (((1,), (1,)), ((), ())),
            preferred_element_type=jnp.float32,
        )
        band[a] = turned.astype(jnp.bfloat16)


def first_kernel(first, groups, group, kernel, off, slc, *rest):
    outs, (head, tail, slab, band, gains, shifts, sems) = rest[:groups], rest[groups:]
    acq, _, lines, cols = slc.shape
    width = cols // groups

    def columns(s):
        return pl.ds(pl.multiple_of((group[0] ^ s) * width, width), width)

    order = [*range(1, groups), 0]
    small = [
        pltpu.make_async_copy(kernel, gains, sems.at[groups]),
        pltpu.make_async_copy(off, shifts, sems.at[groups + 1]),
    ]
    for copy in small:
        copy.start()
    copies = {}
    for s in order:
        at = columns(s)
        copies[s] = pltpu.make_async_copy(slc.at[:, :, :, at], slab.at[:, :, :, at], sems.at[s])
        copies[s].start()
    for copy in small:
        copy.wait()
    build_bands(first, [(0, lines)], group, gains, shifts, band)
    for s in order:
        copies[s].wait()
        at = columns(s)
        for a in range(acq):
            for x in range(2):
                total = jnp.dot(band[a], slab[a, x, :, at], preferred_element_type=jnp.float32)
                outs[s][a, x] = total.astype(jnp.bfloat16)
    head[...] = slab[:, :, :HALO, :]
    tail[...] = slab[:, :, lines - HALO :, :]


def edge_kernel(first, groups, begin, count, halo_at, group, kernel, off, slab, halo, *rest):
    outs, band = rest[:groups], rest[groups]
    acq, _, _, cols = slab.shape
    width = cols // groups
    build_bands(first, [(begin, count), (halo_at, HALO)], group, kernel, off, band)
    for s in [*range(1, groups), 0]:
        at = pl.ds(pl.multiple_of((group[0] ^ s) * width, width), width)
        for a in range(acq):
            for x in range(2):
                lines = jnp.concatenate(
                    [slab[a, x, begin : begin + count, at], halo[a, x, :, at]], axis=0
                )
                total = jnp.dot(band[a], lines, preferred_element_type=jnp.float32)
                outs[s][a, x] = total.astype(jnp.bfloat16)


SMEM = pl.BlockSpec(memory_space=pltpu.SMEM)
VMEM = pl.BlockSpec(memory_space=pltpu.VMEM)
ANY = pl.BlockSpec(memory_space=pl.ANY)


def resample_cost(acq, cols, rows):
    return pl.CostEstimate(
        flops=2 * acq * 2 * CHUNK * rows * cols,
        bytes_accessed=acq * 2 * (rows + CHUNK) * cols * 2,
        transcendentals=0,
    )


def resample_first(first, group, kernel, offsets, slc, groups):
    acq, _, lines, cols = slc.shape
    piece = pltpu.VMEM((acq, 2, CHUNK, cols // groups), jnp.bfloat16)
    halo = pltpu.VMEM((acq, 2, HALO, cols), jnp.bfloat16)
    slab = pltpu.VMEM(slc.shape, jnp.bfloat16)
    return pl.pallas_call(
        functools.partial(first_kernel, first, groups),
        in_specs=[SMEM, ANY, ANY, ANY],
        out_specs=[VMEM] * (groups + 3),
        out_shape=[piece] * groups + [halo, halo, slab],
        scratch_shapes=[
            pltpu.VMEM((acq, CHUNK, lines), jnp.bfloat16),
            pltpu.VMEM(kernel.shape, kernel.dtype),
            pltpu.VMEM(offsets.shape, offsets.dtype),
            pltpu.SemaphoreType.DMA((groups + 2,)),
        ],
        compiler_params=pltpu.CompilerParams(vmem_limit_bytes=16 * MIB),
        cost_estimate=resample_cost(acq, cols, lines),
        name="resample_first",
    )(group, kernel, offsets, slc)


def resample_edge(first, begin, count, halo_at, group, kernel, offsets, slab, halo, groups):
    acq, _, lines, cols = slab.shape
    piece = pltpu.VMEM((acq, 2, CHUNK, cols // groups), jnp.bfloat16)
    return pl.pallas_call(
        functools.partial(edge_kernel, first, groups, begin, count, halo_at),
        in_specs=[SMEM, VMEM, VMEM, VMEM, VMEM],
        out_specs=[VMEM] * groups,
        out_shape=[piece] * groups,
        scratch_shapes=[pltpu.VMEM((acq, CHUNK, count + HALO), jnp.bfloat16)],
        compiler_params=pltpu.CompilerParams(vmem_limit_bytes=16 * MIB),
        cost_estimate=resample_cost(acq, cols, count + HALO),
        name="resample_edge",
    )(group, kernel, offsets, slab, halo)


def interfere_kernel(groups, place, table, *rest):
    blocks, (out, parts, halves, pooled, flat, inverse, turned, slab, sem) = rest[:groups], rest[-9:]
    acq, _, lines, width = blocks[0].shape
    looks = lines // LOOK_R
    count = table.shape[1]
    total = groups * acq
    slots = total * (total - 1) // 2
    tiles = width // LANES
    lane = lax.broadcasted_iota(jnp.int32, (looks, LANES), 1)
    steps = [LOOK_C >> (level + 1) for level in range(LOOK_C.bit_length() - 1)]

    def merge(one, two, step):
        left = one + pltpu.roll(one, LANES - step, 1)
        right = two + pltpu.roll(two, step, 1)
        return jnp.where((lane & step) == 0, left, right)

    def unpack(tile):
        at = pl.ds(pl.multiple_of(tile * LANES, LANES), LANES)
        for r, block in enumerate(blocks):
            for a in range(acq):
                real = block[a, 0, :, at].astype(jnp.float32) * 0.125
                imag = block[a, 1, :, at].astype(jnp.float32) * 0.125
                parts[r * acq + a, 0] = real
                parts[r * acq + a, 1] = imag
                parts[r * acq + a, 2] = real + imag
                parts[r * acq + a, 3] = real - imag

    def cross(tile, pairs):
        sums = {pair: [0.0, 0.0, 0.0] for pair in pairs}
        for j in range(LOOK_R):
            at = slice(j * looks, (j + 1) * looks)
            left = {i: [parts[i, c, at, :] for c in (2, 0, 1)] for i in sorted({i for i, _ in pairs})}
            right = {i: [parts[i, c, at, :] for c in (0, 2, 3)] for i in sorted({i for _, i in pairs})}
            for pair in pairs:
                for t in range(3):
                    sums[pair][t] = sums[pair][t] + left[pair[0]][t] * right[pair[1]][t]
        for i, k in pairs:
            one, two, three = sums[i, k]
            slot = i * (2 * total - i - 1) // 2 + k - i - 1
            halves[tile, slot] = merge(one - three, one - two, steps[0])

    def power(tile, i):
        field = 0.0
        for j in range(LOOK_R):
            for c in range(2):
                value = parts[i, c, j * looks : (j + 1) * looks, :]
                field = field + value * value
        halves[tile, slots + i] = merge(field, field, steps[0])

    def work(tile, carry):
        unpack(tile)
        for r in range(groups):
            for q in range(r, groups):
                first = range(r * acq, (r + 1) * acq)
                second = range(q * acq, (q + 1) * acq)
                cross(tile, [(i, k) for i in first for k in second if i < k])
        for i in range(total):
            power(tile, i)
        return carry

    def fold(slot):
        fields = [halves[tile, slot] for tile in range(tiles)]
        for step in steps[1:]:
            fields = [
                merge(fields[i], fields[min(i + 1, len(fields) - 1)], step)
                for i in range(0, len(fields), 2)
            ]
        return fields[0]

    def fold_slots(b, carry):
        for u in range(acq):
            pooled[b * acq + u] = fold(b * acq + u)
        return carry

    lax.fori_loop(0, tiles, work, 0)
    for i in range(total):
        inverse[i] = lax.rsqrt(fold(slots + i) + 1e-6)
    lax.fori_loop(0, slots // acq, fold_slots, 0)

    def select(p, carry):
        sign = table[3, p].astype(jnp.float32)
        scale = inverse[table[1, p]] * inverse[table[2, p]]
        value = pooled[table[0, p]] * scale
        at = pl.multiple_of(p * looks, looks)
        flat[pl.ds(at, looks), :] = jnp.where((lane & steps[0]) == 0, value, value * sign)
        return carry

    lax.fori_loop(0, count, select, 0, unroll=max(b for b in range(1, 7) if count % b == 0))
    span = LANES // LOOK_C
    for g in range(looks):
        turned[g] = flat[pl.ds(g, count, stride=looks), :].T
        for x in range(2):
            for tile in range(tiles):
                t = x * steps[0] + sum(((tile >> n) & 1) * step for n, step in enumerate(steps[1:]))
                slab[x, g, tile * span : (tile + 1) * span, :] = turned[g, pl.ds(t, span, stride=LOOK_C), :]
    copy = pltpu.make_async_copy(slab, out.at[:, pl.ds(place * looks, looks)], sem)
    copy.start()
    copy.wait()


def interfere(place, chunks, table, blocks, before):
    groups = len(blocks)
    acq, _, lines, width = blocks[0].shape
    looks, windows, count = lines // LOOK_R, width // LOOK_C, table.shape[1]
    total = groups * acq
    rows = total * (total - 1) // 2 + total
    extra = [] if before is None else [before]
    return pl.pallas_call(
        functools.partial(interfere_kernel, groups, place),
        in_specs=[SMEM] + [VMEM] * groups + [ANY] * len(extra),
        out_specs=ANY,
        out_shape=pltpu.HBM((2, chunks * looks, windows, count), jnp.float32),
        scratch_shapes=[
            pltpu.VMEM((total, 4, lines, LANES), jnp.float32),
            pltpu.VMEM((width // LANES, rows, looks, LANES), jnp.float32),
            pltpu.VMEM((rows, looks, LANES), jnp.float32),
            pltpu.VMEM((count * looks, LANES), jnp.float32),
            pltpu.VMEM((total, looks, LANES), jnp.float32),
            pltpu.VMEM((looks, LANES, count), jnp.float32),
            pltpu.VMEM((2, looks, windows, count), jnp.float32),
            pltpu.SemaphoreType.DMA,
        ],
        input_output_aliases={} if before is None else {1 + groups: 0},
        compiler_params=pltpu.CompilerParams(vmem_limit_bytes=16 * MIB),
        cost_estimate=pl.CostEstimate(
            flops=count * 8 * lines * width,
            bytes_accessed=groups * acq * 2 * lines * width * 2 * 12,
            transcendentals=0,
        ),
        name="interfere",
    )(table, *blocks, *extra)


def pair_table(pairs, groups, acq, mine):
    total = groups * acq
    near = ((pairs // acq) ^ mine) * acq + pairs % acq
    m, s = near[:, 0], near[:, 1]
    low, high = jnp.minimum(m, s), jnp.maximum(m, s)
    slot = low * (2 * total - low - 1) // 2 + high - low - 1
    return jnp.stack([slot, m, s, jnp.where(m < s, 1, -1)]).astype(jnp.int32)


def local(slc, offsets, weights, pairs):
    acq, _, lines, cols = slc.shape
    groups = lax.axis_size("acq")
    size = lax.axis_size("pix")
    group = jnp.reshape(lax.axis_index("acq"), (1,)).astype(jnp.int32)
    kernel = weights.T
    table = pair_table(pairs, groups, acq, group[0])
    chunks = lines // CHUNK
    reach = CHUNK + TILE * 2

    up = [(i, i + 1) for i in range(size - 1)]
    down = [(j, i) for i, j in up]

    def send(blocks):
        moved = [blocks[0]]
        for s in range(1, groups):
            moved.append(lax.ppermute(blocks[s], "acq", [(i, i ^ s) for i in range(groups)]))
        return moved

    *blocks, head, tail, slab = resample_first(
        CHUNK, group, *[pltpu.with_memory_space_constraint(t, pltpu.HBM) for t in (kernel, offsets, slc)], groups
    )
    above = lax.ppermute(tail, "pix", up)
    below = lax.ppermute(head, "pix", down)
    above, below = lax.optimization_barrier((above, below))
    middle = send(blocks)
    top = send(
        resample_edge(0, 0, reach, -HALO, group, kernel, offsets, slab, above, groups)
    )
    late = resample_edge(
        lines - CHUNK, lines - reach, reach, lines, group, kernel, offsets, slab, below, groups
    )
    bottom = send(late)
    result = None
    for place, moved in ((1, middle), (0, top), (2, bottom)):
        result = interfere(place, chunks, table, moved, result)
    return jnp.transpose(result, (0, 3, 1, 2))


def solution(mesh):
    placed = (P("acq", None, "pix", None), P("acq", "pix"), P(), P())
    return jax.shard_map(
        local, mesh=mesh, in_specs=placed, out_specs=P(None, None, "pix", "acq"), check_vma=False
    )
```

```python
import functools

import jax
import jax.numpy as jnp
from jax import lax
from jax.experimental import pallas as pl
from jax.experimental.pallas import tpu as pltpu
from jax.sharding import PartitionSpec as P

LOOK_R = 4
LOOK_C = 16
CHUNK = 32
HALO = 24
TILE = 16
LANES = 128
MIB = 1024 * 1024


def build_bands(first, sources, group, kernel, off, band):
    acq, taps = off.shape[0], kernel.shape[0]
    gains = kernel[...].astype(jnp.float32) * 0.125
    lane = lax.broadcasted_iota(jnp.int32, gains.shape, 1)
    rows = sum(count for _, count in sources)
    index = lax.broadcasted_iota(jnp.int32, (rows, CHUNK), 0)
    source = jnp.zeros((rows, CHUNK), jnp.int32)
    at = 0
    for begin, count in sources:
        source = jnp.where(index >= at, index + (begin - at), source)
        at += count
    target = first + lax.broadcasted_iota(jnp.int32, (rows, CHUNK), 1)
    base = source - target + (taps // 2 - 1)
    row = lax.broadcasted_iota(jnp.int32, (CHUNK, CHUNK), 0)
    col = lax.broadcasted_iota(jnp.int32, (CHUNK, CHUNK), 1)
    blocks = CHUNK // LOOK_R
    order = jnp.where(col == (row % blocks) * LOOK_R + row // blocks, 1.0, 0.0).astype(jnp.bfloat16)
    for a in range(acq):
        tap = base - off[a : a + 1, first : first + CHUNK]
        total = jnp.zeros((rows, CHUNK), jnp.float32)
        gain = jnp.sum(jnp.where(lane == group[0] * acq + a, gains, 0.0), axis=1, keepdims=True)
        for k in range(taps):
            total = jnp.where(tap == k, gain[k : k + 1, :], total)
        turned = lax.dot_general(
            order, total.astype(jnp.bfloat16), (((1,), (1,)), ((), ())),
            preferred_element_type=jnp.float32,
        )
        band[a] = turned.astype(jnp.bfloat16)


def first_kernel(first, groups, group, kernel, off, slc, *rest):
    outs, (head, tail, slab, band, gains, shifts, sems) = rest[:groups], rest[groups:]
    acq, _, lines, cols = slc.shape
    width = cols // groups

    def columns(s):
        return pl.ds(pl.multiple_of((group[0] ^ s) * width, width), width)

    order = [*range(1, groups), 0]
    small = [
        pltpu.make_async_copy(kernel, gains, sems.at[groups]),
        pltpu.make_async_copy(off, shifts, sems.at[groups + 1]),
    ]
    for copy in small:
        copy.start()
    copies = {}
    for s in order:
        at = columns(s)
        copies[s] = pltpu.make_async_copy(slc.at[:, :, :, at], slab.at[:, :, :, at], sems.at[s])
        copies[s].start()
    for copy in small:
        copy.wait()
    build_bands(first, [(0, lines)], group, gains, shifts, band)
    for s in order:
        copies[s].wait()
        at = columns(s)
        for a in range(acq):
            for x in range(2):
                total = jnp.dot(band[a], slab[a, x, :, at], preferred_element_type=jnp.float32)
                outs[s][a, x] = total.astype(jnp.bfloat16)
    head[...] = slab[:, :, :HALO, :]
    tail[...] = slab[:, :, lines - HALO :, :]


def edge_kernel(first, groups, begin, count, halo_at, group, kernel, off, slab, halo, *rest):
    outs, band = rest[:groups], rest[groups]
    acq, _, _, cols = slab.shape
    width = cols // groups
    build_bands(first, [(begin, count), (halo_at, HALO)], group, kernel, off, band)
    for s in [*range(1, groups), 0]:
        at = pl.ds(pl.multiple_of((group[0] ^ s) * width, width), width)
        for a in range(acq):
            for x in range(2):
                lines = jnp.concatenate(
                    [slab[a, x, begin : begin + count, at], halo[a, x, :, at]], axis=0
                )
                total = jnp.dot(band[a], lines, preferred_element_type=jnp.float32)
                outs[s][a, x] = total.astype(jnp.bfloat16)


SMEM = pl.BlockSpec(memory_space=pltpu.SMEM)
VMEM = pl.BlockSpec(memory_space=pltpu.VMEM)
ANY = pl.BlockSpec(memory_space=pl.ANY)


def resample_cost(acq, cols, rows):
    return pl.CostEstimate(
        flops=2 * acq * 2 * CHUNK * rows * cols,
        bytes_accessed=acq * 2 * (rows + CHUNK) * cols * 2,
        transcendentals=0,
    )


def resample_first(first, group, kernel, offsets, slc, groups):
    acq, _, lines, cols = slc.shape
    piece = pltpu.VMEM((acq, 2, CHUNK, cols // groups), jnp.bfloat16)
    halo = pltpu.VMEM((acq, 2, HALO, cols), jnp.bfloat16)
    slab = pltpu.VMEM(slc.shape, jnp.bfloat16)
    return pl.pallas_call(
        functools.partial(first_kernel, first, groups),
        in_specs=[SMEM, ANY, ANY, ANY],
        out_specs=[VMEM] * (groups + 3),
        out_shape=[piece] * groups + [halo, halo, slab],
        scratch_shapes=[
            pltpu.VMEM((acq, CHUNK, lines), jnp.bfloat16),
            pltpu.VMEM(kernel.shape, kernel.dtype),
            pltpu.VMEM(offsets.shape, offsets.dtype),
            pltpu.SemaphoreType.DMA((groups + 2,)),
        ],
        compiler_params=pltpu.CompilerParams(vmem_limit_bytes=16 * MIB),
        cost_estimate=resample_cost(acq, cols, lines),
        name="resample_first",
    )(group, kernel, offsets, slc)


def resample_edge(first, begin, count, halo_at, group, kernel, offsets, slab, halo, groups):
    acq, _, lines, cols = slab.shape
    piece = pltpu.VMEM((acq, 2, CHUNK, cols // groups), jnp.bfloat16)
    return pl.pallas_call(
        functools.partial(edge_kernel, first, groups, begin, count, halo_at),
        in_specs=[SMEM, VMEM, VMEM, VMEM, VMEM],
        out_specs=[VMEM] * groups,
        out_shape=[piece] * groups,
        scratch_shapes=[pltpu.VMEM((acq, CHUNK, count + HALO), jnp.bfloat16)],
        compiler_params=pltpu.CompilerParams(vmem_limit_bytes=16 * MIB),
        cost_estimate=resample_cost(acq, cols, count + HALO),
        name="resample_edge",
    )(group, kernel, offsets, slab, halo)


def slot_of(low, high):
    return high * (high - 1) // 2 + low


def look_sums(blocks, begin, parts, terms, sums, slot_rows, power_rows):
    acq, _, lines, width = blocks[0].shape
    looks = lines // LOOK_R
    windows = width // LOOK_C
    both = 2 * looks
    tiles = width // LANES
    total, fresh = len(blocks) * acq, begin * acq
    base = slot_of(0, fresh)
    split = (slot_of(0, total) - base) * both
    used = split + (total - fresh) * looks

    def pool(tile):
        row = lax.broadcasted_iota(jnp.int32, (2 * LANES, windows), 0)
        window = lax.broadcasted_iota(jnp.int32, (2 * LANES, windows), 1)
        wanted = tile * (LANES // LOOK_C) + (row % LANES) // LOOK_C
        return jnp.where(wanted == window, 1.0, 0.0).astype(jnp.bfloat16)

    def put(row, field):
        first = field.astype(jnp.bfloat16)
        terms[row : row + both, :LANES] = first
        terms[row : row + both, LANES:] = (field - first.astype(jnp.float32)).astype(jnp.bfloat16)

    def settle(tile):
        result = jnp.dot(terms[...], pool(tile), preferred_element_type=jnp.float32)
        sums[slot_rows : slot_rows + split, :] += result[:split]
        sums[power_rows : power_rows + used - split, :] += result[split:used]

    def unpack(tile):
        at = pl.ds(pl.multiple_of(tile * LANES, LANES), LANES)
        for r, block in enumerate(blocks):
            for a in range(acq):
                real = block[a, 0, :, at].astype(jnp.float32)
                imag = block[a, 1, :, at].astype(jnp.float32)
                parts[r * acq + a, 0] = real
                parts[r * acq + a, 1] = imag
                parts[r * acq + a, 2] = real + imag
                parts[r * acq + a, 3] = real - imag

    def cross(pairs):
        totals = {pair: [0.0, 0.0, 0.0] for pair in pairs}
        for j in range(LOOK_R):
            at = slice(j * looks, (j + 1) * looks)
            left = {i: [parts[i, c, at, :] for c in (2, 0, 1)] for i in sorted({i for i, _ in pairs})}
            right = {i: [parts[i, c, at, :] for c in (0, 2, 3)] for i in sorted({i for _, i in pairs})}
            for pair in pairs:
                for t in range(3):
                    totals[pair][t] = totals[pair][t] + left[pair[0]][t] * right[pair[1]][t]
        for i, k in pairs:
            one, two, three = totals[i, k]
            put((slot_of(i, k) - base) * both, jnp.concatenate([one - three, one - two], axis=0))

    def powers(members):
        fields = []
        for i in members:
            field = 0.0
            for j in range(LOOK_R):
                for c in range(2):
                    value = parts[i, c, j * looks : (j + 1) * looks, :]
                    field = field + value * value
            fields.append(field)
        put(split + (members[0] - fresh) * looks, jnp.concatenate(fields, axis=0))

    def work(tile):
        unpack(tile)
        for q in range(begin, len(blocks)):
            for r in range(q + 1):
                first = range(r * acq, (r + 1) * acq)
                second = range(q * acq, (q + 1) * acq)
                cross([(i, k) for i in first for k in second if i < k])
        for i in range(fresh, total, 2):
            powers((i, min(i + 1, total - 1)))

    def turn(tile, carry):
        settle(tile - 1)
        work(tile)
        return carry

    work(0)
    lax.fori_loop(1, tiles, turn, 0)
    settle(tiles - 1)


def near_kernel(groups, *rest):
    blocks, (sums, parts, terms) = rest[:groups], rest[groups:]
    acq, _, lines, _ = blocks[0].shape
    looks = lines // LOOK_R
    sums[...] = jnp.zeros(sums.shape, jnp.float32)
    look_sums(blocks, 0, parts, terms, sums, 0, slot_of(0, groups * acq) * 2 * looks)


def interfere_kernel(groups, known, place, table, *rest):
    blocks, rest = rest[:groups], rest[groups:]
    out, parts, terms, sums, flat, inverse, slab, sem = rest[-8:]
    acq, _, lines, width = blocks[0].shape
    looks = lines // LOOK_R
    count = table.shape[1]
    both = 2 * looks
    total, fresh = groups * acq, known * acq
    start, split = slot_of(0, fresh) * both, slot_of(0, total) * both
    sums[...] = jnp.zeros(sums.shape, jnp.float32)
    if known:
        near = rest[0]
        sums[:start, :] = near[:start, :]
        sums[split : split + fresh * looks, :] = near[start : start + fresh * looks, :]
    look_sums(blocks, known, parts, terms, sums, start, split + fresh * looks)
    inverse[...] = lax.rsqrt(sums[split : split + total * looks, :] + 1e-6)

    def select(p, carry):
        at = pl.multiple_of(table[0, p] * both, both)
        m = pl.multiple_of(table[1, p] * looks, looks)
        s = pl.multiple_of(table[2, p] * looks, looks)
        scale = inverse[pl.ds(m, looks), :] * inverse[pl.ds(s, looks), :]
        turned = scale * table[3, p].astype(jnp.float32)
        value = sums[pl.ds(at, both), :] * jnp.concatenate([scale, turned], axis=0)
        flat[pl.ds(pl.multiple_of(p * both, both), both), :] = value
        return carry

    lax.fori_loop(0, count, select, 0, unroll=max(b for b in range(1, 7) if count % b == 0))
    for x in range(2):
        for g in range(looks):
            slab[x, g] = flat[pl.ds(x * looks + g, count, stride=both), :].T
    copy = pltpu.make_async_copy(slab, out.at[:, pl.ds(place * looks, looks)], sem)
    copy.start()
    copy.wait()


def work_space(groups, known, acq, lines, looks):
    total, fresh = groups * acq, known * acq
    count = total - fresh
    rows = (slot_of(0, total) - slot_of(0, fresh)) * 2 * looks + (count + count % 2) * looks
    return [
        pltpu.VMEM((total, 4, lines, LANES), jnp.float32),
        pltpu.VMEM((rows, 2 * LANES), jnp.bfloat16),
    ]


def interfere_cost(pairs, acq, lines, width):
    return pl.CostEstimate(
        flops=pairs * 8 * lines * width,
        bytes_accessed=acq * 2 * lines * width * 2 * 12,
        transcendentals=0,
    )


def interfere_near(blocks):
    groups = len(blocks)
    acq, _, lines, width = blocks[0].shape
    looks, windows, total = lines // LOOK_R, width // LOOK_C, groups * acq
    return pl.pallas_call(
        functools.partial(near_kernel, groups),
        in_specs=[VMEM] * groups,
        out_specs=VMEM,
        out_shape=pltpu.VMEM(((slot_of(0, total) * 2 + total) * looks, windows), jnp.float32),
        scratch_shapes=work_space(groups, 0, acq, lines, looks),
        compiler_params=pltpu.CompilerParams(vmem_limit_bytes=16 * MIB),
        cost_estimate=interfere_cost(slot_of(0, total), total, lines, width),
        name="interfere_near",
    )(*blocks)


def interfere(place, chunks, table, blocks, near, known, before):
    groups = len(blocks)
    acq, _, lines, width = blocks[0].shape
    looks, windows, count = lines // LOOK_R, width // LOOK_C, table.shape[1]
    total = groups * acq
    near = [] if near is None else [near]
    extra = [] if before is None else [before]
    return pl.pallas_call(
        functools.partial(interfere_kernel, groups, known, place),
        in_specs=[SMEM] + [VMEM] * (groups + len(near)) + [ANY] * len(extra),
        out_specs=ANY,
        out_shape=pltpu.HBM((2, chunks * looks, windows, count), jnp.float32),
        scratch_shapes=work_space(groups, known, acq, lines, looks)
        + [
            pltpu.VMEM(((slot_of(0, total) * 2 + total) * looks, windows), jnp.float32),
            pltpu.VMEM((count * 2 * looks, windows), jnp.float32),
            pltpu.VMEM((total * looks, windows), jnp.float32),
            pltpu.VMEM((2, looks, windows, count), jnp.float32),
            pltpu.SemaphoreType.DMA,
        ],
        input_output_aliases={} if before is None else {1 + groups + len(near): 0},
        compiler_params=pltpu.CompilerParams(vmem_limit_bytes=16 * MIB),
        cost_estimate=interfere_cost(count, total, lines, width),
        name="interfere",
    )(table, *blocks, *near, *extra)


def pair_table(pairs, groups, acq, mine):
    close = ((pairs // acq) ^ mine) * acq + pairs % acq
    m, s = close[:, 0], close[:, 1]
    slot = slot_of(jnp.minimum(m, s), jnp.maximum(m, s))
    return jnp.stack([slot, m, s, jnp.where(m < s, 1, -1)]).astype(jnp.int32)


def local(slc, offsets, weights, pairs):
    acq, _, lines, cols = slc.shape
    groups = lax.axis_size("acq")
    size = lax.axis_size("pix")
    group = jnp.reshape(lax.axis_index("acq"), (1,)).astype(jnp.int32)
    kernel = weights.T
    table = pair_table(pairs, groups, acq, group[0])
    chunks = lines // CHUNK
    reach = CHUNK + TILE * 2

    up = [(i, i + 1) for i in range(size - 1)]
    down = [(j, i) for i, j in up]

    def send(blocks):
        moved = [blocks[0]]
        for s in range(1, groups):
            moved.append(lax.ppermute(blocks[s], "acq", [(i, i ^ s) for i in range(groups)]))
        return moved

    *blocks, head, tail, slab = resample_first(
        CHUNK, group, *[pltpu.with_memory_space_constraint(t, pltpu.HBM) for t in (kernel, offsets, slc)], groups
    )
    above = lax.ppermute(tail, "pix", up)
    below = lax.ppermute(head, "pix", down)
    above, below = lax.optimization_barrier((above, below))
    middle = send(blocks)
    top = send(
        resample_edge(0, 0, reach, -HALO, group, kernel, offsets, slab, above, groups)
    )
    late = resample_edge(
        lines - CHUNK, lines - reach, reach, lines, group, kernel, offsets, slab, below, groups
    )
    bottom = send(late)
    result = None
    for place, moved, known in ((1, middle, 0), (0, top, 0), (2, bottom, groups - 1)):
        near = None
        if known:
            mine, result = lax.optimization_barrier((moved[0], result))
            near = interfere_near([mine, *moved[1:known]])
        result = interfere(place, chunks, table, moved, near, known, result)
    return jnp.transpose(result, (0, 3, 1, 2))


def solution(mesh):
    placed = (P("acq", None, "pix", None), P("acq", "pix"), P(), P())
    return jax.shard_map(
        local, mesh=mesh, in_specs=placed, out_specs=P(None, None, "pix", "acq"), check_vma=False
    )
```

```python
import functools

import jax
import jax.numpy as jnp
from jax import lax
from jax.experimental import pallas as pl
from jax.experimental.pallas import tpu as pltpu
from jax.sharding import PartitionSpec as P

LOOK_R = 4
LOOK_C = 16
CHUNK = 32
HALO = 24
TILE = 16
LANES = 128
MIB = 1024 * 1024


def build_bands(first, sources, group, kernel, shift, band):
    acq, taps = band.shape[0], kernel.shape[0]
    gains = kernel[...].astype(jnp.float32) * 0.125
    lane = lax.broadcasted_iota(jnp.int32, gains.shape, 1)
    rows = sum(count for _, count in sources)
    index = lax.broadcasted_iota(jnp.int32, (rows, CHUNK), 0)
    source = jnp.zeros((rows, CHUNK), jnp.int32)
    at = 0
    for begin, count in sources:
        source = jnp.where(index >= at, index + (begin - at), source)
        at += count
    target = first + lax.broadcasted_iota(jnp.int32, (rows, CHUNK), 1)
    base = source - target + (taps // 2 - 1)
    row = lax.broadcasted_iota(jnp.int32, (CHUNK, CHUNK), 0)
    col = lax.broadcasted_iota(jnp.int32, (CHUNK, CHUNK), 1)
    blocks = CHUNK // LOOK_R
    order = jnp.where(col == (row % blocks) * LOOK_R + row // blocks, 1.0, 0.0).astype(jnp.bfloat16)
    for a in range(acq):
        tap = base - shift(a)
        total = jnp.zeros((rows, CHUNK), jnp.float32)
        gain = jnp.sum(jnp.where(lane == group[0] * acq + a, gains, 0.0), axis=1, keepdims=True)
        for k in range(taps):
            total = jnp.where(tap == k, gain[k : k + 1, :], total)
        turned = lax.dot_general(
            order, total.astype(jnp.bfloat16), (((1,), (1,)), ((), ())),
            preferred_element_type=jnp.float32,
        )
        band[a] = turned.astype(jnp.bfloat16)


def first_kernel(first, groups, group, side, kernel, off, slc, *rest):
    outs, (inner, outer, slab, band, gains, shifts, sems) = rest[:groups], rest[groups:]
    acq, _, lines, cols = slc.shape
    width = cols // groups

    def columns(s):
        return pl.ds(pl.multiple_of((group[0] ^ s) * width, width), width)

    order = [*range(1, groups), 0]
    small = [
        pltpu.make_async_copy(kernel, gains, sems.at[groups]),
        pltpu.make_async_copy(off, shifts, sems.at[groups + 1]),
    ]
    for copy in small:
        copy.start()
    copies = {}
    for s in order:
        at = columns(s)
        copies[s] = pltpu.make_async_copy(slc.at[:, :, :, at], slab.at[:, :, :, at], sems.at[s])
        copies[s].start()
    for copy in small:
        copy.wait()
    build_bands(first, [(0, lines)], group, gains, lambda a: shifts[a : a + 1, first : first + CHUNK], band)
    for s in order:
        copies[s].wait()
        at = columns(s)
        for a in range(acq):
            for x in range(2):
                total = jnp.dot(band[a], slab[a, x, :, at], preferred_element_type=jnp.float32)
                outs[s][a, x] = total.astype(jnp.bfloat16)
    for even, head, tail in ((0, outer, inner), (1, inner, outer)):

        @pl.when(side[0] == even)
        def _(head=head, tail=tail):
            head[...] = slab[:, :, :HALO, :]
            tail[...] = slab[:, :, lines - HALO :, :]


def edge_kernel(groups, parity, count, group, side, kernel, off, slab, halo, *rest):
    outs, band = rest[:groups], rest[groups]
    acq, _, lines, cols = slab.shape
    width = cols // groups
    bottom = side[0] == parity
    first = jnp.where(bottom, lines - CHUNK, 0)
    begin = pl.multiple_of(jnp.where(bottom, lines - count, 0), TILE)
    outside = jnp.where(bottom, lines, -HALO)

    def shift(a):
        return jnp.where(bottom, off[a : a + 1, lines - CHUNK :], off[a : a + 1, :CHUNK])

    build_bands(first, [(begin, count), (outside, HALO)], group, kernel, shift, band)
    for s in [*range(1, groups), 0]:
        at = pl.ds(pl.multiple_of((group[0] ^ s) * width, width), width)
        for a in range(acq):
            for x in range(2):
                lines_in = jnp.concatenate(
                    [slab[a, x, pl.ds(begin, count), at], halo[a, x, :, at]], axis=0
                )
                total = jnp.dot(band[a], lines_in, preferred_element_type=jnp.float32)
                outs[s][a, x] = total.astype(jnp.bfloat16)


SMEM = pl.BlockSpec(memory_space=pltpu.SMEM)
VMEM = pl.BlockSpec(memory_space=pltpu.VMEM)
ANY = pl.BlockSpec(memory_space=pl.ANY)


def resample_cost(acq, cols, rows):
    return pl.CostEstimate(
        flops=2 * acq * 2 * CHUNK * rows * cols,
        bytes_accessed=acq * 2 * (rows + CHUNK) * cols * 2,
        transcendentals=0,
    )


def resample_first(first, group, side, kernel, offsets, slc, groups):
    acq, _, lines, cols = slc.shape
    piece = pltpu.VMEM((acq, 2, CHUNK, cols // groups), jnp.bfloat16)
    halo = pltpu.VMEM((acq, 2, HALO, cols), jnp.bfloat16)
    slab = pltpu.VMEM(slc.shape, jnp.bfloat16)
    return pl.pallas_call(
        functools.partial(first_kernel, first, groups),
        in_specs=[SMEM, SMEM, ANY, ANY, ANY],
        out_specs=[VMEM] * (groups + 3),
        out_shape=[piece] * groups + [halo, halo, slab],
        scratch_shapes=[
            pltpu.VMEM((acq, CHUNK, lines), jnp.bfloat16),
            pltpu.VMEM(kernel.shape, kernel.dtype),
            pltpu.VMEM(offsets.shape, offsets.dtype),
            pltpu.SemaphoreType.DMA((groups + 2,)),
        ],
        compiler_params=pltpu.CompilerParams(vmem_limit_bytes=16 * MIB),
        cost_estimate=resample_cost(acq, cols, lines),
        name="resample_first",
    )(group, side, kernel, offsets, slc)


def resample_edge(parity, count, group, side, kernel, offsets, slab, halo, groups):
    acq, _, lines, cols = slab.shape
    piece = pltpu.VMEM((acq, 2, CHUNK, cols // groups), jnp.bfloat16)
    return pl.pallas_call(
        functools.partial(edge_kernel, groups, parity, count),
        in_specs=[SMEM, SMEM, VMEM, VMEM, VMEM, VMEM],
        out_specs=[VMEM] * groups,
        out_shape=[piece] * groups,
        scratch_shapes=[pltpu.VMEM((acq, CHUNK, count + HALO), jnp.bfloat16)],
        compiler_params=pltpu.CompilerParams(vmem_limit_bytes=16 * MIB),
        cost_estimate=resample_cost(acq, cols, count + HALO),
        name="resample_edge",
    )(group, side, kernel, offsets, slab, halo)


def slot_of(low, high):
    return high * (high - 1) // 2 + low


def look_sums(blocks, begin, parts, terms, sums, slot_rows, power_rows):
    acq, _, lines, width = blocks[0].shape
    looks = lines // LOOK_R
    windows = width // LOOK_C
    both = 2 * looks
    tiles = width // LANES
    total, fresh = len(blocks) * acq, begin * acq
    base = slot_of(0, fresh)
    split = (slot_of(0, total) - base) * both
    used = split + (total - fresh) * looks

    def pool(tile):
        row = lax.broadcasted_iota(jnp.int32, (2 * LANES, windows), 0)
        window = lax.broadcasted_iota(jnp.int32, (2 * LANES, windows), 1)
        wanted = tile * (LANES // LOOK_C) + (row % LANES) // LOOK_C
        return jnp.where(wanted == window, 1.0, 0.0).astype(jnp.bfloat16)

    def put(row, field):
        first = field.astype(jnp.bfloat16)
        terms[row : row + both, :LANES] = first
        terms[row : row + both, LANES:] = (field - first.astype(jnp.float32)).astype(jnp.bfloat16)

    def settle(tile):
        result = jnp.dot(terms[...], pool(tile), preferred_element_type=jnp.float32)
        sums[slot_rows : slot_rows + split, :] += result[:split]
        sums[power_rows : power_rows + used - split, :] += result[split:used]

    def unpack(tile):
        at = pl.ds(pl.multiple_of(tile * LANES, LANES), LANES)
        for r, block in enumerate(blocks):
            for a in range(acq):
                real = block[a, 0, :, at].astype(jnp.float32)
                imag = block[a, 1, :, at].astype(jnp.float32)
                parts[r * acq + a, 0] = real
                parts[r * acq + a, 1] = imag
                parts[r * acq + a, 2] = real + imag
                parts[r * acq + a, 3] = real - imag

    def cross(pairs):
        totals = {pair: [0.0, 0.0, 0.0] for pair in pairs}
        for j in range(LOOK_R):
            at = slice(j * looks, (j + 1) * looks)
            left = {i: [parts[i, c, at, :] for c in (2, 0, 1)] for i in sorted({i for i, _ in pairs})}
            right = {i: [parts[i, c, at, :] for c in (0, 2, 3)] for i in sorted({i for _, i in pairs})}
            for pair in pairs:
                for t in range(3):
                    totals[pair][t] = totals[pair][t] + left[pair[0]][t] * right[pair[1]][t]
        for i, k in pairs:
            one, two, three = totals[i, k]
            put((slot_of(i, k) - base) * both, jnp.concatenate([one - three, one - two], axis=0))

    def powers(members):
        fields = []
        for i in members:
            field = 0.0
            for j in range(LOOK_R):
                for c in range(2):
                    value = parts[i, c, j * looks : (j + 1) * looks, :]
                    field = field + value * value
            fields.append(field)
        put(split + (members[0] - fresh) * looks, jnp.concatenate(fields, axis=0))

    def work(tile):
        unpack(tile)
        for q in range(begin, len(blocks)):
            for r in range(q + 1):
                first = range(r * acq, (r + 1) * acq)
                second = range(q * acq, (q + 1) * acq)
                cross([(i, k) for i in first for k in second if i < k])
        for i in range(fresh, total, 2):
            powers((i, min(i + 1, total - 1)))

    def turn(tile, carry):
        settle(tile - 1)
        work(tile)
        return carry

    work(0)
    lax.fori_loop(1, tiles, turn, 0)
    settle(tiles - 1)


def near_kernel(groups, *rest):
    blocks, (sums, parts, terms) = rest[:groups], rest[groups:]
    acq, _, lines, _ = blocks[0].shape
    looks = lines // LOOK_R
    sums[...] = jnp.zeros(sums.shape, jnp.float32)
    look_sums(blocks, 0, parts, terms, sums, 0, slot_of(0, groups * acq) * 2 * looks)


def interfere_kernel(groups, known, spot, table, *rest):
    blocks, rest = rest[:groups], rest[groups:]
    out, parts, terms, sums, flat, inverse, slab, sem = rest[-8:]
    acq, _, lines, width = blocks[0].shape
    looks = lines // LOOK_R
    count = table.shape[1]
    both = 2 * looks
    total, fresh = groups * acq, known * acq
    start, split = slot_of(0, fresh) * both, slot_of(0, total) * both
    sums[...] = jnp.zeros(sums.shape, jnp.float32)
    if known:
        near = rest[0]
        sums[:start, :] = near[:start, :]
        sums[split : split + fresh * looks, :] = near[start : start + fresh * looks, :]
    look_sums(blocks, known, parts, terms, sums, start, split + fresh * looks)
    inverse[...] = lax.rsqrt(sums[split : split + total * looks, :] + 1e-6)

    def select(p, carry):
        at = pl.multiple_of(table[0, p] * both, both)
        m = pl.multiple_of(table[1, p] * looks, looks)
        s = pl.multiple_of(table[2, p] * looks, looks)
        scale = inverse[pl.ds(m, looks), :] * inverse[pl.ds(s, looks), :]
        turned = scale * table[3, p].astype(jnp.float32)
        value = sums[pl.ds(at, both), :] * jnp.concatenate([scale, turned], axis=0)
        flat[pl.ds(pl.multiple_of(p * both, both), both), :] = value
        return carry

    lax.fori_loop(0, count, select, 0, unroll=max(b for b in range(1, 7) if count % b == 0))
    copies = []
    for g in range(looks):
        for x in range(2):
            slab[x, g] = flat[pl.ds(x * looks + g, count, stride=both), :].T
        copies.append(pltpu.make_async_copy(slab.at[:, g], out.at[:, spot[0] * looks + g], sem.at[g]))
        copies[-1].start()
    for copy in copies:
        copy.wait()


def work_space(groups, known, acq, lines, looks):
    total, fresh = groups * acq, known * acq
    count = total - fresh
    rows = (slot_of(0, total) - slot_of(0, fresh)) * 2 * looks + (count + count % 2) * looks
    return [
        pltpu.VMEM((total, 4, lines, LANES), jnp.float32),
        pltpu.VMEM((rows, 2 * LANES), jnp.bfloat16),
    ]


def interfere_cost(pairs, acq, lines, width):
    return pl.CostEstimate(
        flops=pairs * 8 * lines * width,
        bytes_accessed=acq * 2 * lines * width * 2 * 12,
        transcendentals=0,
    )


def interfere_near(blocks):
    groups = len(blocks)
    acq, _, lines, width = blocks[0].shape
    looks, windows, total = lines // LOOK_R, width // LOOK_C, groups * acq
    return pl.pallas_call(
        functools.partial(near_kernel, groups),
        in_specs=[VMEM] * groups,
        out_specs=VMEM,
        out_shape=pltpu.VMEM(((slot_of(0, total) * 2 + total) * looks, windows), jnp.float32),
        scratch_shapes=work_space(groups, 0, acq, lines, looks),
        compiler_params=pltpu.CompilerParams(vmem_limit_bytes=16 * MIB),
        cost_estimate=interfere_cost(slot_of(0, total), total, lines, width),
        name="interfere_near",
    )(*blocks)


def interfere(place, chunks, table, blocks, near, known, before):
    groups = len(blocks)
    acq, _, lines, width = blocks[0].shape
    looks, windows, count = lines // LOOK_R, width // LOOK_C, table.shape[1]
    total = groups * acq
    near = [] if near is None else [near]
    extra = [] if before is None else [before]
    return pl.pallas_call(
        functools.partial(interfere_kernel, groups, known),
        in_specs=[SMEM, SMEM] + [VMEM] * (groups + len(near)) + [ANY] * len(extra),
        out_specs=ANY,
        out_shape=pltpu.HBM((2, chunks * looks, windows, count), jnp.float32),
        scratch_shapes=work_space(groups, known, acq, lines, looks)
        + [
            pltpu.VMEM(((slot_of(0, total) * 2 + total) * looks, windows), jnp.float32),
            pltpu.VMEM((count * 2 * looks, windows), jnp.float32),
            pltpu.VMEM((total * looks, windows), jnp.float32),
            pltpu.VMEM((2, looks, windows, count), jnp.float32),
            pltpu.SemaphoreType.DMA((looks,)),
        ],
        input_output_aliases={} if before is None else {2 + groups + len(near): 0},
        compiler_params=pltpu.CompilerParams(vmem_limit_bytes=16 * MIB),
        cost_estimate=interfere_cost(count, total, lines, width),
        name="interfere",
    )(place, table, *blocks, *near, *extra)


def pair_table(pairs, groups, acq, mine):
    close = ((pairs // acq) ^ mine) * acq + pairs % acq
    m, s = close[:, 0], close[:, 1]
    slot = slot_of(jnp.minimum(m, s), jnp.maximum(m, s))
    return jnp.stack([slot, m, s, jnp.where(m < s, 1, -1)]).astype(jnp.int32)


def local(slc, offsets, weights, pairs):
    acq, _, lines, cols = slc.shape
    groups = lax.axis_size("acq")
    size = lax.axis_size("pix")
    row = lax.axis_index("pix")
    odd = row % 2
    group = jnp.reshape(lax.axis_index("acq"), (1,)).astype(jnp.int32)
    side = jnp.reshape(odd, (1,)).astype(jnp.int32)
    kernel = weights.T
    table = pair_table(pairs, groups, acq, group[0])
    chunks = lines // CHUNK
    reach = CHUNK + TILE * 2

    def send(blocks):
        moved = [blocks[0]]
        for s in range(1, groups):
            moved.append(lax.ppermute(blocks[s], "acq", [(i, i ^ s) for i in range(groups)]))
        return moved

    def swap(halo, begin):
        pairs_up = [(i, i + 1) for i in range(begin, size - 1, 2)]
        return lax.ppermute(halo, "pix", pairs_up + [(j, i) for i, j in pairs_up])

    *blocks, inner, outer, slab = resample_first(
        CHUNK, group, side, *[pltpu.with_memory_space_constraint(t, pltpu.HBM) for t in (kernel, offsets, slc)], groups
    )
    inside = swap(inner, 0)
    across = swap(outer, 1)
    middle = send(blocks)
    pieces = resample_edge(0, reach, group, side, kernel, offsets, slab, inside, groups)
    *pieces, slab = lax.optimization_barrier((*pieces, slab))
    second = send(pieces)
    third = send(resample_edge(1, reach, group, side, kernel, offsets, slab, across, groups))
    low, high = jnp.zeros_like(odd), jnp.full_like(odd, chunks - 1)
    spots = (
        jnp.full_like(odd, 1),
        jnp.where(odd == 0, high, low),
        jnp.where(odd == 0, low, high),
    )
    result = None
    for spot, moved, known in zip(spots, (middle, second, third), (0, 0, groups - 1)):
        place = jnp.reshape(spot, (1,)).astype(jnp.int32)
        near = None
        if known:
            mine, result = lax.optimization_barrier((moved[0], result))
            near = interfere_near([mine, *moved[1:known]])
        result = interfere(place, chunks, table, moved, near, known, result)
    return jnp.transpose(result, (0, 3, 1, 2))


def solution(mesh):
    placed = (P("acq", None, "pix", None), P("acq", "pix"), P(), P())
    return jax.shard_map(
        local, mesh=mesh, in_specs=placed, out_specs=P(None, None, "pix", "acq"), check_vma=False
    )
```

```python
import functools

import jax
import jax.numpy as jnp
from jax import lax
from jax.experimental import pallas as pl
from jax.experimental.pallas import tpu as pltpu
from jax.sharding import PartitionSpec as P

LOOK_R = 4
LOOK_C = 16
CHUNK = 32
HALO = 24
TILE = 16
LANES = 128
MIB = 1024 * 1024


def build_bands(first, sources, group, kernel, shift, band):
    acq, taps = band.shape[0], kernel.shape[0]
    gains = kernel[...].astype(jnp.float32) * 0.125
    lane = lax.broadcasted_iota(jnp.int32, gains.shape, 1)
    rows = sum(count for _, count in sources)
    index = lax.broadcasted_iota(jnp.int32, (rows, CHUNK), 0)
    source = jnp.zeros((rows, CHUNK), jnp.int32)
    at = 0
    for begin, count in sources:
        source = jnp.where(index >= at, index + (begin - at), source)
        at += count
    target = first + lax.broadcasted_iota(jnp.int32, (rows, CHUNK), 1)
    base = source - target + (taps // 2 - 1)
    row = lax.broadcasted_iota(jnp.int32, (CHUNK, CHUNK), 0)
    col = lax.broadcasted_iota(jnp.int32, (CHUNK, CHUNK), 1)
    blocks = CHUNK // LOOK_R
    order = jnp.where(col == (row % blocks) * LOOK_R + row // blocks, 1.0, 0.0).astype(jnp.bfloat16)
    for a in range(acq):
        tap = base - shift(a)
        total = jnp.zeros((rows, CHUNK), jnp.float32)
        gain = jnp.sum(jnp.where(lane == group[0] * acq + a, gains, 0.0), axis=1, keepdims=True)
        for k in range(taps):
            total = jnp.where(tap == k, gain[k : k + 1, :], total)
        turned = lax.dot_general(
            order, total.astype(jnp.bfloat16), (((1,), (1,)), ((), ())),
            preferred_element_type=jnp.float32,
        )
        band[a] = turned.astype(jnp.bfloat16)


def copy_edge(bottom, slab, halo):
    lines = slab.shape[2]

    @pl.when(bottom)
    def _():
        halo[...] = slab[:, :, lines - HALO :, :]

    @pl.when(jnp.logical_not(bottom))
    def _():
        halo[...] = slab[:, :, :HALO, :]


def first_kernel(first, groups, group, side, kernel, off, slc, *rest):
    outs, (inner, outer, slab, band, gains, shifts, sems) = rest[:groups], rest[groups:]
    acq, _, lines, cols = slc.shape
    width = cols // groups

    def columns(s):
        return pl.ds(pl.multiple_of((group[0] ^ s) * width, width), width)

    order = [*range(1, groups), 0]
    small = [
        pltpu.make_async_copy(kernel, gains, sems.at[groups]),
        pltpu.make_async_copy(off, shifts, sems.at[groups + 1]),
    ]
    for copy in small:
        copy.start()
    copies = {}
    for s in order:
        at = columns(s)
        copies[s] = pltpu.make_async_copy(slc.at[:, :, :, at], slab.at[:, :, :, at], sems.at[s])
        copies[s].start()
    for copy in small:
        copy.wait()
    build_bands(first, [(0, lines)], group, gains, lambda a: shifts[a : a + 1, first : first + CHUNK], band)
    for s in order:
        copies[s].wait()
        at = columns(s)
        for a in range(acq):
            for x in range(2):
                total = jnp.dot(band[a], slab[a, x, :, at], preferred_element_type=jnp.float32)
                outs[s][a, x] = total.astype(jnp.bfloat16)
    copy_edge(side[0] == 0, slab, inner)
    copy_edge(side[0] == 1, slab, outer)


def edge_kernel(groups, parity, count, group, side, kernel, off, slab, halo, _, *rest):
    outs, band = rest[:groups], rest[-1]
    acq, _, lines, cols = slab.shape
    width = cols // groups
    bottom = side[0] == parity
    first = jnp.where(bottom, lines - CHUNK, 0)
    begin = pl.multiple_of(jnp.where(bottom, lines - count, 0), TILE)
    outside = jnp.where(bottom, lines, -HALO)

    def shift(a):
        return jnp.where(bottom, off[a : a + 1, lines - CHUNK :], off[a : a + 1, :CHUNK])

    build_bands(first, [(begin, count), (outside, HALO)], group, kernel, shift, band)
    for s in [*range(1, groups), 0]:
        at = pl.ds(pl.multiple_of((group[0] ^ s) * width, width), width)
        for a in range(acq):
            for x in range(2):
                lines_in = jnp.concatenate(
                    [slab[a, x, pl.ds(begin, count), at], halo[a, x, :, at]], axis=0
                )
                total = jnp.dot(band[a], lines_in, preferred_element_type=jnp.float32)
                outs[s][a, x] = total.astype(jnp.bfloat16)


SMEM = pl.BlockSpec(memory_space=pltpu.SMEM)
VMEM = pl.BlockSpec(memory_space=pltpu.VMEM)
ANY = pl.BlockSpec(memory_space=pl.ANY)


def resample_cost(acq, cols, rows):
    return pl.CostEstimate(
        flops=2 * acq * 2 * CHUNK * rows * cols,
        bytes_accessed=acq * 2 * (rows + CHUNK) * cols * 2,
        transcendentals=0,
    )


def resample_first(first, group, side, kernel, offsets, slc, groups):
    acq, _, lines, cols = slc.shape
    piece = pltpu.VMEM((acq, 2, CHUNK, cols // groups), jnp.bfloat16)
    halo = pltpu.VMEM((acq, 2, HALO, cols), jnp.bfloat16)
    slab = pltpu.VMEM(slc.shape, jnp.bfloat16)
    return pl.pallas_call(
        functools.partial(first_kernel, first, groups),
        in_specs=[SMEM, SMEM, ANY, ANY, ANY],
        out_specs=[VMEM] * (groups + 3),
        out_shape=[piece] * groups + [halo, halo, slab],
        scratch_shapes=[
            pltpu.VMEM((acq, CHUNK, lines), jnp.bfloat16),
            pltpu.VMEM(kernel.shape, kernel.dtype),
            pltpu.VMEM(offsets.shape, offsets.dtype),
            pltpu.SemaphoreType.DMA((groups + 2,)),
        ],
        compiler_params=pltpu.CompilerParams(vmem_limit_bytes=10 * MIB),
        cost_estimate=resample_cost(acq, cols, lines),
        name="resample_first",
    )(group, side, kernel, offsets, slc)


def resample_edge(parity, count, group, side, kernel, offsets, slab, halo, after, groups):
    acq, _, lines, cols = slab.shape
    piece = pltpu.VMEM((acq, 2, CHUNK, cols // groups), jnp.bfloat16)
    return pl.pallas_call(
        functools.partial(edge_kernel, groups, parity, count),
        in_specs=[SMEM, SMEM, VMEM, VMEM, VMEM, VMEM, ANY],
        out_specs=[VMEM] * groups,
        out_shape=[piece] * groups,
        scratch_shapes=[pltpu.VMEM((acq, CHUNK, count + HALO), jnp.bfloat16)],
        compiler_params=pltpu.CompilerParams(vmem_limit_bytes=10 * MIB),
        cost_estimate=resample_cost(acq, cols, count + HALO),
        name="resample_edge",
    )(group, side, kernel, offsets, slab, halo, after)


def slot_of(low, high):
    return high * (high - 1) // 2 + low


def look_sums(blocks, begin, parts, terms, sums, slot_rows, power_rows):
    acq, _, lines, width = blocks[0].shape
    looks = lines // LOOK_R
    windows = width // LOOK_C
    both = 2 * looks
    tiles = width // LANES
    total, fresh = len(blocks) * acq, begin * acq
    base = slot_of(0, fresh)
    split = (slot_of(0, total) - base) * both
    used = split + (total - fresh) * looks

    def pool(tile):
        row = lax.broadcasted_iota(jnp.int32, (2 * LANES, windows), 0)
        window = lax.broadcasted_iota(jnp.int32, (2 * LANES, windows), 1)
        wanted = tile * (LANES // LOOK_C) + (row % LANES) // LOOK_C
        return jnp.where(wanted == window, 1.0, 0.0).astype(jnp.bfloat16)

    def put(row, field):
        first = field.astype(jnp.bfloat16)
        terms[row : row + both, :LANES] = first
        terms[row : row + both, LANES:] = (field - first.astype(jnp.float32)).astype(jnp.bfloat16)

    def settle(tile):
        result = jnp.dot(terms[...], pool(tile), preferred_element_type=jnp.float32)
        sums[slot_rows : slot_rows + split, :] += result[:split]
        sums[power_rows : power_rows + used - split, :] += result[split:used]

    def unpack(tile):
        at = pl.ds(pl.multiple_of(tile * LANES, LANES), LANES)
        for r, block in enumerate(blocks):
            for a in range(acq):
                real = block[a, 0, :, at].astype(jnp.float32)
                imag = block[a, 1, :, at].astype(jnp.float32)
                parts[r * acq + a, 0] = real
                parts[r * acq + a, 1] = imag
                parts[r * acq + a, 2] = real + imag
                parts[r * acq + a, 3] = real - imag

    def cross(pairs):
        totals = {pair: [0.0, 0.0, 0.0] for pair in pairs}
        for j in range(LOOK_R):
            at = slice(j * looks, (j + 1) * looks)
            left = {i: [parts[i, c, at, :] for c in (2, 0, 1)] for i in sorted({i for i, _ in pairs})}
            right = {i: [parts[i, c, at, :] for c in (0, 2, 3)] for i in sorted({i for _, i in pairs})}
            for pair in pairs:
                for t in range(3):
                    totals[pair][t] = totals[pair][t] + left[pair[0]][t] * right[pair[1]][t]
        for i, k in pairs:
            one, two, three = totals[i, k]
            put((slot_of(i, k) - base) * both, jnp.concatenate([one - three, one - two], axis=0))

    def powers(members):
        fields = []
        for i in members:
            field = 0.0
            for j in range(LOOK_R):
                for c in range(2):
                    value = parts[i, c, j * looks : (j + 1) * looks, :]
                    field = field + value * value
            fields.append(field)
        put(split + (members[0] - fresh) * looks, jnp.concatenate(fields, axis=0))

    def work(tile):
        unpack(tile)
        for q in range(begin, len(blocks)):
            for r in range(q + 1):
                first = range(r * acq, (r + 1) * acq)
                second = range(q * acq, (q + 1) * acq)
                cross([(i, k) for i in first for k in second if i < k])
        for i in range(fresh, total, 2):
            powers((i, min(i + 1, total - 1)))

    def turn(tile, carry):
        settle(tile - 1)
        work(tile)
        return carry

    work(0)
    lax.fori_loop(1, tiles, turn, 0)
    settle(tiles - 1)


def near_kernel(groups, *rest):
    blocks, (sums, parts, terms) = rest[:groups], rest[groups:]
    acq, _, lines, _ = blocks[0].shape
    looks = lines // LOOK_R
    sums[...] = jnp.zeros(sums.shape, jnp.float32)
    look_sums(blocks, 0, parts, terms, sums, 0, slot_of(0, groups * acq) * 2 * looks)


def interfere_kernel(groups, known, spot, table, *rest):
    blocks, rest = rest[:groups], rest[groups:]
    out, parts, terms, sums, flat, inverse, slab, sem = rest[-8:]
    acq, _, lines, width = blocks[0].shape
    looks = lines // LOOK_R
    count = table.shape[1]
    both = 2 * looks
    total, fresh = groups * acq, known * acq
    start, split = slot_of(0, fresh) * both, slot_of(0, total) * both
    sums[...] = jnp.zeros(sums.shape, jnp.float32)
    if known:
        near = rest[0]
        sums[:start, :] = near[:start, :]
        sums[split : split + fresh * looks, :] = near[start : start + fresh * looks, :]
    look_sums(blocks, known, parts, terms, sums, start, split + fresh * looks)
    inverse[...] = lax.rsqrt(sums[split : split + total * looks, :] + 1e-6)

    def select(p, carry):
        at = pl.multiple_of(table[0, p] * both, both)
        m = pl.multiple_of(table[1, p] * looks, looks)
        s = pl.multiple_of(table[2, p] * looks, looks)
        scale = inverse[pl.ds(m, looks), :] * inverse[pl.ds(s, looks), :]
        turned = scale * table[3, p].astype(jnp.float32)
        value = sums[pl.ds(at, both), :] * jnp.concatenate([scale, turned], axis=0)
        flat[pl.ds(pl.multiple_of(p * both, both), both), :] = value
        return carry

    lax.fori_loop(0, count, select, 0, unroll=max(b for b in range(1, 7) if count % b == 0))
    copies = []
    for g in range(looks):
        for x in range(2):
            slab[x, g] = flat[pl.ds(x * looks + g, count, stride=both), :].T
        copies.append(pltpu.make_async_copy(slab.at[:, g], out.at[:, spot[0] * looks + g], sem.at[g]))
        copies[-1].start()
    for copy in copies:
        copy.wait()


def work_space(groups, known, acq, lines, looks):
    total, fresh = groups * acq, known * acq
    count = total - fresh
    rows = (slot_of(0, total) - slot_of(0, fresh)) * 2 * looks + (count + count % 2) * looks
    return [
        pltpu.VMEM((total, 4, lines, LANES), jnp.float32),
        pltpu.VMEM((rows, 2 * LANES), jnp.bfloat16),
    ]


def interfere_cost(pairs, acq, lines, width):
    return pl.CostEstimate(
        flops=pairs * 8 * lines * width,
        bytes_accessed=acq * 2 * lines * width * 2 * 12,
        transcendentals=0,
    )


def interfere_near(blocks):
    groups = len(blocks)
    acq, _, lines, width = blocks[0].shape
    looks, windows, total = lines // LOOK_R, width // LOOK_C, groups * acq
    return pl.pallas_call(
        functools.partial(near_kernel, groups),
        in_specs=[VMEM] * groups,
        out_specs=VMEM,
        out_shape=pltpu.VMEM(((slot_of(0, total) * 2 + total) * looks, windows), jnp.float32),
        scratch_shapes=work_space(groups, 0, acq, lines, looks),
        compiler_params=pltpu.CompilerParams(vmem_limit_bytes=8 * MIB),
        cost_estimate=interfere_cost(slot_of(0, total), total, lines, width),
        name="interfere_near",
    )(*blocks)


def interfere(place, chunks, table, blocks, near, known, before):
    groups = len(blocks)
    acq, _, lines, width = blocks[0].shape
    looks, windows, count = lines // LOOK_R, width // LOOK_C, table.shape[1]
    total = groups * acq
    near = [] if near is None else [near]
    extra = [] if before is None else [before]
    return pl.pallas_call(
        functools.partial(interfere_kernel, groups, known),
        in_specs=[SMEM, SMEM] + [VMEM] * (groups + len(near)) + [ANY] * len(extra),
        out_specs=ANY,
        out_shape=pltpu.HBM((2, chunks * looks, windows, count), jnp.float32),
        scratch_shapes=work_space(groups, known, acq, lines, looks)
        + [
            pltpu.VMEM(((slot_of(0, total) * 2 + total) * looks, windows), jnp.float32),
            pltpu.VMEM((count * 2 * looks, windows), jnp.float32),
            pltpu.VMEM((total * looks, windows), jnp.float32),
            pltpu.VMEM((2, looks, windows, count), jnp.float32),
            pltpu.SemaphoreType.DMA((looks,)),
        ],
        input_output_aliases={} if before is None else {2 + groups + len(near): 0},
        compiler_params=pltpu.CompilerParams(vmem_limit_bytes=8 * MIB),
        cost_estimate=interfere_cost(count, total, lines, width),
        name="interfere",
    )(place, table, *blocks, *near, *extra)


def pair_table(pairs, groups, acq, mine):
    close = ((pairs // acq) ^ mine) * acq + pairs % acq
    m, s = close[:, 0], close[:, 1]
    slot = slot_of(jnp.minimum(m, s), jnp.maximum(m, s))
    return jnp.stack([slot, m, s, jnp.where(m < s, 1, -1)]).astype(jnp.int32)


def local(slc, offsets, weights, pairs):
    acq, _, lines, cols = slc.shape
    groups = lax.axis_size("acq")
    size = lax.axis_size("pix")
    row = lax.axis_index("pix")
    odd = row % 2
    group = jnp.reshape(lax.axis_index("acq"), (1,)).astype(jnp.int32)
    side = jnp.reshape(odd, (1,)).astype(jnp.int32)
    kernel = weights.T
    table = pair_table(pairs, groups, acq, group[0])
    chunks = lines // CHUNK
    reach = CHUNK + TILE * 2

    def send(blocks):
        moved = [blocks[0]]
        for s in range(1, groups):
            moved.append(lax.ppermute(blocks[s], "acq", [(i, i ^ s) for i in range(groups)]))
        return moved

    def swap(halo, begin):
        pairs_up = [(i, i + 1) for i in range(begin, size - 1, 2)]
        return lax.ppermute(halo, "pix", pairs_up + [(j, i) for i, j in pairs_up])

    *blocks, inner, outer, slab = resample_first(
        CHUNK, group, side, *[pltpu.with_memory_space_constraint(t, pltpu.HBM) for t in (kernel, offsets, slc)], groups
    )
    inside = swap(inner, 0)
    middle = send(blocks)
    pieces = resample_edge(0, reach, group, side, kernel, offsets, slab, inside, inner, groups)
    across = swap(outer, 1)
    second = send(pieces)
    third = send(
        resample_edge(1, reach, group, side, kernel, offsets, slab, across, middle[3], groups)
    )
    low, high = jnp.zeros_like(odd), jnp.full_like(odd, chunks - 1)
    spots = (
        jnp.full_like(odd, 1),
        jnp.where(odd == 0, high, low),
        jnp.where(odd == 0, low, high),
    )
    result = None
    for spot, moved, known in zip(spots, (middle, second, third), (0, 0, groups - 1)):
        place = jnp.reshape(spot, (1,)).astype(jnp.int32)
        near = None
        if known:
            mine, result = lax.optimization_barrier((moved[0], result))
            near = interfere_near([mine, *moved[1:known]])
        result = interfere(place, chunks, table, moved, near, known, result)
    return jnp.transpose(result, (0, 3, 1, 2))


def solution(mesh):
    placed = (P("acq", None, "pix", None), P("acq", "pix"), P(), P())
    return jax.shard_map(
        local, mesh=mesh, in_specs=placed, out_specs=P(None, None, "pix", "acq"), check_vma=False
    )
```

```python
import functools

import jax
import jax.numpy as jnp
from jax import lax
from jax.experimental import pallas as pl
from jax.experimental.pallas import tpu as pltpu
from jax.sharding import PartitionSpec as P

LOOK_R = 4
LOOK_C = 16
CHUNK = 32
HALO = 24
TILE = 16
LANES = 128
MIB = 1024 * 1024


def build_bands(first, sources, group, kernel, shift, band):
    acq, taps = band.shape[0], kernel.shape[0]
    gains = kernel[...].astype(jnp.float32) * 0.125
    lane = lax.broadcasted_iota(jnp.int32, gains.shape, 1)
    rows = sum(count for _, count in sources)
    index = lax.broadcasted_iota(jnp.int32, (rows, CHUNK), 0)
    source = jnp.zeros((rows, CHUNK), jnp.int32)
    at = 0
    for begin, count in sources:
        source = jnp.where(index >= at, index + (begin - at), source)
        at += count
    target = first + lax.broadcasted_iota(jnp.int32, (rows, CHUNK), 1)
    base = source - target + (taps // 2 - 1)
    row = lax.broadcasted_iota(jnp.int32, (CHUNK, CHUNK), 0)
    col = lax.broadcasted_iota(jnp.int32, (CHUNK, CHUNK), 1)
    blocks = CHUNK // LOOK_R
    order = jnp.where(col == (row % blocks) * LOOK_R + row // blocks, 1.0, 0.0).astype(jnp.bfloat16)
    for a in range(acq):
        tap = base - shift(a)
        total = jnp.zeros((rows, CHUNK), jnp.float32)
        gain = jnp.sum(jnp.where(lane == group[0] * acq + a, gains, 0.0), axis=1, keepdims=True)
        for k in range(taps):
            total = jnp.where(tap == k, gain[k : k + 1, :], total)
        turned = lax.dot_general(
            order, total.astype(jnp.bfloat16), (((1,), (1,)), ((), ())),
            preferred_element_type=jnp.float32,
        )
        band[a] = turned.astype(jnp.bfloat16)


def copy_edge(bottom, slab, halo):
    lines = slab.shape[2]

    @pl.when(bottom)
    def _():
        halo[...] = slab[:, :, lines - HALO :, :]

    @pl.when(jnp.logical_not(bottom))
    def _():
        halo[...] = slab[:, :, :HALO, :]


def first_kernel(first, groups, group, side, kernel, off, slc, *rest):
    outs, (inner, outer, slab, band, gains, shifts, sems) = rest[:groups], rest[groups:]
    acq, _, lines, cols = slc.shape
    width = cols // groups

    def columns(s):
        return pl.ds(pl.multiple_of((group[0] ^ s) * width, width), width)

    order = [*range(1, groups), 0]
    small = [
        pltpu.make_async_copy(kernel, gains, sems.at[groups]),
        pltpu.make_async_copy(off, shifts, sems.at[groups + 1]),
    ]
    for copy in small:
        copy.start()
    copies = {}
    for s in order:
        at = columns(s)
        copies[s] = pltpu.make_async_copy(slc.at[:, :, :, at], slab.at[:, :, :, at], sems.at[s])
        copies[s].start()
    for copy in small:
        copy.wait()
    build_bands(first, [(0, lines)], group, gains, lambda a: shifts[a : a + 1, first : first + CHUNK], band)
    for s in order:
        copies[s].wait()
        at = columns(s)
        for a in range(acq):
            for x in range(2):
                total = jnp.dot(band[a], slab[a, x, :, at], preferred_element_type=jnp.float32)
                outs[s][a, x] = total.astype(jnp.bfloat16)
    copy_edge(side[0] == 0, slab, inner)
    copy_edge(side[0] == 1, slab, outer)


def edge_kernel(groups, parity, count, group, side, kernel, off, slab, halo, _, *rest):
    outs, band = rest[:groups], rest[-1]
    acq, _, lines, cols = slab.shape
    width = cols // groups
    bottom = side[0] == parity
    first = jnp.where(bottom, lines - CHUNK, 0)
    begin = pl.multiple_of(jnp.where(bottom, lines - count, 0), TILE)
    outside = jnp.where(bottom, lines, -HALO)

    def shift(a):
        return jnp.where(bottom, off[a : a + 1, lines - CHUNK :], off[a : a + 1, :CHUNK])

    build_bands(first, [(begin, count), (outside, HALO)], group, kernel, shift, band)
    for s in [*range(1, groups), 0]:
        at = pl.ds(pl.multiple_of((group[0] ^ s) * width, width), width)
        for a in range(acq):
            for x in range(2):
                lines_in = jnp.concatenate(
                    [slab[a, x, pl.ds(begin, count), at], halo[a, x, :, at]], axis=0
                )
                total = jnp.dot(band[a], lines_in, preferred_element_type=jnp.float32)
                outs[s][a, x] = total.astype(jnp.bfloat16)


SMEM = pl.BlockSpec(memory_space=pltpu.SMEM)
VMEM = pl.BlockSpec(memory_space=pltpu.VMEM)
ANY = pl.BlockSpec(memory_space=pl.ANY)


def resample_cost(acq, cols, rows):
    return pl.CostEstimate(
        flops=2 * acq * 2 * CHUNK * rows * cols,
        bytes_accessed=acq * 2 * (rows + CHUNK) * cols * 2,
        transcendentals=0,
    )


def resample_first(first, group, side, kernel, offsets, slc, groups):
    acq, _, lines, cols = slc.shape
    piece = pltpu.VMEM((acq, 2, CHUNK, cols // groups), jnp.bfloat16)
    halo = pltpu.VMEM((acq, 2, HALO, cols), jnp.bfloat16)
    slab = pltpu.VMEM(slc.shape, jnp.bfloat16)
    return pl.pallas_call(
        functools.partial(first_kernel, first, groups),
        in_specs=[SMEM, SMEM, ANY, ANY, ANY],
        out_specs=[VMEM] * (groups + 3),
        out_shape=[piece] * groups + [halo, halo, slab],
        scratch_shapes=[
            pltpu.VMEM((acq, CHUNK, lines), jnp.bfloat16),
            pltpu.VMEM(kernel.shape, kernel.dtype),
            pltpu.VMEM(offsets.shape, offsets.dtype),
            pltpu.SemaphoreType.DMA((groups + 2,)),
        ],
        compiler_params=pltpu.CompilerParams(vmem_limit_bytes=10 * MIB),
        cost_estimate=resample_cost(acq, cols, lines),
        name="resample_first",
    )(group, side, kernel, offsets, slc)


def resample_edge(parity, count, group, side, kernel, offsets, slab, halo, after, groups):
    acq, _, lines, cols = slab.shape
    piece = pltpu.VMEM((acq, 2, CHUNK, cols // groups), jnp.bfloat16)
    return pl.pallas_call(
        functools.partial(edge_kernel, groups, parity, count),
        in_specs=[SMEM, SMEM, VMEM, VMEM, VMEM, VMEM, ANY],
        out_specs=[VMEM] * groups,
        out_shape=[piece] * groups,
        scratch_shapes=[pltpu.VMEM((acq, CHUNK, count + HALO), jnp.bfloat16)],
        compiler_params=pltpu.CompilerParams(vmem_limit_bytes=10 * MIB),
        cost_estimate=resample_cost(acq, cols, count + HALO),
        name="resample_edge",
    )(group, side, kernel, offsets, slab, halo, after)


def slot_of(low, high):
    return high * (high - 1) // 2 + low


def look_sums(blocks, begin, parts, terms, sums, slot_rows, power_rows):
    acq, _, lines, width = blocks[0].shape
    looks = lines // LOOK_R
    windows = width // LOOK_C
    both = 2 * looks
    tiles = width // LANES
    total, fresh = len(blocks) * acq, begin * acq
    base = slot_of(0, fresh)
    split = (slot_of(0, total) - base) * both
    used = split + (total - fresh) * looks

    def pool(tile):
        row = lax.broadcasted_iota(jnp.int32, (2 * LANES, windows), 0)
        window = lax.broadcasted_iota(jnp.int32, (2 * LANES, windows), 1)
        wanted = tile * (LANES // LOOK_C) + (row % LANES) // LOOK_C
        return jnp.where(wanted == window, 1.0, 0.0).astype(jnp.bfloat16)

    def put(row, field):
        first = field.astype(jnp.bfloat16)
        terms[row : row + both, :LANES] = first
        terms[row : row + both, LANES:] = (field - first.astype(jnp.float32)).astype(jnp.bfloat16)

    def settle(tile):
        result = jnp.dot(terms[...], pool(tile), preferred_element_type=jnp.float32)
        sums[slot_rows : slot_rows + split, :] += result[:split]
        sums[power_rows : power_rows + used - split, :] += result[split:used]

    def unpack(tile):
        at = pl.ds(pl.multiple_of(tile * LANES, LANES), LANES)
        for r, block in enumerate(blocks):
            for a in range(acq):
                real = block[a, 0, :, at].astype(jnp.float32)
                imag = block[a, 1, :, at].astype(jnp.float32)
                parts[r * acq + a, 0] = real
                parts[r * acq + a, 1] = imag
                parts[r * acq + a, 2] = real + imag
                parts[r * acq + a, 3] = real - imag

    def cross(pairs):
        totals = {pair: [0.0, 0.0, 0.0] for pair in pairs}
        for j in range(LOOK_R):
            at = slice(j * looks, (j + 1) * looks)
            left = {i: [parts[i, c, at, :] for c in (2, 0, 1)] for i in sorted({i for i, _ in pairs})}
            right = {i: [parts[i, c, at, :] for c in (0, 2, 3)] for i in sorted({i for _, i in pairs})}
            for pair in pairs:
                for t in range(3):
                    totals[pair][t] = totals[pair][t] + left[pair[0]][t] * right[pair[1]][t]
        for i, k in pairs:
            one, two, three = totals[i, k]
            put((slot_of(i, k) - base) * both, jnp.concatenate([one - three, one - two], axis=0))

    def powers(members):
        fields = []
        for i in members:
            field = 0.0
            for j in range(LOOK_R):
                for c in range(2):
                    value = parts[i, c, j * looks : (j + 1) * looks, :]
                    field = field + value * value
            fields.append(field)
        put(split + (members[0] - fresh) * looks, jnp.concatenate(fields, axis=0))

    def work(tile):
        unpack(tile)
        for q in range(begin, len(blocks)):
            for r in range(q + 1):
                first = range(r * acq, (r + 1) * acq)
                second = range(q * acq, (q + 1) * acq)
                cross([(i, k) for i in first for k in second if i < k])
        for i in range(fresh, total, 2):
            powers((i, min(i + 1, total - 1)))

    def turn(tile, carry):
        settle(tile - 1)
        work(tile)
        return carry

    work(0)
    lax.fori_loop(1, tiles, turn, 0)
    settle(tiles - 1)


def near_kernel(groups, *rest):
    blocks, (sums, parts, terms) = rest[:groups], rest[groups:]
    acq, _, lines, _ = blocks[0].shape
    looks = lines // LOOK_R
    sums[...] = jnp.zeros(sums.shape, jnp.float32)
    look_sums(blocks, 0, parts, terms, sums, 0, slot_of(0, groups * acq) * 2 * looks)


def interfere_kernel(groups, known, turn, table, *rest):
    blocks, rest = rest[:groups], rest[groups:]
    out, parts, terms, sums, flat, inverse, slab, sem = rest[-8:]
    acq, _, lines, width = blocks[0].shape
    looks = lines // LOOK_R
    count = table.shape[1]
    both = 2 * looks
    total, fresh = groups * acq, known * acq
    start, split = slot_of(0, fresh) * both, slot_of(0, total) * both
    sums[...] = jnp.zeros(sums.shape, jnp.float32)
    if known:
        near = rest[0]
        sums[:start, :] = near[:start, :]
        sums[split : split + fresh * looks, :] = near[start : start + fresh * looks, :]
    look_sums(blocks, known, parts, terms, sums, start, split + fresh * looks)
    inverse[...] = lax.rsqrt(sums[split : split + total * looks, :] + 1e-6)

    def select(p, carry):
        at = pl.multiple_of(table[0, p] * both, both)
        m = pl.multiple_of(table[1, p] * looks, looks)
        s = pl.multiple_of(table[2, p] * looks, looks)
        scale = inverse[pl.ds(m, looks), :] * inverse[pl.ds(s, looks), :]
        turned = scale * table[3, p].astype(jnp.float32)
        value = sums[pl.ds(at, both), :] * jnp.concatenate([scale, turned], axis=0)
        flat[pl.ds(pl.multiple_of(p * both, both), both), :] = value
        return carry

    lax.fori_loop(0, count, select, 0, unroll=max(b for b in range(1, 7) if count % b == 0))
    copies = []
    for g in range(looks):
        for x in range(2):
            slab[x, g] = flat[pl.ds(x * looks + g, count, stride=both), :].T
        copies.append(pltpu.make_async_copy(slab.at[:, g], out.at[:, table[4, turn] * looks + g], sem.at[g]))
        copies[-1].start()
    for copy in copies:
        copy.wait()


def work_space(groups, known, acq, lines, looks):
    total, fresh = groups * acq, known * acq
    count = total - fresh
    rows = (slot_of(0, total) - slot_of(0, fresh)) * 2 * looks + (count + count % 2) * looks
    return [
        pltpu.VMEM((total, 4, lines, LANES), jnp.float32),
        pltpu.VMEM((rows, 2 * LANES), jnp.bfloat16),
    ]


def interfere_cost(pairs, acq, lines, width):
    return pl.CostEstimate(
        flops=pairs * 8 * lines * width,
        bytes_accessed=acq * 2 * lines * width * 2 * 12,
        transcendentals=0,
    )


def interfere_near(blocks):
    groups = len(blocks)
    acq, _, lines, width = blocks[0].shape
    looks, windows, total = lines // LOOK_R, width // LOOK_C, groups * acq
    return pl.pallas_call(
        functools.partial(near_kernel, groups),
        in_specs=[VMEM] * groups,
        out_specs=VMEM,
        out_shape=pltpu.VMEM(((slot_of(0, total) * 2 + total) * looks, windows), jnp.float32),
        scratch_shapes=work_space(groups, 0, acq, lines, looks),
        compiler_params=pltpu.CompilerParams(vmem_limit_bytes=8 * MIB),
        cost_estimate=interfere_cost(slot_of(0, total), total, lines, width),
        name="interfere_near",
    )(*blocks)


def interfere(turn, chunks, table, blocks, near, known, before):
    groups = len(blocks)
    acq, _, lines, width = blocks[0].shape
    looks, windows, count = lines // LOOK_R, width // LOOK_C, table.shape[1]
    total = groups * acq
    near = [] if near is None else [near]
    extra = [] if before is None else [before]
    return pl.pallas_call(
        functools.partial(interfere_kernel, groups, known, turn),
        in_specs=[SMEM] + [VMEM] * (groups + len(near)) + [ANY] * len(extra),
        out_specs=ANY,
        out_shape=pltpu.HBM((2, chunks * looks, windows, count), jnp.float32),
        scratch_shapes=work_space(groups, known, acq, lines, looks)
        + [
            pltpu.VMEM(((slot_of(0, total) * 2 + total) * looks, windows), jnp.float32),
            pltpu.VMEM((count * 2 * looks, windows), jnp.float32),
            pltpu.VMEM((total * looks, windows), jnp.float32),
            pltpu.VMEM((2, looks, windows, count), jnp.float32),
            pltpu.SemaphoreType.DMA((looks,)),
        ],
        input_output_aliases={} if before is None else {1 + groups + len(near): 0},
        compiler_params=pltpu.CompilerParams(vmem_limit_bytes=8 * MIB),
        cost_estimate=interfere_cost(count, total, lines, width),
        name="interfere",
    )(table, *blocks, *near, *extra)


def pair_table(pairs, groups, acq, mine, odd, chunks):
    close = ((pairs // acq) ^ mine) * acq + pairs % acq
    m, s = close[:, 0], close[:, 1]
    slot = slot_of(jnp.minimum(m, s), jnp.maximum(m, s))
    turn = jnp.arange(pairs.shape[0])
    edge = jnp.where((turn == 1) == (odd == 0), chunks - 1, 0)
    place = jnp.where(turn == 0, 1, edge)
    return jnp.stack([slot, m, s, jnp.where(m < s, 1, -1), place]).astype(jnp.int32)


def local(slc, offsets, weights, pairs):
    acq, _, lines, cols = slc.shape
    groups = lax.axis_size("acq")
    size = lax.axis_size("pix")
    row = lax.axis_index("pix")
    odd = row % 2
    group = jnp.reshape(lax.axis_index("acq"), (1,)).astype(jnp.int32)
    side = jnp.reshape(odd, (1,)).astype(jnp.int32)
    kernel = weights.T
    chunks = lines // CHUNK
    table = pair_table(pairs, groups, acq, group[0], odd, chunks)
    reach = CHUNK + TILE * 2

    def send(blocks):
        moved = [blocks[0]]
        for s in range(1, groups):
            moved.append(lax.ppermute(blocks[s], "acq", [(i, i ^ s) for i in range(groups)]))
        return moved

    def swap(halo, begin):
        pairs_up = [(i, i + 1) for i in range(begin, size - 1, 2)]
        return lax.ppermute(halo, "pix", pairs_up + [(j, i) for i, j in pairs_up])

    *blocks, inner, outer, slab = resample_first(
        CHUNK, group, side, *[pltpu.with_memory_space_constraint(t, pltpu.HBM) for t in (kernel, offsets, slc)], groups
    )
    inside = swap(inner, 0)
    middle = send(blocks)
    pieces = resample_edge(0, reach, group, side, kernel, offsets, slab, inside, inner, groups)
    across = swap(outer, 1)
    second = send(pieces)
    third = send(
        resample_edge(1, reach, group, side, kernel, offsets, slab, across, pieces[0], groups)
    )
    result = None
    for turn, (moved, known) in enumerate(((middle, 0), (second, 0), (third, groups - 1))):
        near = None
        if known:
            mine, result = lax.optimization_barrier((moved[0], result))
            near = interfere_near([mine, *moved[1:known]])
        result = interfere(turn, chunks, table, moved, near, known, result)
    return jnp.transpose(result, (0, 3, 1, 2))


def solution(mesh):
    placed = (P("acq", None, "pix", None), P("acq", "pix"), P(), P())
    return jax.shard_map(
        local, mesh=mesh, in_specs=placed, out_specs=P(None, None, "pix", "acq"), check_vma=False
    )
```

```python
import functools

import jax
import jax.numpy as jnp
from jax import lax
from jax.experimental import pallas as pl
from jax.experimental.pallas import tpu as pltpu
from jax.sharding import PartitionSpec as P

LOOK_R = 4
LOOK_C = 16
CHUNK = 32
HALO = 24
ORDER = (0, 2, 3, 1)
TILE = 16
LANES = 128
MIB = 1024 * 1024


def build_bands(first, sources, group, kernel, shift, band):
    acq, taps = band.shape[0], kernel.shape[0]
    gains = kernel[...].astype(jnp.float32) * 0.125
    lane = lax.broadcasted_iota(jnp.int32, gains.shape, 1)
    rows = sum(count for _, count in sources)
    index = lax.broadcasted_iota(jnp.int32, (rows, CHUNK), 0)
    source = jnp.zeros((rows, CHUNK), jnp.int32)
    at = 0
    for begin, count in sources:
        source = jnp.where(index >= at, index + (begin - at), source)
        at += count
    target = first + lax.broadcasted_iota(jnp.int32, (rows, CHUNK), 1)
    base = source - target + (taps // 2 - 1)
    row = lax.broadcasted_iota(jnp.int32, (CHUNK, CHUNK), 0)
    col = lax.broadcasted_iota(jnp.int32, (CHUNK, CHUNK), 1)
    blocks = CHUNK // LOOK_R
    order = jnp.where(col == (row % blocks) * LOOK_R + row // blocks, 1.0, 0.0).astype(jnp.bfloat16)
    for a in range(acq):
        tap = base - shift(a)
        total = jnp.zeros((rows, CHUNK), jnp.float32)
        gain = jnp.sum(jnp.where(lane == group[0] * acq + a, gains, 0.0), axis=1, keepdims=True)
        for k in range(taps):
            total = jnp.where(tap == k, gain[k : k + 1, :], total)
        turned = lax.dot_general(
            order, total.astype(jnp.bfloat16), (((1,), (1,)), ((), ())),
            preferred_element_type=jnp.float32,
        )
        band[a] = turned.astype(jnp.bfloat16)


def copy_edge(bottom, slab, halo):
    lines = slab.shape[2]

    @pl.when(bottom)
    def _():
        halo[...] = slab[:, :, lines - HALO :, :]

    @pl.when(jnp.logical_not(bottom))
    def _():
        halo[...] = slab[:, :, :HALO, :]


def first_kernel(first, groups, group, side, kernel, off, slc, *rest):
    outs, (inner, outer, slab, band, gains, shifts, sems) = rest[:groups], rest[groups:]
    acq, _, lines, cols = slc.shape
    width = cols // groups

    def columns(s):
        return pl.ds(pl.multiple_of((group[0] ^ s) * width, width), width)

    order = [*range(1, groups), 0]
    small = [
        pltpu.make_async_copy(kernel, gains, sems.at[groups]),
        pltpu.make_async_copy(off, shifts, sems.at[groups + 1]),
    ]
    for copy in small:
        copy.start()
    copies = {}
    for s in order:
        at = columns(s)
        copies[s] = pltpu.make_async_copy(slc.at[:, :, :, at], slab.at[:, :, :, at], sems.at[s])
        copies[s].start()
    for copy in small:
        copy.wait()
    build_bands(first, [(0, lines)], group, gains, lambda a: shifts[a : a + 1, first : first + CHUNK], band)
    for s in order:
        copies[s].wait()
        at = columns(s)
        for a in range(acq):
            for x in range(2):
                total = jnp.dot(band[a], slab[a, x, :, at], preferred_element_type=jnp.float32)
                outs[s][a, x] = total.astype(jnp.bfloat16)
    copy_edge(side[0] == 0, slab, inner)
    copy_edge(side[0] == 1, slab, outer)


def edge_kernel(groups, parity, count, group, side, kernel, off, slab, halo, _, *rest):
    outs, band = rest[:groups], rest[-1]
    acq, _, lines, cols = slab.shape
    width = cols // groups
    bottom = side[0] == parity
    first = jnp.where(bottom, lines - CHUNK, 0)
    begin = pl.multiple_of(jnp.where(bottom, lines - count, 0), TILE)
    outside = jnp.where(bottom, lines, -HALO)

    def shift(a):
        return jnp.where(bottom, off[a : a + 1, lines - CHUNK :], off[a : a + 1, :CHUNK])

    build_bands(first, [(begin, count), (outside, HALO)], group, kernel, shift, band)
    for s in [*range(1, groups), 0]:
        at = pl.ds(pl.multiple_of((group[0] ^ s) * width, width), width)
        for a in range(acq):
            for x in range(2):
                lines_in = jnp.concatenate(
                    [slab[a, x, pl.ds(begin, count), at], halo[a, x, :, at]], axis=0
                )
                total = jnp.dot(band[a], lines_in, preferred_element_type=jnp.float32)
                outs[s][a, x] = total.astype(jnp.bfloat16)


SMEM = pl.BlockSpec(memory_space=pltpu.SMEM)
VMEM = pl.BlockSpec(memory_space=pltpu.VMEM)
ANY = pl.BlockSpec(memory_space=pl.ANY)


def resample_cost(acq, cols, rows):
    return pl.CostEstimate(
        flops=2 * acq * 2 * CHUNK * rows * cols,
        bytes_accessed=acq * 2 * (rows + CHUNK) * cols * 2,
        transcendentals=0,
    )


def resample_first(first, group, side, kernel, offsets, slc, groups):
    acq, _, lines, cols = slc.shape
    piece = pltpu.VMEM((acq, 2, CHUNK, cols // groups), jnp.bfloat16)
    halo = pltpu.VMEM((acq, 2, HALO, cols), jnp.bfloat16)
    slab = pltpu.VMEM(slc.shape, jnp.bfloat16)
    return pl.pallas_call(
        functools.partial(first_kernel, first, groups),
        in_specs=[SMEM, SMEM, ANY, ANY, ANY],
        out_specs=[VMEM] * (groups + 3),
        out_shape=[piece] * groups + [halo, halo, slab],
        scratch_shapes=[
            pltpu.VMEM((acq, CHUNK, lines), jnp.bfloat16),
            pltpu.VMEM(kernel.shape, kernel.dtype),
            pltpu.VMEM(offsets.shape, offsets.dtype),
            pltpu.SemaphoreType.DMA((groups + 2,)),
        ],
        compiler_params=pltpu.CompilerParams(vmem_limit_bytes=10 * MIB),
        cost_estimate=resample_cost(acq, cols, lines),
        name="resample_first",
    )(group, side, kernel, offsets, slc)


def resample_edge(parity, count, group, side, kernel, offsets, slab, halo, after, groups):
    acq, _, lines, cols = slab.shape
    piece = pltpu.VMEM((acq, 2, CHUNK, cols // groups), jnp.bfloat16)
    return pl.pallas_call(
        functools.partial(edge_kernel, groups, parity, count),
        in_specs=[SMEM, SMEM, VMEM, VMEM, VMEM, VMEM, ANY],
        out_specs=[VMEM] * groups,
        out_shape=[piece] * groups,
        scratch_shapes=[pltpu.VMEM((acq, CHUNK, count + HALO), jnp.bfloat16)],
        compiler_params=pltpu.CompilerParams(vmem_limit_bytes=10 * MIB),
        cost_estimate=resample_cost(acq, cols, count + HALO),
        name="resample_edge",
    )(group, side, kernel, offsets, slab, halo, after)


def slot_of(low, high):
    return high * (high - 1) // 2 + low


def look_sums(blocks, begin, parts, terms, sums, slot_rows, power_rows):
    acq, _, lines, width = blocks[0].shape
    looks = lines // LOOK_R
    windows = width // LOOK_C
    both = 2 * looks
    tiles = width // LANES
    total, fresh = len(blocks) * acq, begin * acq
    base = slot_of(0, fresh)
    split = (slot_of(0, total) - base) * both
    used = split + (total - fresh) * looks

    def pool(tile):
        row = lax.broadcasted_iota(jnp.int32, (2 * LANES, windows), 0)
        window = lax.broadcasted_iota(jnp.int32, (2 * LANES, windows), 1)
        wanted = tile * (LANES // LOOK_C) + (row % LANES) // LOOK_C
        return jnp.where(wanted == window, 1.0, 0.0).astype(jnp.bfloat16)

    def put(row, field):
        first = field.astype(jnp.bfloat16)
        terms[row : row + both, :LANES] = first
        terms[row : row + both, LANES:] = (field - first.astype(jnp.float32)).astype(jnp.bfloat16)

    def settle(tile):
        result = jnp.dot(terms[...], pool(tile), preferred_element_type=jnp.float32)
        sums[slot_rows : slot_rows + split, :] += result[:split]
        sums[power_rows : power_rows + used - split, :] += result[split:used]

    def unpack(tile):
        at = pl.ds(pl.multiple_of(tile * LANES, LANES), LANES)
        for r, block in enumerate(blocks):
            for a in range(acq):
                real = block[a, 0, :, at].astype(jnp.float32)
                imag = block[a, 1, :, at].astype(jnp.float32)
                parts[r * acq + a, 0] = real
                parts[r * acq + a, 1] = imag
                parts[r * acq + a, 2] = real + imag
                parts[r * acq + a, 3] = real - imag

    def cross(pairs):
        totals = {pair: [0.0, 0.0, 0.0] for pair in pairs}
        for j in range(LOOK_R):
            at = slice(j * looks, (j + 1) * looks)
            left = {i: [parts[i, c, at, :] for c in (2, 0, 1)] for i in sorted({i for i, _ in pairs})}
            right = {i: [parts[i, c, at, :] for c in (0, 2, 3)] for i in sorted({i for _, i in pairs})}
            for pair in pairs:
                for t in range(3):
                    totals[pair][t] = totals[pair][t] + left[pair[0]][t] * right[pair[1]][t]
        for i, k in pairs:
            one, two, three = totals[i, k]
            put((slot_of(i, k) - base) * both, jnp.concatenate([one - three, one - two], axis=0))

    def powers(members):
        fields = []
        for i in members:
            field = 0.0
            for j in range(LOOK_R):
                for c in range(2):
                    value = parts[i, c, j * looks : (j + 1) * looks, :]
                    field = field + value * value
            fields.append(field)
        put(split + (members[0] - fresh) * looks, jnp.concatenate(fields, axis=0))

    def work(tile):
        unpack(tile)
        for q in range(begin, len(blocks)):
            for r in range(q + 1):
                first = range(r * acq, (r + 1) * acq)
                second = range(q * acq, (q + 1) * acq)
                cross([(i, k) for i in first for k in second if i < k])
        for i in range(fresh, total, 2):
            powers((i, min(i + 1, total - 1)))

    def turn(tile, carry):
        settle(tile - 1)
        work(tile)
        return carry

    work(0)
    lax.fori_loop(1, tiles, turn, 0)
    settle(tiles - 1)


def near_kernel(groups, *rest):
    blocks, (sums, parts, terms) = rest[:groups], rest[groups:]
    acq, _, lines, _ = blocks[0].shape
    looks = lines // LOOK_R
    sums[...] = jnp.zeros(sums.shape, jnp.float32)
    look_sums(blocks, 0, parts, terms, sums, 0, slot_of(0, groups * acq) * 2 * looks)


def interfere_kernel(groups, known, turn, table, *rest):
    blocks, rest = rest[:groups], rest[groups:]
    out, parts, terms, sums, flat, inverse, slab, sem = rest[-8:]
    acq, _, lines, width = blocks[0].shape
    looks = lines // LOOK_R
    count = table.shape[1]
    both = 2 * looks
    total, fresh = groups * acq, known * acq
    start, split = slot_of(0, fresh) * both, slot_of(0, total) * both
    sums[...] = jnp.zeros(sums.shape, jnp.float32)
    if known:
        near = rest[0]
        sums[:start, :] = near[:start, :]
        sums[split : split + fresh * looks, :] = near[start : start + fresh * looks, :]
    look_sums(blocks, known, parts, terms, sums, start, split + fresh * looks)
    inverse[...] = lax.rsqrt(sums[split : split + total * looks, :] + 1e-6)

    def select(p, carry):
        at = pl.multiple_of(table[0, p] * both, both)
        m = pl.multiple_of(table[1, p] * looks, looks)
        s = pl.multiple_of(table[2, p] * looks, looks)
        scale = inverse[pl.ds(m, looks), :] * inverse[pl.ds(s, looks), :]
        turned = scale * table[3, p].astype(jnp.float32)
        value = sums[pl.ds(at, both), :] * jnp.concatenate([scale, turned], axis=0)
        flat[pl.ds(pl.multiple_of(p * both, both), both), :] = value
        return carry

    lax.fori_loop(0, count, select, 0, unroll=max(b for b in range(1, 7) if count % b == 0))
    copies = []
    for g in range(looks):
        for x in range(2):
            slab[x, g] = flat[pl.ds(x * looks + g, count, stride=both), :].T
        copies.append(pltpu.make_async_copy(slab.at[:, g], out.at[:, table[4, turn] * looks + g], sem.at[g]))
        copies[-1].start()
    for copy in copies:
        copy.wait()


def work_space(groups, known, acq, lines, looks):
    total, fresh = groups * acq, known * acq
    count = total - fresh
    rows = (slot_of(0, total) - slot_of(0, fresh)) * 2 * looks + (count + count % 2) * looks
    return [
        pltpu.VMEM((total, 4, lines, LANES), jnp.float32),
        pltpu.VMEM((rows, 2 * LANES), jnp.bfloat16),
    ]


def interfere_cost(pairs, acq, lines, width):
    return pl.CostEstimate(
        flops=pairs * 8 * lines * width,
        bytes_accessed=acq * 2 * lines * width * 2 * 12,
        transcendentals=0,
    )


def interfere_near(blocks):
    groups = len(blocks)
    acq, _, lines, width = blocks[0].shape
    looks, windows, total = lines // LOOK_R, width // LOOK_C, groups * acq
    return pl.pallas_call(
        functools.partial(near_kernel, groups),
        in_specs=[VMEM] * groups,
        out_specs=VMEM,
        out_shape=pltpu.VMEM(((slot_of(0, total) * 2 + total) * looks, windows), jnp.float32),
        scratch_shapes=work_space(groups, 0, acq, lines, looks),
        compiler_params=pltpu.CompilerParams(vmem_limit_bytes=8 * MIB),
        cost_estimate=interfere_cost(slot_of(0, total), total, lines, width),
        name="interfere_near",
    )(*blocks)


def interfere(turn, chunks, table, blocks, near, known, before):
    groups = len(blocks)
    acq, _, lines, width = blocks[0].shape
    looks, windows, count = lines // LOOK_R, width // LOOK_C, table.shape[1]
    total = groups * acq
    near = [] if near is None else [near]
    extra = [] if before is None else [before]
    return pl.pallas_call(
        functools.partial(interfere_kernel, groups, known, turn),
        in_specs=[SMEM] + [VMEM] * (groups + len(near)) + [ANY] * len(extra),
        out_specs=ANY,
        out_shape=pltpu.HBM((2, chunks * looks, windows, count), jnp.float32),
        scratch_shapes=work_space(groups, known, acq, lines, looks)
        + [
            pltpu.VMEM(((slot_of(0, total) * 2 + total) * looks, windows), jnp.float32),
            pltpu.VMEM((count * 2 * looks, windows), jnp.float32),
            pltpu.VMEM((total * looks, windows), jnp.float32),
            pltpu.VMEM((2, looks, windows, count), jnp.float32),
            pltpu.SemaphoreType.DMA((looks,)),
        ],
        input_output_aliases={} if before is None else {1 + groups + len(near): 0},
        compiler_params=pltpu.CompilerParams(vmem_limit_bytes=8 * MIB),
        cost_estimate=interfere_cost(count, total, lines, width),
        name="interfere",
    )(table, *blocks, *near, *extra)


def pair_table(pairs, groups, acq, mine, odd, chunks):
    apart = (pairs // acq) ^ mine
    rank = sum(jnp.where(apart == s, r, 0) for r, s in enumerate(ORDER))
    close = rank * acq + pairs % acq
    m, s = close[:, 0], close[:, 1]
    slot = slot_of(jnp.minimum(m, s), jnp.maximum(m, s))
    turn = jnp.arange(pairs.shape[0])
    edge = jnp.where((turn == 1) == (odd == 0), chunks - 1, 0)
    place = jnp.where(turn == 0, 1, edge)
    return jnp.stack([slot, m, s, jnp.where(m < s, 1, -1), place]).astype(jnp.int32)


def local(slc, offsets, weights, pairs):
    acq, _, lines, cols = slc.shape
    groups = lax.axis_size("acq")
    size = lax.axis_size("pix")
    row = lax.axis_index("pix")
    odd = row % 2
    group = jnp.reshape(lax.axis_index("acq"), (1,)).astype(jnp.int32)
    side = jnp.reshape(odd, (1,)).astype(jnp.int32)
    kernel = weights.T
    chunks = lines // CHUNK
    table = pair_table(pairs, groups, acq, group[0], odd, chunks)
    reach = CHUNK + TILE * 2

    def send(blocks):
        moved = [blocks[0]]
        for s in ORDER[1:]:
            moved.append(lax.ppermute(blocks[s], "acq", [(i, i ^ s) for i in range(groups)]))
        return moved

    def swap(halo, begin):
        pairs_up = [(i, i + 1) for i in range(begin, size - 1, 2)]
        return lax.ppermute(halo, "pix", pairs_up + [(j, i) for i, j in pairs_up])

    *blocks, inner, outer, slab = resample_first(
        CHUNK, group, side, *[pltpu.with_memory_space_constraint(t, pltpu.HBM) for t in (kernel, offsets, slc)], groups
    )
    inside = swap(inner, 0)
    middle = send(blocks)
    pieces = resample_edge(0, reach, group, side, kernel, offsets, slab, inside, inner, groups)
    across = swap(outer, 1)
    second = send(pieces)
    third = send(
        resample_edge(1, reach, group, side, kernel, offsets, slab, across, pieces[0], groups)
    )
    result = None
    for turn, (moved, known) in enumerate(((middle, 0), (second, 0), (third, 2))):
        near = None
        if known:
            mine, result = lax.optimization_barrier((moved[0], result))
            near = interfere_near([mine, *moved[1:known]])
        result = interfere(turn, chunks, table, moved, near, known, result)
    return jnp.transpose(result, (0, 3, 1, 2))


def solution(mesh):
    placed = (P("acq", None, "pix", None), P("acq", "pix"), P(), P())
    return jax.shard_map(
        local, mesh=mesh, in_specs=placed, out_specs=P(None, None, "pix", "acq"), check_vma=False
    )
```

```python
import functools

import jax
import jax.numpy as jnp
from jax import lax
from jax.experimental import pallas as pl
from jax.experimental.pallas import tpu as pltpu
from jax.sharding import PartitionSpec as P

LOOK_R = 4
LOOK_C = 16
CHUNK = 32
HALO = 24
ORDER = (0, 1, 2, 3)
TILE = 16
LANES = 128
MIB = 1024 * 1024


def build_bands(first, sources, group, kernel, shift, band):
    acq, taps = band.shape[0], kernel.shape[0]
    gains = kernel[...].astype(jnp.float32) * 0.125
    lane = lax.broadcasted_iota(jnp.int32, gains.shape, 1)
    rows = sum(count for _, count in sources)
    index = lax.broadcasted_iota(jnp.int32, (rows, CHUNK), 0)
    source = jnp.zeros((rows, CHUNK), jnp.int32)
    at = 0
    for begin, count in sources:
        source = jnp.where(index >= at, index + (begin - at), source)
        at += count
    target = first + lax.broadcasted_iota(jnp.int32, (rows, CHUNK), 1)
    base = source - target + (taps // 2 - 1)
    row = lax.broadcasted_iota(jnp.int32, (CHUNK, CHUNK), 0)
    col = lax.broadcasted_iota(jnp.int32, (CHUNK, CHUNK), 1)
    blocks = CHUNK // LOOK_R
    order = jnp.where(col == (row % blocks) * LOOK_R + row // blocks, 1.0, 0.0).astype(jnp.bfloat16)
    for a in range(acq):
        tap = base - shift(a)
        total = jnp.zeros((rows, CHUNK), jnp.float32)
        gain = jnp.sum(jnp.where(lane == group[0] * acq + a, gains, 0.0), axis=1, keepdims=True)
        for k in range(taps):
            total = jnp.where(tap == k, gain[k : k + 1, :], total)
        turned = lax.dot_general(
            order, total.astype(jnp.bfloat16), (((1,), (1,)), ((), ())),
            preferred_element_type=jnp.float32,
        )
        band[a] = turned.astype(jnp.bfloat16)


def copy_edge(bottom, slab, halo):
    lines = slab.shape[2]

    @pl.when(bottom)
    def _():
        halo[...] = slab[:, :, lines - HALO :, :]

    @pl.when(jnp.logical_not(bottom))
    def _():
        halo[...] = slab[:, :, :HALO, :]


def first_kernel(first, groups, group, side, kernel, off, slc, *rest):
    outs, (inner, outer, slab, band, gains, shifts, sems) = rest[:groups], rest[groups:]
    acq, _, lines, cols = slc.shape
    width = cols // groups

    def columns(s):
        return pl.ds(pl.multiple_of((group[0] ^ s) * width, width), width)

    order = [*range(1, groups), 0]
    small = [
        pltpu.make_async_copy(kernel, gains, sems.at[groups]),
        pltpu.make_async_copy(off, shifts, sems.at[groups + 1]),
    ]
    for copy in small:
        copy.start()
    copies = {}
    for s in order:
        at = columns(s)
        copies[s] = pltpu.make_async_copy(slc.at[:, :, :, at], slab.at[:, :, :, at], sems.at[s])
        copies[s].start()
    for copy in small:
        copy.wait()
    build_bands(first, [(0, lines)], group, gains, lambda a: shifts[a : a + 1, first : first + CHUNK], band)
    for s in order:
        copies[s].wait()
        at = columns(s)
        for a in range(acq):
            for x in range(2):
                total = jnp.dot(band[a], slab[a, x, :, at], preferred_element_type=jnp.float32)
                outs[s][a, x] = total.astype(jnp.bfloat16)
    copy_edge(side[0] == 0, slab, inner)
    copy_edge(side[0] == 1, slab, outer)


def edge_kernel(groups, parity, count, group, side, kernel, off, slab, halo, _, *rest):
    outs, band = rest[:groups], rest[-1]
    acq, _, lines, cols = slab.shape
    width = cols // groups
    bottom = side[0] == parity
    first = jnp.where(bottom, lines - CHUNK, 0)
    begin = pl.multiple_of(jnp.where(bottom, lines - count, 0), TILE)
    outside = jnp.where(bottom, lines, -HALO)

    def shift(a):
        return jnp.where(bottom, off[a : a + 1, lines - CHUNK :], off[a : a + 1, :CHUNK])

    build_bands(first, [(begin, count), (outside, HALO)], group, kernel, shift, band)
    for s in [*range(1, groups), 0]:
        at = pl.ds(pl.multiple_of((group[0] ^ s) * width, width), width)
        for a in range(acq):
            for x in range(2):
                lines_in = jnp.concatenate(
                    [slab[a, x, pl.ds(begin, count), at], halo[a, x, :, at]], axis=0
                )
                total = jnp.dot(band[a], lines_in, preferred_element_type=jnp.float32)
                outs[s][a, x] = total.astype(jnp.bfloat16)


SMEM = pl.BlockSpec(memory_space=pltpu.SMEM)
VMEM = pl.BlockSpec(memory_space=pltpu.VMEM)
ANY = pl.BlockSpec(memory_space=pl.ANY)


def resample_cost(acq, cols, rows):
    return pl.CostEstimate(
        flops=2 * acq * 2 * CHUNK * rows * cols,
        bytes_accessed=acq * 2 * (rows + CHUNK) * cols * 2,
        transcendentals=0,
    )


def resample_first(first, group, side, kernel, offsets, slc, groups):
    acq, _, lines, cols = slc.shape
    piece = pltpu.VMEM((acq, 2, CHUNK, cols // groups), jnp.bfloat16)
    halo = pltpu.VMEM((acq, 2, HALO, cols), jnp.bfloat16)
    slab = pltpu.VMEM(slc.shape, jnp.bfloat16)
    return pl.pallas_call(
        functools.partial(first_kernel, first, groups),
        in_specs=[SMEM, SMEM, ANY, ANY, ANY],
        out_specs=[VMEM] * (groups + 3),
        out_shape=[piece] * groups + [halo, halo, slab],
        scratch_shapes=[
            pltpu.VMEM((acq, CHUNK, lines), jnp.bfloat16),
            pltpu.VMEM(kernel.shape, kernel.dtype),
            pltpu.VMEM(offsets.shape, offsets.dtype),
            pltpu.SemaphoreType.DMA((groups + 2,)),
        ],
        compiler_params=pltpu.CompilerParams(vmem_limit_bytes=10 * MIB),
        cost_estimate=resample_cost(acq, cols, lines),
        name="resample_first",
    )(group, side, kernel, offsets, slc)


def resample_edge(parity, count, group, side, kernel, offsets, slab, halo, after, groups):
    acq, _, lines, cols = slab.shape
    piece = pltpu.VMEM((acq, 2, CHUNK, cols // groups), jnp.bfloat16)
    return pl.pallas_call(
        functools.partial(edge_kernel, groups, parity, count),
        in_specs=[SMEM, SMEM, VMEM, VMEM, VMEM, VMEM, ANY],
        out_specs=[VMEM] * groups,
        out_shape=[piece] * groups,
        scratch_shapes=[pltpu.VMEM((acq, CHUNK, count + HALO), jnp.bfloat16)],
        compiler_params=pltpu.CompilerParams(vmem_limit_bytes=10 * MIB),
        cost_estimate=resample_cost(acq, cols, count + HALO),
        name="resample_edge",
    )(group, side, kernel, offsets, slab, halo, after)


def slot_of(low, high):
    return high * (high - 1) // 2 + low


def look_sums(blocks, begin, parts, terms, sums, slot_rows, power_rows):
    acq, _, lines, width = blocks[0].shape
    looks = lines // LOOK_R
    both = 2 * looks
    tiles = width // LANES
    total, fresh = len(blocks) * acq, begin * acq
    base = slot_of(0, fresh)
    split = (slot_of(0, total) - base) * both
    used = split + (total - fresh) * looks

    def pool(tile):
        row = lax.broadcasted_iota(jnp.int32, (2 * LANES, LANES), 0)
        window = lax.broadcasted_iota(jnp.int32, (2 * LANES, LANES), 1) % (LANES // 2)
        wanted = tile * (LANES // LOOK_C) + (row % LANES) // LOOK_C
        return jnp.where(wanted == window, 1.0, 0.0).astype(jnp.bfloat16)

    def put(row, field):
        first = field.astype(jnp.bfloat16)
        terms[row : row + both, :LANES] = first
        terms[row : row + both, LANES:] = (field - first.astype(jnp.float32)).astype(jnp.bfloat16)

    def settle(tile):
        result = jnp.dot(terms[...], pool(tile), preferred_element_type=jnp.float32)
        sums[slot_rows : slot_rows + split, :] += result[:split]
        sums[power_rows : power_rows + used - split, :] += result[split:used]

    def unpack(tile):
        at = pl.ds(pl.multiple_of(tile * LANES, LANES), LANES)
        for r, block in enumerate(blocks):
            for a in range(acq):
                real = block[a, 0, :, at].astype(jnp.float32)
                imag = block[a, 1, :, at].astype(jnp.float32)
                parts[r * acq + a, 0] = real
                parts[r * acq + a, 1] = imag
                parts[r * acq + a, 2] = real + imag
                parts[r * acq + a, 3] = real - imag

    def cross(pairs):
        totals = {pair: [0.0, 0.0, 0.0] for pair in pairs}
        for j in range(LOOK_R):
            at = slice(j * looks, (j + 1) * looks)
            left = {i: [parts[i, c, at, :] for c in (2, 0, 1)] for i in sorted({i for i, _ in pairs})}
            right = {i: [parts[i, c, at, :] for c in (0, 2, 3)] for i in sorted({i for _, i in pairs})}
            for pair in pairs:
                for t in range(3):
                    totals[pair][t] = totals[pair][t] + left[pair[0]][t] * right[pair[1]][t]
        for i, k in pairs:
            one, two, three = totals[i, k]
            put((slot_of(i, k) - base) * both, jnp.concatenate([one - three, one - two], axis=0))

    def powers(members):
        fields = []
        for i in members:
            field = 0.0
            for j in range(LOOK_R):
                for c in range(2):
                    value = parts[i, c, j * looks : (j + 1) * looks, :]
                    field = field + value * value
            fields.append(field)
        put(split + (members[0] - fresh) * looks, jnp.concatenate(fields, axis=0))

    def work(tile):
        unpack(tile)
        for q in range(begin, len(blocks)):
            for r in range(q + 1):
                first = range(r * acq, (r + 1) * acq)
                second = range(q * acq, (q + 1) * acq)
                cross([(i, k) for i in first for k in second if i < k])
        for i in range(fresh, total, 2):
            powers((i, min(i + 1, total - 1)))

    def turn(tile, carry):
        settle(tile - 1)
        work(tile)
        return carry

    work(0)
    lax.fori_loop(1, tiles, turn, 0)
    settle(tiles - 1)


def near_kernel(groups, *rest):
    blocks, (sums, parts, terms) = rest[:groups], rest[groups:]
    acq, _, lines, _ = blocks[0].shape
    looks = lines // LOOK_R
    sums[...] = jnp.zeros(sums.shape, jnp.float32)
    look_sums(blocks, 0, parts, terms, sums, 0, slot_of(0, groups * acq) * 2 * looks)


def interfere_kernel(groups, known, turn, table, *rest):
    blocks, rest = rest[:groups], rest[groups:]
    out, parts, terms, sums, flat, inverse, slab, sem = rest[-8:]
    acq, _, lines, width = blocks[0].shape
    looks = lines // LOOK_R
    count = table.shape[1]
    both = 2 * looks
    total, fresh = groups * acq, known * acq
    start, split = slot_of(0, fresh) * both, slot_of(0, total) * both
    sums[...] = jnp.zeros(sums.shape, jnp.float32)
    if known:
        near = rest[0]
        sums[:start, :] = near[:start, :]
        sums[split : split + fresh * looks, :] = near[start : start + fresh * looks, :]
    windows = width // LOOK_C
    look_sums(blocks, known, parts, terms, sums, start, split + fresh * looks)
    inverse[...] = lax.rsqrt(sums[split : split + total * looks, :] + 1e-6)

    left = lax.broadcasted_iota(jnp.int32, (looks, LANES), 1) < LANES // 2

    def select(p, carry):
        at = pl.multiple_of(table[0, p] * both, both)
        m = pl.multiple_of(table[1, p] * looks, looks)
        s = pl.multiple_of(table[2, p] * looks, looks)
        scale = inverse[pl.ds(m, looks), :] * inverse[pl.ds(s, looks), :]
        imag = sums[pl.ds(at + looks, looks), :] * table[3, p].astype(jnp.float32)
        value = jnp.where(left, sums[pl.ds(at, looks), :], imag) * scale
        flat[pl.ds(pl.multiple_of(p * looks, looks), looks), :] = value
        return carry

    lax.fori_loop(0, count, select, 0, unroll=max(b for b in range(1, 7) if count % b == 0))
    copies = []
    for g in range(looks):
        turned = flat[pl.ds(g, count, stride=looks), :].T
        for x in range(2):
            slab[x, g] = turned[x * (LANES // 2) : x * (LANES // 2) + windows]
        copies.append(pltpu.make_async_copy(slab.at[:, g], out.at[:, table[4, turn] * looks + g], sem.at[g]))
        copies[-1].start()
    for copy in copies:
        copy.wait()


def work_space(groups, known, acq, lines, looks):
    total, fresh = groups * acq, known * acq
    count = total - fresh
    rows = (slot_of(0, total) - slot_of(0, fresh)) * 2 * looks + (count + count % 2) * looks
    return [
        pltpu.VMEM((total, 4, lines, LANES), jnp.float32),
        pltpu.VMEM((rows, 2 * LANES), jnp.bfloat16),
    ]


def interfere_cost(pairs, acq, lines, width):
    return pl.CostEstimate(
        flops=pairs * 8 * lines * width,
        bytes_accessed=acq * 2 * lines * width * 2 * 12,
        transcendentals=0,
    )


def interfere_near(blocks):
    groups = len(blocks)
    acq, _, lines, width = blocks[0].shape
    looks, windows, total = lines // LOOK_R, width // LOOK_C, groups * acq
    return pl.pallas_call(
        functools.partial(near_kernel, groups),
        in_specs=[VMEM] * groups,
        out_specs=VMEM,
        out_shape=pltpu.VMEM(((slot_of(0, total) * 2 + total) * looks, LANES), jnp.float32),
        scratch_shapes=work_space(groups, 0, acq, lines, looks),
        compiler_params=pltpu.CompilerParams(vmem_limit_bytes=8 * MIB),
        cost_estimate=interfere_cost(slot_of(0, total), total, lines, width),
        name="interfere_near",
    )(*blocks)


def interfere(turn, chunks, table, blocks, near, known, before):
    groups = len(blocks)
    acq, _, lines, width = blocks[0].shape
    looks, windows, count = lines // LOOK_R, width // LOOK_C, table.shape[1]
    total = groups * acq
    near = [] if near is None else [near]
    extra = [] if before is None else [before]
    return pl.pallas_call(
        functools.partial(interfere_kernel, groups, known, turn),
        in_specs=[SMEM] + [VMEM] * (groups + len(near)) + [ANY] * len(extra),
        out_specs=ANY,
        out_shape=pltpu.HBM((2, chunks * looks, windows, count), jnp.float32),
        scratch_shapes=work_space(groups, known, acq, lines, looks)
        + [
            pltpu.VMEM(((slot_of(0, total) * 2 + total) * looks, LANES), jnp.float32),
            pltpu.VMEM((count * looks, LANES), jnp.float32),
            pltpu.VMEM((total * looks, LANES), jnp.float32),
            pltpu.VMEM((2, looks, windows, count), jnp.float32),
            pltpu.SemaphoreType.DMA((looks,)),
        ],
        input_output_aliases={} if before is None else {1 + groups + len(near): 0},
        compiler_params=pltpu.CompilerParams(vmem_limit_bytes=8 * MIB),
        cost_estimate=interfere_cost(count, total, lines, width),
        name="interfere",
    )(table, *blocks, *near, *extra)


def pair_table(pairs, groups, acq, mine, odd, chunks):
    apart = (pairs // acq) ^ mine
    rank = sum(jnp.where(apart == s, r, 0) for r, s in enumerate(ORDER))
    close = rank * acq + pairs % acq
    m, s = close[:, 0], close[:, 1]
    slot = slot_of(jnp.minimum(m, s), jnp.maximum(m, s))
    turn = jnp.arange(pairs.shape[0])
    edge = jnp.where((turn == 1) == (odd == 0), chunks - 1, 0)
    place = jnp.where(turn == 0, 1, edge)
    return jnp.stack([slot, m, s, jnp.where(m < s, 1, -1), place]).astype(jnp.int32)


def local(slc, offsets, weights, pairs):
    acq, _, lines, cols = slc.shape
    groups = lax.axis_size("acq")
    size = lax.axis_size("pix")
    row = lax.axis_index("pix")
    odd = row % 2
    group = jnp.reshape(lax.axis_index("acq"), (1,)).astype(jnp.int32)
    side = jnp.reshape(odd, (1,)).astype(jnp.int32)
    kernel = weights.T
    chunks = lines // CHUNK
    table = pair_table(pairs, groups, acq, group[0], odd, chunks)
    reach = CHUNK + TILE * 2

    def send(blocks):
        moved = [blocks[0]]
        for s in ORDER[1:]:
            moved.append(lax.ppermute(blocks[s], "acq", [(i, i ^ s) for i in range(groups)]))
        return moved

    def swap(halo, begin):
        pairs_up = [(i, i + 1) for i in range(begin, size - 1, 2)]
        return lax.ppermute(halo, "pix", pairs_up + [(j, i) for i, j in pairs_up])

    *blocks, inner, outer, slab = resample_first(
        CHUNK, group, side, *[pltpu.with_memory_space_constraint(t, pltpu.HBM) for t in (kernel, offsets, slc)], groups
    )
    inside = swap(inner, 0)
    middle = send(blocks)
    pieces = resample_edge(0, reach, group, side, kernel, offsets, slab, inside, inner, groups)
    across = swap(outer, 1)
    second = send(pieces)
    third = send(
        resample_edge(1, reach, group, side, kernel, offsets, slab, across, pieces[0], groups)
    )
    result = None
    for turn, (moved, known) in enumerate(((middle, 0), (second, 0), (third, 2))):
        near = None
        if known:
            mine, result = lax.optimization_barrier((moved[0], result))
            near = interfere_near([mine, *moved[1:known]])
        result = interfere(turn, chunks, table, moved, near, known, result)
    return jnp.transpose(result, (0, 3, 1, 2))


def solution(mesh):
    placed = (P("acq", None, "pix", None), P("acq", "pix"), P(), P())
    return jax.shard_map(
        local, mesh=mesh, in_specs=placed, out_specs=P(None, None, "pix", "acq"), check_vma=False
    )
```

```python
import functools

import jax
import jax.numpy as jnp
from jax import lax
from jax.experimental import pallas as pl
from jax.experimental.pallas import tpu as pltpu
from jax.sharding import PartitionSpec as P

LOOK_R = 4
LOOK_C = 16
CHUNK = 32
HALO = 24
ORDER = (0, 1, 2, 3)
TILE = 16
LANES = 128
MIB = 1024 * 1024


def build_bands(first, sources, group, kernel, shift, band):
    acq, taps = band.shape[0], kernel.shape[0]
    gains = kernel[...].astype(jnp.float32) * 0.125
    lane = lax.broadcasted_iota(jnp.int32, gains.shape, 1)
    rows = sum(count for _, count in sources)
    index = lax.broadcasted_iota(jnp.int32, (rows, CHUNK), 0)
    source = jnp.zeros((rows, CHUNK), jnp.int32)
    at = 0
    for begin, count in sources:
        source = jnp.where(index >= at, index + (begin - at), source)
        at += count
    target = first + lax.broadcasted_iota(jnp.int32, (rows, CHUNK), 1)
    base = source - target + (taps // 2 - 1)
    row = lax.broadcasted_iota(jnp.int32, (CHUNK, CHUNK), 0)
    col = lax.broadcasted_iota(jnp.int32, (CHUNK, CHUNK), 1)
    blocks = CHUNK // LOOK_R
    order = jnp.where(col == (row % blocks) * LOOK_R + row // blocks, 1.0, 0.0).astype(jnp.bfloat16)
    for a in range(acq):
        tap = base - shift(a)
        total = jnp.zeros((rows, CHUNK), jnp.float32)
        gain = jnp.sum(jnp.where(lane == group[0] * acq + a, gains, 0.0), axis=1, keepdims=True)
        for k in range(taps):
            total = jnp.where(tap == k, gain[k : k + 1, :], total)
        turned = lax.dot_general(
            order, total.astype(jnp.bfloat16), (((1,), (1,)), ((), ())),
            preferred_element_type=jnp.float32,
        )
        band[a] = turned.astype(jnp.bfloat16)


def copy_edge(bottom, slab, halo):
    lines = slab.shape[2]

    @pl.when(bottom)
    def _():
        halo[...] = slab[:, :, lines - HALO :, :]

    @pl.when(jnp.logical_not(bottom))
    def _():
        halo[...] = slab[:, :, :HALO, :]


def first_kernel(first, groups, group, side, kernel, off, slc, *rest):
    outs, (inner, outer, slab, band, gains, shifts, sems) = rest[:groups], rest[groups:]
    acq, _, lines, cols = slc.shape
    width = cols // groups

    def columns(s):
        return pl.ds(pl.multiple_of((group[0] ^ s) * width, width), width)

    order = [*range(1, groups), 0]
    small = [
        pltpu.make_async_copy(kernel, gains, sems.at[groups]),
        pltpu.make_async_copy(off, shifts, sems.at[groups + 1]),
    ]
    for copy in small:
        copy.start()
    copies = {}
    for s in order:
        at = columns(s)
        copies[s] = pltpu.make_async_copy(slc.at[:, :, :, at], slab.at[:, :, :, at], sems.at[s])
        copies[s].start()
    for copy in small:
        copy.wait()
    build_bands(first, [(0, lines)], group, gains, lambda a: shifts[a : a + 1, first : first + CHUNK], band)
    for s in order:
        copies[s].wait()
        at = columns(s)
        for a in range(acq):
            for x in range(2):
                total = jnp.dot(band[a], slab[a, x, :, at], preferred_element_type=jnp.float32)
                outs[s][a, x] = total.astype(jnp.bfloat16)
    copy_edge(side[0] == 0, slab, inner)
    copy_edge(side[0] == 1, slab, outer)


def edge_kernel(groups, parity, count, group, side, kernel, off, slab, halo, _, *rest):
    outs, band = rest[:groups], rest[-1]
    acq, _, lines, cols = slab.shape
    width = cols // groups
    bottom = side[0] == parity
    first = jnp.where(bottom, lines - CHUNK, 0)
    begin = pl.multiple_of(jnp.where(bottom, lines - count, 0), TILE)
    outside = jnp.where(bottom, lines, -HALO)

    def shift(a):
        return jnp.where(bottom, off[a : a + 1, lines - CHUNK :], off[a : a + 1, :CHUNK])

    build_bands(first, [(begin, count), (outside, HALO)], group, kernel, shift, band)
    for s in [*range(1, groups), 0]:
        at = pl.ds(pl.multiple_of((group[0] ^ s) * width, width), width)
        for a in range(acq):
            for x in range(2):
                lines_in = jnp.concatenate(
                    [slab[a, x, pl.ds(begin, count), at], halo[a, x, :, at]], axis=0
                )
                total = jnp.dot(band[a], lines_in, preferred_element_type=jnp.float32)
                outs[s][a, x] = total.astype(jnp.bfloat16)


SMEM = pl.BlockSpec(memory_space=pltpu.SMEM)
VMEM = pl.BlockSpec(memory_space=pltpu.VMEM)
ANY = pl.BlockSpec(memory_space=pl.ANY)


def resample_cost(acq, cols, rows):
    return pl.CostEstimate(
        flops=2 * acq * 2 * CHUNK * rows * cols,
        bytes_accessed=acq * 2 * (rows + CHUNK) * cols * 2,
        transcendentals=0,
    )


def resample_first(first, group, side, kernel, offsets, slc, groups):
    acq, _, lines, cols = slc.shape
    piece = pltpu.VMEM((acq, 2, CHUNK, cols // groups), jnp.bfloat16)
    halo = pltpu.VMEM((acq, 2, HALO, cols), jnp.bfloat16)
    slab = pltpu.VMEM(slc.shape, jnp.bfloat16)
    return pl.pallas_call(
        functools.partial(first_kernel, first, groups),
        in_specs=[SMEM, SMEM, ANY, ANY, ANY],
        out_specs=[VMEM] * (groups + 3),
        out_shape=[piece] * groups + [halo, halo, slab],
        scratch_shapes=[
            pltpu.VMEM((acq, CHUNK, lines), jnp.bfloat16),
            pltpu.VMEM(kernel.shape, kernel.dtype),
            pltpu.VMEM(offsets.shape, offsets.dtype),
            pltpu.SemaphoreType.DMA((groups + 2,)),
        ],
        compiler_params=pltpu.CompilerParams(vmem_limit_bytes=10 * MIB),
        cost_estimate=resample_cost(acq, cols, lines),
        name="resample_first",
    )(group, side, kernel, offsets, slc)


def resample_edge(parity, count, group, side, kernel, offsets, slab, halo, after, groups):
    acq, _, lines, cols = slab.shape
    piece = pltpu.VMEM((acq, 2, CHUNK, cols // groups), jnp.bfloat16)
    return pl.pallas_call(
        functools.partial(edge_kernel, groups, parity, count),
        in_specs=[SMEM, SMEM, VMEM, VMEM, VMEM, VMEM, ANY],
        out_specs=[VMEM] * groups,
        out_shape=[piece] * groups,
        scratch_shapes=[pltpu.VMEM((acq, CHUNK, count + HALO), jnp.bfloat16)],
        compiler_params=pltpu.CompilerParams(vmem_limit_bytes=10 * MIB),
        cost_estimate=resample_cost(acq, cols, count + HALO),
        name="resample_edge",
    )(group, side, kernel, offsets, slab, halo, after)


def slot_of(low, high):
    return high * (high - 1) // 2 + low


def look_sums(blocks, begin, parts, terms, sums, slot_rows, power_rows):
    acq, _, lines, width = blocks[0].shape
    looks = lines // LOOK_R
    both = 2 * looks
    tiles = width // LANES
    total, fresh = len(blocks) * acq, begin * acq
    base = slot_of(0, fresh)
    split = (slot_of(0, total) - base) * both
    used = split + (total - fresh) * looks

    def pool(tile):
        row = lax.broadcasted_iota(jnp.int32, (2 * LANES, LANES), 0)
        window = lax.broadcasted_iota(jnp.int32, (2 * LANES, LANES), 1) % (LANES // 2)
        wanted = tile * (LANES // LOOK_C) + (row % LANES) // LOOK_C
        return jnp.where(wanted == window, 1.0, 0.0).astype(jnp.bfloat16)

    def put(row, field):
        first = field.astype(jnp.bfloat16)
        terms[row : row + both, :LANES] = first
        terms[row : row + both, LANES:] = (field - first.astype(jnp.float32)).astype(jnp.bfloat16)

    def settle(tile):
        result = jnp.dot(terms[...], pool(tile), preferred_element_type=jnp.float32)
        sums[slot_rows : slot_rows + split, :] += result[:split]
        sums[power_rows : power_rows + used - split, :] += result[split:used]

    def unpack(tile):
        at = pl.ds(pl.multiple_of(tile * LANES, LANES), LANES)
        for r, block in enumerate(blocks):
            for a in range(acq):
                real = block[a, 0, :, at].astype(jnp.float32)
                imag = block[a, 1, :, at].astype(jnp.float32)
                parts[r * acq + a, 0] = real
                parts[r * acq + a, 1] = imag
                parts[r * acq + a, 2] = real + imag
                parts[r * acq + a, 3] = real - imag

    def cross(pairs):
        totals = {pair: [0.0, 0.0, 0.0] for pair in pairs}
        for j in range(LOOK_R):
            at = slice(j * looks, (j + 1) * looks)
            left = {i: [parts[i, c, at, :] for c in (2, 0, 1)] for i in sorted({i for i, _ in pairs})}
            right = {i: [parts[i, c, at, :] for c in (0, 2, 3)] for i in sorted({i for _, i in pairs})}
            for pair in pairs:
                for t in range(3):
                    totals[pair][t] = totals[pair][t] + left[pair[0]][t] * right[pair[1]][t]
        for i, k in pairs:
            one, two, three = totals[i, k]
            put((slot_of(i, k) - base) * both, jnp.concatenate([one - three, one - two], axis=0))

    def powers(members):
        fields = []
        for i in members:
            field = 0.0
            for j in range(LOOK_R):
                for c in range(2):
                    value = parts[i, c, j * looks : (j + 1) * looks, :]
                    field = field + value * value
            fields.append(field)
        put(split + (members[0] - fresh) * looks, jnp.concatenate(fields, axis=0))

    def work(tile):
        unpack(tile)
        for q in range(begin, len(blocks)):
            for r in range(q + 1):
                first = range(r * acq, (r + 1) * acq)
                second = range(q * acq, (q + 1) * acq)
                cross([(i, k) for i in first for k in second if i < k])
        for i in range(fresh, total, 2):
            powers((i, min(i + 1, total - 1)))

    def turn(tile, carry):
        settle(tile - 1)
        work(tile)
        return carry

    work(0)
    lax.fori_loop(1, tiles, turn, 0)
    settle(tiles - 1)


def near_kernel(groups, *rest):
    blocks, (sums, parts, terms) = rest[:groups], rest[groups:]
    acq, _, lines, _ = blocks[0].shape
    looks = lines // LOOK_R
    sums[...] = jnp.zeros(sums.shape, jnp.float32)
    look_sums(blocks, 0, parts, terms, sums, 0, slot_of(0, groups * acq) * 2 * looks)


def interfere_kernel(via, known, turn, table, *rest):
    groups = len(via)
    blocks, rest = [rest[via.index(r)] for r in range(groups)], rest[groups:]
    out, parts, terms, sums, flat, inverse, slab, sem = rest[-8:]
    acq, _, lines, width = blocks[0].shape
    looks = lines // LOOK_R
    count = table.shape[1]
    both = 2 * looks
    total, fresh = groups * acq, known * acq
    start, split = slot_of(0, fresh) * both, slot_of(0, total) * both
    sums[...] = jnp.zeros(sums.shape, jnp.float32)
    if known:
        near = rest[0]
        sums[:start, :] = near[:start, :]
        sums[split : split + fresh * looks, :] = near[start : start + fresh * looks, :]
    windows = width // LOOK_C
    look_sums(blocks, known, parts, terms, sums, start, split + fresh * looks)
    inverse[...] = lax.rsqrt(sums[split : split + total * looks, :] + 1e-6)

    left = lax.broadcasted_iota(jnp.int32, (looks, LANES), 1) < LANES // 2

    def select(p, carry):
        at = pl.multiple_of(table[0, p] * both, both)
        m = pl.multiple_of(table[1, p] * looks, looks)
        s = pl.multiple_of(table[2, p] * looks, looks)
        scale = inverse[pl.ds(m, looks), :] * inverse[pl.ds(s, looks), :]
        imag = sums[pl.ds(at + looks, looks), :] * table[3, p].astype(jnp.float32)
        value = jnp.where(left, sums[pl.ds(at, looks), :], imag) * scale
        flat[pl.ds(pl.multiple_of(p * looks, looks), looks), :] = value
        return carry

    lax.fori_loop(0, count, select, 0, unroll=max(b for b in range(1, 7) if count % b == 0))
    copies = []
    for g in range(looks):
        turned = flat[pl.ds(g, count, stride=looks), :].T
        for x in range(2):
            slab[x, g] = turned[x * (LANES // 2) : x * (LANES // 2) + windows]
        copies.append(pltpu.make_async_copy(slab.at[:, g], out.at[:, table[4, turn] * looks + g], sem.at[g]))
        copies[-1].start()
    for copy in copies:
        copy.wait()


def work_space(groups, known, acq, lines, looks):
    total, fresh = groups * acq, known * acq
    count = total - fresh
    rows = (slot_of(0, total) - slot_of(0, fresh)) * 2 * looks + (count + count % 2) * looks
    return [
        pltpu.VMEM((total, 4, lines, LANES), jnp.float32),
        pltpu.VMEM((rows, 2 * LANES), jnp.bfloat16),
    ]


def interfere_cost(pairs, acq, lines, width):
    return pl.CostEstimate(
        flops=pairs * 8 * lines * width,
        bytes_accessed=acq * 2 * lines * width * 2 * 12,
        transcendentals=0,
    )


def interfere_near(blocks):
    groups = len(blocks)
    acq, _, lines, width = blocks[0].shape
    looks, windows, total = lines // LOOK_R, width // LOOK_C, groups * acq
    return pl.pallas_call(
        functools.partial(near_kernel, groups),
        in_specs=[VMEM] * groups,
        out_specs=VMEM,
        out_shape=pltpu.VMEM(((slot_of(0, total) * 2 + total) * looks, LANES), jnp.float32),
        scratch_shapes=work_space(groups, 0, acq, lines, looks),
        compiler_params=pltpu.CompilerParams(vmem_limit_bytes=8 * MIB),
        cost_estimate=interfere_cost(slot_of(0, total), total, lines, width),
        name="interfere_near",
    )(*blocks)


def interfere(turn, chunks, table, blocks, via, near, known, before):
    groups = len(blocks)
    acq, _, lines, width = blocks[0].shape
    looks, windows, count = lines // LOOK_R, width // LOOK_C, table.shape[1]
    total = groups * acq
    near = [] if near is None else [near]
    extra = [] if before is None else [before]
    return pl.pallas_call(
        functools.partial(interfere_kernel, via, known, turn),
        in_specs=[SMEM] + [VMEM] * (groups + len(near)) + [ANY] * len(extra),
        out_specs=ANY,
        out_shape=pltpu.HBM((2, chunks * looks, windows, count), jnp.float32),
        scratch_shapes=work_space(groups, known, acq, lines, looks)
        + [
            pltpu.VMEM(((slot_of(0, total) * 2 + total) * looks, LANES), jnp.float32),
            pltpu.VMEM((count * looks, LANES), jnp.float32),
            pltpu.VMEM((total * looks, LANES), jnp.float32),
            pltpu.VMEM((2, looks, windows, count), jnp.float32),
            pltpu.SemaphoreType.DMA((looks,)),
        ],
        input_output_aliases={} if before is None else {1 + groups + len(near): 0},
        compiler_params=pltpu.CompilerParams(vmem_limit_bytes=8 * MIB),
        cost_estimate=interfere_cost(count, total, lines, width),
        name="interfere",
    )(table, *[blocks[r] for r in via], *near, *extra)


def pair_table(pairs, groups, acq, mine, odd, chunks):
    apart = (pairs // acq) ^ mine
    rank = sum(jnp.where(apart == s, r, 0) for r, s in enumerate(ORDER))
    close = rank * acq + pairs % acq
    m, s = close[:, 0], close[:, 1]
    slot = slot_of(jnp.minimum(m, s), jnp.maximum(m, s))
    turn = jnp.arange(pairs.shape[0])
    edge = jnp.where((turn == 1) == (odd == 0), chunks - 1, 0)
    place = jnp.where(turn == 0, 1, edge)
    return jnp.stack([slot, m, s, jnp.where(m < s, 1, -1), place]).astype(jnp.int32)


def local(slc, offsets, weights, pairs):
    acq, _, lines, cols = slc.shape
    groups = lax.axis_size("acq")
    size = lax.axis_size("pix")
    row = lax.axis_index("pix")
    odd = row % 2
    group = jnp.reshape(lax.axis_index("acq"), (1,)).astype(jnp.int32)
    side = jnp.reshape(odd, (1,)).astype(jnp.int32)
    kernel = weights.T
    chunks = lines // CHUNK
    table = pair_table(pairs, groups, acq, group[0], odd, chunks)
    reach = CHUNK + TILE * 2

    def send(blocks):
        moved = [blocks[0]]
        for s in ORDER[1:]:
            moved.append(lax.ppermute(blocks[s], "acq", [(i, i ^ s) for i in range(groups)]))
        return moved

    def swap(halo, begin):
        pairs_up = [(i, i + 1) for i in range(begin, size - 1, 2)]
        return lax.ppermute(halo, "pix", pairs_up + [(j, i) for i, j in pairs_up])

    *blocks, inner, outer, slab = resample_first(
        CHUNK, group, side, *[pltpu.with_memory_space_constraint(t, pltpu.HBM) for t in (kernel, offsets, slc)], groups
    )
    inside = swap(inner, 0)
    middle = send(blocks)
    pieces = resample_edge(0, reach, group, side, kernel, offsets, slab, inside, inner, groups)
    across = swap(outer, 1)
    second = send(pieces)
    third = send(
        resample_edge(1, reach, group, side, kernel, offsets, slab, across, pieces[0], groups)
    )
    result = None
    for turn, (moved, known) in enumerate(((middle, 0), (second, 0), (third, 2))):
        near = None
        if known:
            mine, result = lax.optimization_barrier((moved[0], result))
            near = interfere_near([mine, *moved[1:known]])
        result = interfere(turn, chunks, table, moved, ((0, 2, 1, 3), (0, 2, 1, 3), (0, 2, 1, 3))[turn], near, known, result)
    return jnp.transpose(result, (0, 3, 1, 2))


def solution(mesh):
    placed = (P("acq", None, "pix", None), P("acq", "pix"), P(), P())
    return jax.shard_map(
        local, mesh=mesh, in_specs=placed, out_specs=P(None, None, "pix", "acq"), check_vma=False
    )
```

```python
import functools

import jax
import jax.numpy as jnp
from jax import lax
from jax.experimental import pallas as pl
from jax.experimental.pallas import tpu as pltpu
from jax.sharding import PartitionSpec as P

LOOK_R = 4
LOOK_C = 16
CHUNK = 32
HALO = 24
ORDER = (0, 1, 2, 3)
TILE = 16
LANES = 128
MIB = 1024 * 1024


def build_bands(first, sources, group, kernel, shift, band):
    acq, taps = band.shape[0], kernel.shape[0]
    gains = kernel[...].astype(jnp.float32) * 0.125
    lane = lax.broadcasted_iota(jnp.int32, gains.shape, 1)
    rows = sum(count for _, count in sources)
    index = lax.broadcasted_iota(jnp.int32, (rows, CHUNK), 0)
    source = jnp.zeros((rows, CHUNK), jnp.int32)
    at = 0
    for begin, count in sources:
        source = jnp.where(index >= at, index + (begin - at), source)
        at += count
    target = first + lax.broadcasted_iota(jnp.int32, (rows, CHUNK), 1)
    base = source - target + (taps // 2 - 1)
    row = lax.broadcasted_iota(jnp.int32, (CHUNK, CHUNK), 0)
    col = lax.broadcasted_iota(jnp.int32, (CHUNK, CHUNK), 1)
    blocks = CHUNK // LOOK_R
    order = jnp.where(col == (row % blocks) * LOOK_R + row // blocks, 1.0, 0.0).astype(jnp.bfloat16)
    for a in range(acq):
        tap = base - shift(a)
        total = jnp.zeros((rows, CHUNK), jnp.float32)
        gain = jnp.sum(jnp.where(lane == group[0] * acq + a, gains, 0.0), axis=1, keepdims=True)
        for k in range(taps):
            total = jnp.where(tap == k, gain[k : k + 1, :], total)
        turned = lax.dot_general(
            order, total.astype(jnp.bfloat16), (((1,), (1,)), ((), ())),
            preferred_element_type=jnp.float32,
        )
        band[a] = turned.astype(jnp.bfloat16)


def copy_edge(bottom, slab, halo):
    lines = slab.shape[2]

    @pl.when(bottom)
    def _():
        halo[...] = slab[:, :, lines - HALO :, :]

    @pl.when(jnp.logical_not(bottom))
    def _():
        halo[...] = slab[:, :, :HALO, :]


def first_kernel(first, groups, group, side, kernel, off, slc, *rest):
    outs, (inner, outer, slab, band, gains, shifts, sems) = rest[:groups], rest[groups:]
    acq, _, lines, cols = slc.shape
    width = cols // groups

    def columns(s):
        return pl.ds(pl.multiple_of((group[0] ^ s) * width, width), width)

    order = [*range(1, groups), 0]
    small = [
        pltpu.make_async_copy(kernel, gains, sems.at[groups]),
        pltpu.make_async_copy(off, shifts, sems.at[groups + 1]),
    ]
    for copy in small:
        copy.start()
    copies = {}
    for s in order:
        at = columns(s)
        copies[s] = pltpu.make_async_copy(slc.at[:, :, :, at], slab.at[:, :, :, at], sems.at[s])
        copies[s].start()
    for copy in small:
        copy.wait()
    build_bands(first, [(0, lines)], group, gains, lambda a: shifts[a : a + 1, first : first + CHUNK], band)
    for s in order:
        copies[s].wait()
        at = columns(s)
        for a in range(acq):
            for x in range(2):
                total = jnp.dot(band[a], slab[a, x, :, at], preferred_element_type=jnp.float32)
                outs[s][a, x] = total.astype(jnp.bfloat16)
    copy_edge(side[0] == 0, slab, inner)
    copy_edge(side[0] == 1, slab, outer)


def edge_kernel(groups, parity, count, group, side, kernel, off, slab, halo, _, *rest):
    outs, band = rest[:groups], rest[-1]
    acq, _, lines, cols = slab.shape
    width = cols // groups
    bottom = side[0] == parity
    first = jnp.where(bottom, lines - CHUNK, 0)
    begin = pl.multiple_of(jnp.where(bottom, lines - count, 0), TILE)
    outside = jnp.where(bottom, lines, -HALO)

    def shift(a):
        return jnp.where(bottom, off[a : a + 1, lines - CHUNK :], off[a : a + 1, :CHUNK])

    build_bands(first, [(begin, count), (outside, HALO)], group, kernel, shift, band)
    for s in [*range(1, groups), 0]:
        at = pl.ds(pl.multiple_of((group[0] ^ s) * width, width), width)
        for a in range(acq):
            for x in range(2):
                lines_in = jnp.concatenate(
                    [slab[a, x, pl.ds(begin, count), at], halo[a, x, :, at]], axis=0
                )
                total = jnp.dot(band[a], lines_in, preferred_element_type=jnp.float32)
                outs[s][a, x] = total.astype(jnp.bfloat16)


SMEM = pl.BlockSpec(memory_space=pltpu.SMEM)
VMEM = pl.BlockSpec(memory_space=pltpu.VMEM)
ANY = pl.BlockSpec(memory_space=pl.ANY)


def resample_cost(acq, cols, rows):
    return pl.CostEstimate(
        flops=2 * acq * 2 * CHUNK * rows * cols,
        bytes_accessed=acq * 2 * (rows + CHUNK) * cols * 2,
        transcendentals=0,
    )


def resample_first(first, group, side, kernel, offsets, slc, groups):
    acq, _, lines, cols = slc.shape
    piece = pltpu.VMEM((acq, 2, CHUNK, cols // groups), jnp.bfloat16)
    halo = pltpu.VMEM((acq, 2, HALO, cols), jnp.bfloat16)
    slab = pltpu.VMEM(slc.shape, jnp.bfloat16)
    return pl.pallas_call(
        functools.partial(first_kernel, first, groups),
        in_specs=[SMEM, SMEM, ANY, ANY, ANY],
        out_specs=[VMEM] * (groups + 3),
        out_shape=[piece] * groups + [halo, halo, slab],
        scratch_shapes=[
            pltpu.VMEM((acq, CHUNK, lines), jnp.bfloat16),
            pltpu.VMEM(kernel.shape, kernel.dtype),
            pltpu.VMEM(offsets.shape, offsets.dtype),
            pltpu.SemaphoreType.DMA((groups + 2,)),
        ],
        compiler_params=pltpu.CompilerParams(vmem_limit_bytes=10 * MIB),
        cost_estimate=resample_cost(acq, cols, lines),
        name="resample_first",
    )(group, side, kernel, offsets, slc)


def resample_edge(parity, count, group, side, kernel, offsets, slab, halo, after, groups):
    acq, _, lines, cols = slab.shape
    piece = pltpu.VMEM((acq, 2, CHUNK, cols // groups), jnp.bfloat16)
    return pl.pallas_call(
        functools.partial(edge_kernel, groups, parity, count),
        in_specs=[SMEM, SMEM, VMEM, VMEM, VMEM, VMEM, ANY],
        out_specs=[VMEM] * groups,
        out_shape=[piece] * groups,
        scratch_shapes=[pltpu.VMEM((acq, CHUNK, count + HALO), jnp.bfloat16)],
        compiler_params=pltpu.CompilerParams(vmem_limit_bytes=10 * MIB),
        cost_estimate=resample_cost(acq, cols, count + HALO),
        name="resample_edge",
    )(group, side, kernel, offsets, slab, halo, after)


def slot_of(low, high):
    return high * (high - 1) // 2 + low


def look_sums(blocks, begin, parts, terms, sums, slot_rows, power_rows):
    acq, _, lines, width = blocks[0].shape
    looks = lines // LOOK_R
    both = 2 * looks
    tiles = width // LANES
    total, fresh = len(blocks) * acq, begin * acq
    base = slot_of(0, fresh)
    split = (slot_of(0, total) - base) * both
    used = split + (total - fresh) * looks

    def pool(tile):
        row = lax.broadcasted_iota(jnp.int32, (2 * LANES, LANES), 0)
        window = lax.broadcasted_iota(jnp.int32, (2 * LANES, LANES), 1) % (LANES // 2)
        wanted = tile * (LANES // LOOK_C) + (row % LANES) // LOOK_C
        return jnp.where(wanted == window, 1.0, 0.0).astype(jnp.bfloat16)

    def put(row, field):
        first = field.astype(jnp.bfloat16)
        terms[row : row + both, :LANES] = first
        terms[row : row + both, LANES:] = (field - first.astype(jnp.float32)).astype(jnp.bfloat16)

    def settle(tile):
        result = jnp.dot(terms[...], pool(tile), preferred_element_type=jnp.float32)
        sums[slot_rows : slot_rows + split, :] += result[:split]
        sums[power_rows : power_rows + used - split, :] += result[split:used]

    def unpack(tile):
        at = pl.ds(pl.multiple_of(tile * LANES, LANES), LANES)
        for r, block in enumerate(blocks):
            for a in range(acq):
                real = block[a, 0, :, at].astype(jnp.float32)
                imag = block[a, 1, :, at].astype(jnp.float32)
                parts[r * acq + a, 0] = real
                parts[r * acq + a, 1] = imag
                parts[r * acq + a, 2] = real + imag
                parts[r * acq + a, 3] = real - imag

    def cross(pairs):
        totals = {pair: [0.0, 0.0, 0.0] for pair in pairs}
        for j in range(LOOK_R):
            at = slice(j * looks, (j + 1) * looks)
            left = {i: [parts[i, c, at, :] for c in (2, 0, 1)] for i in sorted({i for i, _ in pairs})}
            right = {i: [parts[i, c, at, :] for c in (0, 2, 3)] for i in sorted({i for _, i in pairs})}
            for pair in pairs:
                for t in range(3):
                    totals[pair][t] = totals[pair][t] + left[pair[0]][t] * right[pair[1]][t]
        for i, k in pairs:
            one, two, three = totals[i, k]
            put((slot_of(i, k) - base) * both, jnp.concatenate([one - three, one - two], axis=0))

    def powers(members):
        fields = []
        for i in members:
            field = 0.0
            for j in range(LOOK_R):
                for c in range(2):
                    value = parts[i, c, j * looks : (j + 1) * looks, :]
                    field = field + value * value
            fields.append(field)
        put(split + (members[0] - fresh) * looks, jnp.concatenate(fields, axis=0))

    def work(tile):
        unpack(tile)
        for q in range(begin, len(blocks)):
            for r in range(q + 1):
                first = range(r * acq, (r + 1) * acq)
                second = range(q * acq, (q + 1) * acq)
                cross([(i, k) for i in first for k in second if i < k])
        for i in range(fresh, total, 2):
            powers((i, min(i + 1, total - 1)))

    def turn(tile, carry):
        settle(tile - 1)
        work(tile)
        return carry

    work(0)
    lax.fori_loop(1, tiles, turn, 0)
    settle(tiles - 1)


def near_kernel(groups, *rest):
    blocks, (sums, parts, terms) = rest[:groups], rest[groups:]
    acq, _, lines, _ = blocks[0].shape
    looks = lines // LOOK_R
    sums[...] = jnp.zeros(sums.shape, jnp.float32)
    look_sums(blocks, 0, parts, terms, sums, 0, slot_of(0, groups * acq) * 2 * looks)


def interfere_kernel(via, known, turn, table, *rest):
    groups = len(via)
    blocks, rest = [rest[via.index(r)] for r in range(groups)], rest[groups:]
    out, parts, terms, sums, flat, inverse, slab, sem = rest[-8:]
    acq, _, lines, width = blocks[0].shape
    looks = lines // LOOK_R
    count = table.shape[1]
    both = 2 * looks
    total, fresh = groups * acq, known * acq
    start, split = slot_of(0, fresh) * both, slot_of(0, total) * both
    sums[...] = jnp.zeros(sums.shape, jnp.float32)
    if known:
        near = rest[0]
        sums[:start, :] = near[:start, :]
        sums[split : split + fresh * looks, :] = near[start : start + fresh * looks, :]
    windows = width // LOOK_C
    look_sums(blocks, known, parts, terms, sums, start, split + fresh * looks)
    inverse[...] = lax.rsqrt(sums[split : split + total * looks, :] + 1e-6)

    left = lax.broadcasted_iota(jnp.int32, (looks, LANES), 1) < LANES // 2

    def select(p, carry):
        at = pl.multiple_of(table[0, p] * both, both)
        m = pl.multiple_of(table[1, p] * looks, looks)
        s = pl.multiple_of(table[2, p] * looks, looks)
        scale = inverse[pl.ds(m, looks), :] * inverse[pl.ds(s, looks), :]
        imag = sums[pl.ds(at + looks, looks), :] * table[3, p].astype(jnp.float32)
        value = jnp.where(left, sums[pl.ds(at, looks), :], imag) * scale
        flat[pl.ds(pl.multiple_of(p * looks, looks), looks), :] = value
        return carry

    lax.fori_loop(0, count, select, 0, unroll=max(b for b in range(1, 31) if count % b == 0))
    copies = []
    for g in range(looks):
        turned = flat[pl.ds(g, count, stride=looks), :].T
        for x in range(2):
            slab[x, g] = turned[x * (LANES // 2) : x * (LANES // 2) + windows]
        copies.append(pltpu.make_async_copy(slab.at[:, g], out.at[:, table[4, turn] * looks + g], sem.at[g]))
        copies[-1].start()
    for copy in copies:
        copy.wait()


def work_space(groups, known, acq, lines, looks):
    total, fresh = groups * acq, known * acq
    count = total - fresh
    rows = (slot_of(0, total) - slot_of(0, fresh)) * 2 * looks + (count + count % 2) * looks
    return [
        pltpu.VMEM((total, 4, lines, LANES), jnp.float32),
        pltpu.VMEM((rows, 2 * LANES), jnp.bfloat16),
    ]


def interfere_cost(pairs, acq, lines, width):
    return pl.CostEstimate(
        flops=pairs * 8 * lines * width,
        bytes_accessed=acq * 2 * lines * width * 2 * 12,
        transcendentals=0,
    )


def interfere_near(blocks):
    groups = len(blocks)
    acq, _, lines, width = blocks[0].shape
    looks, windows, total = lines // LOOK_R, width // LOOK_C, groups * acq
    return pl.pallas_call(
        functools.partial(near_kernel, groups),
        in_specs=[VMEM] * groups,
        out_specs=VMEM,
        out_shape=pltpu.VMEM(((slot_of(0, total) * 2 + total) * looks, LANES), jnp.float32),
        scratch_shapes=work_space(groups, 0, acq, lines, looks),
        compiler_params=pltpu.CompilerParams(vmem_limit_bytes=8 * MIB),
        cost_estimate=interfere_cost(slot_of(0, total), total, lines, width),
        name="interfere_near",
    )(*blocks)


def interfere(turn, chunks, table, blocks, via, near, known, before):
    groups = len(blocks)
    acq, _, lines, width = blocks[0].shape
    looks, windows, count = lines // LOOK_R, width // LOOK_C, table.shape[1]
    total = groups * acq
    near = [] if near is None else [near]
    extra = [] if before is None else [before]
    return pl.pallas_call(
        functools.partial(interfere_kernel, via, known, turn),
        in_specs=[SMEM] + [VMEM] * (groups + len(near)) + [ANY] * len(extra),
        out_specs=ANY,
        out_shape=pltpu.HBM((2, chunks * looks, windows, count), jnp.float32),
        scratch_shapes=work_space(groups, known, acq, lines, looks)
        + [
            pltpu.VMEM(((slot_of(0, total) * 2 + total) * looks, LANES), jnp.float32),
            pltpu.VMEM((count * looks, LANES), jnp.float32),
            pltpu.VMEM((total * looks, LANES), jnp.float32),
            pltpu.VMEM((2, looks, windows, count), jnp.float32),
            pltpu.SemaphoreType.DMA((looks,)),
        ],
        input_output_aliases={} if before is None else {1 + groups + len(near): 0},
        compiler_params=pltpu.CompilerParams(vmem_limit_bytes=8 * MIB),
        cost_estimate=interfere_cost(count, total, lines, width),
        name="interfere",
    )(table, *[blocks[r] for r in via], *near, *extra)


def pair_table(pairs, groups, acq, mine, odd, chunks):
    apart = (pairs // acq) ^ mine
    rank = sum(jnp.where(apart == s, r, 0) for r, s in enumerate(ORDER))
    close = rank * acq + pairs % acq
    m, s = close[:, 0], close[:, 1]
    slot = slot_of(jnp.minimum(m, s), jnp.maximum(m, s))
    turn = jnp.arange(pairs.shape[0])
    edge = jnp.where((turn == 1) == (odd == 0), chunks - 1, 0)
    place = jnp.where(turn == 0, 1, edge)
    return jnp.stack([slot, m, s, jnp.where(m < s, 1, -1), place]).astype(jnp.int32)


def local(slc, offsets, weights, pairs):
    acq, _, lines, cols = slc.shape
    groups = lax.axis_size("acq")
    size = lax.axis_size("pix")
    row = lax.axis_index("pix")
    odd = row % 2
    group = jnp.reshape(lax.axis_index("acq"), (1,)).astype(jnp.int32)
    side = jnp.reshape(odd, (1,)).astype(jnp.int32)
    kernel = weights.T
    chunks = lines // CHUNK
    table = pair_table(pairs, groups, acq, group[0], odd, chunks)
    reach = CHUNK + TILE * 2

    def send(blocks):
        moved = [blocks[0]]
        for s in ORDER[1:]:
            moved.append(lax.ppermute(blocks[s], "acq", [(i, i ^ s) for i in range(groups)]))
        return moved

    def swap(halo, begin):
        pairs_up = [(i, i + 1) for i in range(begin, size - 1, 2)]
        return lax.ppermute(halo, "pix", pairs_up + [(j, i) for i, j in pairs_up])

    *blocks, inner, outer, slab = resample_first(
        CHUNK, group, side, *[pltpu.with_memory_space_constraint(t, pltpu.HBM) for t in (kernel, offsets, slc)], groups
    )
    inside = swap(inner, 0)
    middle = send(blocks)
    pieces = resample_edge(0, reach, group, side, kernel, offsets, slab, inside, inner, groups)
    across = swap(outer, 1)
    second = send(pieces)
    third = send(
        resample_edge(1, reach, group, side, kernel, offsets, slab, across, pieces[0], groups)
    )
    result = None
    for turn, (moved, known) in enumerate(((middle, 0), (second, 0), (third, 3))):
        near = None
        if known:
            mine, result = lax.optimization_barrier((moved[0], result))
            near = interfere_near([mine, *moved[1:known]])
        result = interfere(turn, chunks, table, moved, ((0, 2, 1, 3), (0, 2, 1, 3), (0, 2, 1, 3))[turn], near, known, result)
    return jnp.transpose(result, (0, 3, 1, 2))


def solution(mesh):
    placed = (P("acq", None, "pix", None), P("acq", "pix"), P(), P())
    return jax.shard_map(
        local, mesh=mesh, in_specs=placed, out_specs=P(None, None, "pix", "acq"), check_vma=False
    )
```

```python
import functools

import jax
import jax.numpy as jnp
from jax import lax
from jax.experimental import pallas as pl
from jax.experimental.pallas import tpu as pltpu
from jax.sharding import PartitionSpec as P

LOOK_R = 4
LOOK_C = 16
CHUNK = 32
HALO = 24
ORDER = (0, 1, 2, 3)
TILE = 16
LANES = 128
MIB = 1024 * 1024


def build_bands(first, sources, group, kernel, shift, band):
    acq, taps = band.shape[0], kernel.shape[0]
    gains = kernel[...].astype(jnp.float32) * 0.125
    lane = lax.broadcasted_iota(jnp.int32, gains.shape, 1)
    rows = sum(count for _, count in sources)
    index = lax.broadcasted_iota(jnp.int32, (rows, CHUNK), 0)
    source = jnp.zeros((rows, CHUNK), jnp.int32)
    at = 0
    for begin, count in sources:
        source = jnp.where(index >= at, index + (begin - at), source)
        at += count
    target = first + lax.broadcasted_iota(jnp.int32, (rows, CHUNK), 1)
    base = source - target + (taps // 2 - 1)
    row = lax.broadcasted_iota(jnp.int32, (CHUNK, CHUNK), 0)
    col = lax.broadcasted_iota(jnp.int32, (CHUNK, CHUNK), 1)
    blocks = CHUNK // LOOK_R
    order = jnp.where(col == (row % blocks) * LOOK_R + row // blocks, 1.0, 0.0).astype(jnp.bfloat16)
    for a in range(acq):
        tap = base - shift(a)
        total = jnp.zeros((rows, CHUNK), jnp.float32)
        gain = jnp.sum(jnp.where(lane == group[0] * acq + a, gains, 0.0), axis=1, keepdims=True)
        for k in range(taps):
            total = jnp.where(tap == k, gain[k : k + 1, :], total)
        turned = lax.dot_general(
            order, total.astype(jnp.bfloat16), (((1,), (1,)), ((), ())),
            preferred_element_type=jnp.float32,
        )
        band[a] = turned.astype(jnp.bfloat16)


def copy_edge(bottom, slab, halo):
    lines = slab.shape[2]

    @pl.when(bottom)
    def _():
        halo[...] = slab[:, :, lines - HALO :, :]

    @pl.when(jnp.logical_not(bottom))
    def _():
        halo[...] = slab[:, :, :HALO, :]


def first_kernel(first, groups, group, side, kernel, off, slc, *rest):
    outs, (inner, outer, slab, band, gains, shifts, sems) = rest[:groups], rest[groups:]
    acq, _, lines, cols = slc.shape
    width = cols // groups

    def columns(s):
        return pl.ds(pl.multiple_of((group[0] ^ s) * width, width), width)

    order = [*range(1, groups), 0]
    small = [
        pltpu.make_async_copy(kernel, gains, sems.at[groups]),
        pltpu.make_async_copy(off, shifts, sems.at[groups + 1]),
    ]
    for copy in small:
        copy.start()
    copies = {}
    for s in order:
        at = columns(s)
        copies[s] = pltpu.make_async_copy(slc.at[:, :, :, at], slab.at[:, :, :, at], sems.at[s])
        copies[s].start()
    for copy in small:
        copy.wait()
    build_bands(first, [(0, lines)], group, gains, lambda a: shifts[a : a + 1, first : first + CHUNK], band)
    for s in order:
        copies[s].wait()
        at = columns(s)
        for a in range(acq):
            for x in range(2):
                total = jnp.dot(band[a], slab[a, x, :, at], preferred_element_type=jnp.float32)
                outs[s][a, x] = total.astype(jnp.bfloat16)
    copy_edge(side[0] == 0, slab, inner)
    copy_edge(side[0] == 1, slab, outer)


def edge_kernel(groups, parity, count, group, side, kernel, off, slab, halo, _, *rest):
    outs, band = rest[:groups], rest[-1]
    acq, _, lines, cols = slab.shape
    width = cols // groups
    bottom = side[0] == parity
    first = jnp.where(bottom, lines - CHUNK, 0)
    begin = pl.multiple_of(jnp.where(bottom, lines - count, 0), TILE)
    outside = jnp.where(bottom, lines, -HALO)

    def shift(a):
        return jnp.where(bottom, off[a : a + 1, lines - CHUNK :], off[a : a + 1, :CHUNK])

    build_bands(first, [(begin, count), (outside, HALO)], group, kernel, shift, band)
    for s in [*range(1, groups), 0]:
        at = pl.ds(pl.multiple_of((group[0] ^ s) * width, width), width)
        for a in range(acq):
            for x in range(2):
                lines_in = jnp.concatenate(
                    [slab[a, x, pl.ds(begin, count), at], halo[a, x, :, at]], axis=0
                )
                total = jnp.dot(band[a], lines_in, preferred_element_type=jnp.float32)
                outs[s][a, x] = total.astype(jnp.bfloat16)


SMEM = pl.BlockSpec(memory_space=pltpu.SMEM)
VMEM = pl.BlockSpec(memory_space=pltpu.VMEM)
ANY = pl.BlockSpec(memory_space=pl.ANY)


def resample_cost(acq, cols, rows):
    return pl.CostEstimate(
        flops=2 * acq * 2 * CHUNK * rows * cols,
        bytes_accessed=acq * 2 * (rows + CHUNK) * cols * 2,
        transcendentals=0,
    )


def resample_first(first, group, side, kernel, offsets, slc, groups):
    acq, _, lines, cols = slc.shape
    piece = pltpu.VMEM((acq, 2, CHUNK, cols // groups), jnp.bfloat16)
    halo = pltpu.VMEM((acq, 2, HALO, cols), jnp.bfloat16)
    slab = pltpu.VMEM(slc.shape, jnp.bfloat16)
    return pl.pallas_call(
        functools.partial(first_kernel, first, groups),
        in_specs=[SMEM, SMEM, ANY, ANY, ANY],
        out_specs=[VMEM] * (groups + 3),
        out_shape=[piece] * groups + [halo, halo, slab],
        scratch_shapes=[
            pltpu.VMEM((acq, CHUNK, lines), jnp.bfloat16),
            pltpu.VMEM(kernel.shape, kernel.dtype),
            pltpu.VMEM(offsets.shape, offsets.dtype),
            pltpu.SemaphoreType.DMA((groups + 2,)),
        ],
        compiler_params=pltpu.CompilerParams(vmem_limit_bytes=10 * MIB),
        cost_estimate=resample_cost(acq, cols, lines),
        name="resample_first",
    )(group, side, kernel, offsets, slc)


def resample_edge(parity, count, group, side, kernel, offsets, slab, halo, after, groups):
    acq, _, lines, cols = slab.shape
    piece = pltpu.VMEM((acq, 2, CHUNK, cols // groups), jnp.bfloat16)
    return pl.pallas_call(
        functools.partial(edge_kernel, groups, parity, count),
        in_specs=[SMEM, SMEM, VMEM, VMEM, VMEM, VMEM, ANY],
        out_specs=[VMEM] * groups,
        out_shape=[piece] * groups,
        scratch_shapes=[pltpu.VMEM((acq, CHUNK, count + HALO), jnp.bfloat16)],
        compiler_params=pltpu.CompilerParams(vmem_limit_bytes=10 * MIB),
        cost_estimate=resample_cost(acq, cols, count + HALO),
        name="resample_edge",
    )(group, side, kernel, offsets, slab, halo, after)


def slot_of(low, high):
    return high * (high - 1) // 2 + low


def look_sums(blocks, begin, parts, terms, sums, slot_rows, power_rows):
    acq, _, lines, width = blocks[0].shape
    looks = lines // LOOK_R
    both = 2 * looks
    tiles = width // LANES
    total, fresh = len(blocks) * acq, begin * acq
    base = slot_of(0, fresh)
    split = (slot_of(0, total) - base) * both
    used = split + (total - fresh) * looks

    def pool(tile):
        row = lax.broadcasted_iota(jnp.int32, (2 * LANES, LANES), 0)
        window = lax.broadcasted_iota(jnp.int32, (2 * LANES, LANES), 1) % (LANES // 2)
        wanted = tile * (LANES // LOOK_C) + (row % LANES) // LOOK_C
        return jnp.where(wanted == window, 1.0, 0.0).astype(jnp.bfloat16)

    def put(row, field):
        first = field.astype(jnp.bfloat16)
        terms[row : row + both, :LANES] = first
        terms[row : row + both, LANES:] = (field - first.astype(jnp.float32)).astype(jnp.bfloat16)

    def settle(tile):
        result = jnp.dot(terms[...], pool(tile), preferred_element_type=jnp.float32)
        sums[slot_rows : slot_rows + split, :] += result[:split]
        sums[power_rows : power_rows + used - split, :] += result[split:used]

    def unpack(tile):
        at = pl.ds(pl.multiple_of(tile * LANES, LANES), LANES)
        for r, block in enumerate(blocks):
            for a in range(acq):
                real = block[a, 0, :, at].astype(jnp.float32)
                imag = block[a, 1, :, at].astype(jnp.float32)
                parts[r * acq + a, 0] = real
                parts[r * acq + a, 1] = imag
                parts[r * acq + a, 2] = real + imag
                if r >= begin:
                    parts[r * acq + a, 3] = real - imag

    def cross(pairs):
        totals = {pair: [0.0, 0.0, 0.0] for pair in pairs}
        for j in range(LOOK_R):
            at = slice(j * looks, (j + 1) * looks)
            left = {i: [parts[i, c, at, :] for c in (2, 0, 1)] for i in sorted({i for i, _ in pairs})}
            right = {i: [parts[i, c, at, :] for c in (0, 2, 3)] for i in sorted({i for _, i in pairs})}
            for pair in pairs:
                for t in range(3):
                    totals[pair][t] = totals[pair][t] + left[pair[0]][t] * right[pair[1]][t]
        for i, k in pairs:
            one, two, three = totals[i, k]
            put((slot_of(i, k) - base) * both, jnp.concatenate([one - three, one - two], axis=0))

    def powers(members):
        fields = []
        for i in members:
            field = 0.0
            for j in range(LOOK_R):
                for c in range(2):
                    value = parts[i, c, j * looks : (j + 1) * looks, :]
                    field = field + value * value
            fields.append(field)
        put(split + (members[0] - fresh) * looks, jnp.concatenate(fields, axis=0))

    def work(tile):
        unpack(tile)
        for q in range(begin, len(blocks)):
            for r in range(q + 1):
                first = range(r * acq, (r + 1) * acq)
                second = range(q * acq, (q + 1) * acq)
                cross([(i, k) for i in first for k in second if i < k])
        for i in range(fresh, total, 2):
            powers((i, min(i + 1, total - 1)))

    def turn(tile, carry):
        settle(tile - 1)
        work(tile)
        return carry

    work(0)
    lax.fori_loop(1, tiles, turn, 0)
    settle(tiles - 1)


def near_kernel(groups, *rest):
    blocks, (sums, parts, terms) = rest[:groups], rest[groups:]
    acq, _, lines, _ = blocks[0].shape
    looks = lines // LOOK_R
    sums[...] = jnp.zeros(sums.shape, jnp.float32)
    look_sums(blocks, 0, parts, terms, sums, 0, slot_of(0, groups * acq) * 2 * looks)


def interfere_kernel(via, known, turn, table, *rest):
    groups = len(via)
    blocks, rest = [rest[via.index(r)] for r in range(groups)], rest[groups:]
    out, parts, terms, sums, flat, inverse, slab, sem = rest[-8:]
    acq, _, lines, width = blocks[0].shape
    looks = lines // LOOK_R
    count = table.shape[1]
    both = 2 * looks
    total, fresh = groups * acq, known * acq
    start, split = slot_of(0, fresh) * both, slot_of(0, total) * both
    sums[...] = jnp.zeros(sums.shape, jnp.float32)
    if known:
        near = rest[0]
        sums[:start, :] = near[:start, :]
        sums[split : split + fresh * looks, :] = near[start : start + fresh * looks, :]
    windows = width // LOOK_C
    look_sums(blocks, known, parts, terms, sums, start, split + fresh * looks)
    inverse[...] = lax.rsqrt(sums[split : split + total * looks, :] + 1e-6)

    left = lax.broadcasted_iota(jnp.int32, (looks, LANES), 1) < LANES // 2

    def select(p, carry):
        at = pl.multiple_of(table[0, p] * both, both)
        m = pl.multiple_of(table[1, p] * looks, looks)
        s = pl.multiple_of(table[2, p] * looks, looks)
        scale = inverse[pl.ds(m, looks), :] * inverse[pl.ds(s, looks), :]
        imag = sums[pl.ds(at + looks, looks), :] * table[3, p].astype(jnp.float32)
        value = jnp.where(left, sums[pl.ds(at, looks), :], imag) * scale
        flat[pl.ds(pl.multiple_of(p * looks, looks), looks), :] = value
        return carry

    lax.fori_loop(0, count, select, 0, unroll=max(b for b in range(1, 31) if count % b == 0))
    copies = []
    for g in range(looks):
        turned = flat[pl.ds(g, count, stride=looks), :].T
        for x in range(2):
            slab[x, g] = turned[x * (LANES // 2) : x * (LANES // 2) + windows]
        copies.append(pltpu.make_async_copy(slab.at[:, g], out.at[:, table[4, turn] * looks + g], sem.at[g]))
        copies[-1].start()
    for copy in copies:
        copy.wait()


def work_space(groups, known, acq, lines, looks):
    total, fresh = groups * acq, known * acq
    count = total - fresh
    rows = (slot_of(0, total) - slot_of(0, fresh)) * 2 * looks + (count + count % 2) * looks
    return [
        pltpu.VMEM((total, 4, lines, LANES), jnp.float32),
        pltpu.VMEM((rows, 2 * LANES), jnp.bfloat16),
    ]


def interfere_cost(pairs, acq, lines, width):
    return pl.CostEstimate(
        flops=pairs * 8 * lines * width,
        bytes_accessed=acq * 2 * lines * width * 2 * 12,
        transcendentals=0,
    )


def interfere_near(blocks):
    groups = len(blocks)
    acq, _, lines, width = blocks[0].shape
    looks, windows, total = lines // LOOK_R, width // LOOK_C, groups * acq
    return pl.pallas_call(
        functools.partial(near_kernel, groups),
        in_specs=[VMEM] * groups,
        out_specs=VMEM,
        out_shape=pltpu.VMEM(((slot_of(0, total) * 2 + total) * looks, LANES), jnp.float32),
        scratch_shapes=work_space(groups, 0, acq, lines, looks),
        compiler_params=pltpu.CompilerParams(vmem_limit_bytes=8 * MIB),
        cost_estimate=interfere_cost(slot_of(0, total), total, lines, width),
        name="interfere_near",
    )(*blocks)


def interfere(turn, chunks, table, blocks, via, near, known, before):
    groups = len(blocks)
    acq, _, lines, width = blocks[0].shape
    looks, windows, count = lines // LOOK_R, width // LOOK_C, table.shape[1]
    total = groups * acq
    near = [] if near is None else [near]
    extra = [] if before is None else [before]
    return pl.pallas_call(
        functools.partial(interfere_kernel, via, known, turn),
        in_specs=[SMEM] + [VMEM] * (groups + len(near)) + [ANY] * len(extra),
        out_specs=ANY,
        out_shape=pltpu.HBM((2, chunks * looks, windows, count), jnp.float32),
        scratch_shapes=work_space(groups, known, acq, lines, looks)
        + [
            pltpu.VMEM(((slot_of(0, total) * 2 + total) * looks, LANES), jnp.float32),
            pltpu.VMEM((count * looks, LANES), jnp.float32),
            pltpu.VMEM((total * looks, LANES), jnp.float32),
            pltpu.VMEM((2, looks, windows, count), jnp.float32),
            pltpu.SemaphoreType.DMA((looks,)),
        ],
        input_output_aliases={} if before is None else {1 + groups + len(near): 0},
        compiler_params=pltpu.CompilerParams(vmem_limit_bytes=8 * MIB),
        cost_estimate=interfere_cost(count, total, lines, width),
        name="interfere",
    )(table, *[blocks[r] for r in via], *near, *extra)


def pair_table(pairs, groups, acq, mine, odd, chunks):
    apart = (pairs // acq) ^ mine
    rank = sum(jnp.where(apart == s, r, 0) for r, s in enumerate(ORDER))
    close = rank * acq + pairs % acq
    m, s = close[:, 0], close[:, 1]
    slot = slot_of(jnp.minimum(m, s), jnp.maximum(m, s))
    turn = jnp.arange(pairs.shape[0])
    edge = jnp.where((turn == 1) == (odd == 0), chunks - 1, 0)
    place = jnp.where(turn == 0, 1, edge)
    return jnp.stack([slot, m, s, jnp.where(m < s, 1, -1), place]).astype(jnp.int32)


def local(slc, offsets, weights, pairs):
    acq, _, lines, cols = slc.shape
    groups = lax.axis_size("acq")
    size = lax.axis_size("pix")
    row = lax.axis_index("pix")
    odd = row % 2
    group = jnp.reshape(lax.axis_index("acq"), (1,)).astype(jnp.int32)
    side = jnp.reshape(odd, (1,)).astype(jnp.int32)
    kernel = weights.T
    chunks = lines // CHUNK
    table = pair_table(pairs, groups, acq, group[0], odd, chunks)
    reach = CHUNK + TILE * 2

    def send(blocks):
        moved = [blocks[0]]
        for s in ORDER[1:]:
            moved.append(lax.ppermute(blocks[s], "acq", [(i, i ^ s) for i in range(groups)]))
        return moved

    def swap(halo, begin):
        pairs_up = [(i, i + 1) for i in range(begin, size - 1, 2)]
        return lax.ppermute(halo, "pix", pairs_up + [(j, i) for i, j in pairs_up])

    *blocks, inner, outer, slab = resample_first(
        CHUNK, group, side, *[pltpu.with_memory_space_constraint(t, pltpu.HBM) for t in (kernel, offsets, slc)], groups
    )
    inside = swap(inner, 0)
    middle = send(blocks)
    pieces = resample_edge(0, reach, group, side, kernel, offsets, slab, inside, inner, groups)
    across = swap(outer, 1)
    second = send(pieces)
    third = send(
        resample_edge(1, reach, group, side, kernel, offsets, slab, across, pieces[0], groups)
    )
    result = None
    for turn, (moved, known) in enumerate(((middle, 0), (second, 0), (third, 3))):
        near = None
        if known:
            mine, result = lax.optimization_barrier((moved[0], result))
            near = interfere_near([mine, *moved[1:known]])
        result = interfere(turn, chunks, table, moved, ((0, 2, 3, 1), (0, 2, 1, 3), (0, 2, 1, 3))[turn], near, known, result)
    return jnp.transpose(result, (0, 3, 1, 2))


def solution(mesh):
    placed = (P("acq", None, "pix", None), P("acq", "pix"), P(), P())
    return jax.shard_map(
        local, mesh=mesh, in_specs=placed, out_specs=P(None, None, "pix", "acq"), check_vma=False
    )
```
